512 devices in a mesh: alpha: 32 (over x, z), beta: 16 (over y, core).
Axes of the slice: x: 4, y: 8, z: 8, core: 2. Of those that a mesh axis runs over, the one named last changes fastest.
Arguments:
- coef: bfloat16 [2, 4096, 32768], P(None, 'alpha', 'beta'), may hold values from -6 to 6
- alpha_diag: float32 [4096], P('alpha'), may hold values from -1 to 1
- beta_diag: float32 [32768], P('beta'), may hold values from -1 to 1
- alpha_tiles: bfloat16 [16, 128, 128], replicated, may hold values from -0.25 to 0.25
- beta_tiles: bfloat16 [16, 128, 128], replicated, may hold values from -0.125 to 0.125
- occupancy: int32 [32, 256], P('alpha', 'beta'), may hold values 0 or 1
- alpha_source: int32 [32, 4], replicated, may hold values from 0 to 31
- alpha_kind: int32 [32, 4], replicated, may hold values from 0 to 15
- alpha_parity: int32 [32, 4], replicated, may hold values from 0 to 1
- slot_device: int32 [256, 1], replicated, may hold values from 0 to 15; in each aligned block of 16 rows (0 to 15, 16 to 31, ...) at most 2 rows name the same one
- slot_offset: int32 [256], replicated, may hold values from 0 to 15
- beta_slot: int32 [256, 16], P('beta'), may hold values from 0 to 15
- beta_kind: int32 [256, 16], P('beta'), may hold values from 0 to 15
- beta_parity: int32 [256, 16], P('beta'), may hold values from 0 to 1
- mixed_block: int32 [16], P('beta'), may hold values from 0 to 15
- mixed_kind: int32 [16], P('beta'), may hold values from 0 to 15
Outputs:
- sigma: bfloat16 [2, 4096, 32768], P(None, 'alpha', 'beta')
The draws below stay inside these ranges and needn't reach their ends.
Inputs may be any that keep to these rules, and one draw needn't show every extreme that they name: `slot_device`: in each aligned block of 16 rows (the slots of one beta index) no number appears in more than 2 rows, and in some block one appears in exactly 2 rows.
All inputs are finite; a program needn't handle non-finite values. No bound on the sum of `occupancy` on one device may be relied on, other than what follows from the above.
Results may differ from the reference program's by a relative error of at most 0.0018.
Values may be sent and summed in bfloat16 or wider, within the bound.
A program may use at most 64 MiB of HBM per device.

```python
import math
import jax
import jax.numpy as jnp
import numpy as np
from jax import lax

BLK = 128
BBLK_DEV = 16
EB = 16
EA = 4
NS = 16
KA = 16
KB = 16
CAP = 2
NA = 4096
NB = 32768
N_ALPHA = 32
N_BETA = 16


def place_ends(result, stream_key, least, top_value):
    dims = result.shape
    place = [jax.random.randint(jax.random.fold_in(stream_key, axis), (), 0, dims[axis]) for axis in range(len(dims))]
    result = result.at[tuple(place)].set(least)
    longest = dims.index(max(dims))
    place[longest] = (place[longest] + 1) % dims[longest]
    return result.at[tuple(place)].set(top_value)


def steps_of(rng, dims, shards, least, largest):
    def one(position, blocks):
        heights = jax.random.uniform(jax.random.fold_in(jax.random.fold_in(rng, 6), position), (blocks,), jnp.float32, least / len(shards), largest / len(shards))
        return jnp.repeat(jnp.exp(heights), dims[position] // blocks).reshape((-1,) + (1,) * (len(dims) - position - 1))

    level = one(*shards[0])
    for cut in shards[1:]:
        level = level * one(*cut)
    return level


def routed_block(key, own, number, rows, number_of, top, bound, slope):
    ranking = jax.random.permutation(key, number_of)
    packed, common = portions_of(number_of, rows * top, bound, slope, True), portions_of(number_of, rows * top, bound, slope, False)
    places = jnp.arange(number_of)

    def named(tallies, turn):
        used = int((tallies > 0).sum())
        fixed = max(1, used // 4)
        shifted = fixed + (places - fixed + turn * (used - fixed)) % max(1, number_of - fixed)
        return jnp.zeros((number_of,), jnp.int32).at[ranking[jnp.where(places < fixed, places, shifted)]].set(jnp.asarray(tallies, jnp.int32))

    tallies = jnp.where(number % 4 == 0, named(packed, number // 4), named(common, number - number // 4 - 1))
    mixed = jax.random.permutation(jax.random.fold_in(own, 3), number_of)
    donor, receiver = mixed[0:number_of // 2 * 2:2], mixed[1:number_of // 2 * 2:2]
    margin = jnp.minimum(tallies[donor] - 1, bound - tallies[receiver]) // 2
    margin = jnp.where((donor == ranking[0]) | (receiver == ranking[0]) | (tallies[receiver] == 0), 0, jnp.maximum(margin, 0))
    shifted = jax.random.randint(jax.random.fold_in(own, 4), (number_of // 2,), 0, 1 << 20) % (margin + 1)
    tallies = tallies.at[donor].add(-shifted).at[receiver].add(shifted)
    members = jnp.searchsorted(jnp.cumsum(tallies), jnp.arange(rows * top), side="right").astype(jnp.int32)
    table = members.reshape(top, rows).T
    table = table[jax.random.permutation(jax.random.fold_in(own, 1), rows)]
    turn = jax.random.randint(jax.random.fold_in(own, 2), (rows, 1), 0, top)
    return jnp.take_along_axis(table, (jnp.arange(top)[None, :] + turn) % top, axis=1)


def portions_of(amount, total, most, slope, full):
    loads = [(1 << 20) // math.isqrt(standing ** slope) + 1 for standing in range(1, amount + 1)]
    largest = most if full else min(most, max(-(-total // amount), total * loads[0] // sum(loads)))
    least = 1 if total - largest >= amount - 1 else 0
    given, spare = [largest] + [least] * (amount - 1), total - largest - least * (amount - 1)
    while spare > 0:
        free = [i for i in range(1, amount) if given[i] < largest] or [i for i in range(1, amount) if given[i] < most]
        pool, budget = sum([loads[i] for i in free]), spare
        for i in free:
            more = min(most - given[i], max(1, budget * loads[i] // pool), spare)
            given[i] = given[i] + more
            spare = spare - more
    return np.array(given)


def normal_values(key, dims, width, bound, shards=(), held_as=jnp.bfloat16):
    level = steps_of(key, dims, shards, -0.22, 0.18) if shards else 1.0
    values = jax.random.normal(key, dims, jnp.float32) * width * level
    return jnp.minimum(jnp.maximum(values, -bound), bound).astype(held_as)


def setup_inputs(seed: int = 0) -> dict:
    splits = jax.random.split(jax.random.key(seed), 17)
    coef = normal_values(splits[0], (2, NA, NB), 1.0, 6.0, ((1, 32), (2, 16)))
    alpha_diag = jnp.clip(jax.random.uniform(splits[1], (NA,), jnp.float32, -1.0, 1.0) * steps_of(splits[1], (NA,), ((0, 32),), -0.4, 0.0), -1.0, 1.0)
    beta_diag = jnp.clip(jax.random.uniform(splits[2], (NB,), jnp.float32, -1.0, 1.0) * steps_of(splits[2], (NB,), ((0, 16),), -0.4, 0.0), -1.0, 1.0)
    alpha_tiles = normal_values(splits[3], (KA, BLK, BLK), (BLK * EA) ** -0.5, 0.25)
    beta_tiles = normal_values(splits[4], (KB, BLK, BLK), (BLK * EB) ** -0.5, 0.125)
    occupancy = place_ends((jax.random.randint(splits[5], (N_ALPHA, NB // BLK), 0, 4) < 3).astype(jnp.int32), jax.random.fold_in(splits[5], 1), 0, 1)
    alpha_source = place_ends(jax.random.randint(splits[6], (N_ALPHA, EA), 0, N_ALPHA), jax.random.fold_in(splits[6], 1), 0, N_ALPHA - 1).astype(jnp.int32)
    alpha_kind = place_ends(jax.random.randint(splits[7], (N_ALPHA, EA), 0, KA), jax.random.fold_in(splits[7], 1), 0, KA - 1).astype(jnp.int32)
    alpha_parity = place_ends(jax.random.randint(splits[8], (N_ALPHA, EA), 0, 2), jax.random.fold_in(splits[8], 1), 0, 1).astype(jnp.int32)
    slot_device_keys = jax.random.split(jax.random.fold_in(splits[9], 1), (N_BETA * NS) // NS)
    slot_device_turns = jax.random.permutation(jax.random.fold_in(splits[9], 3), (N_BETA * NS) // NS)
    slot_device = jax.vmap(lambda own, number: routed_block(jax.random.fold_in(splits[9], 2), own, number, NS, N_BETA, 1, CAP, 2))(slot_device_keys, slot_device_turns).reshape((N_BETA * NS, 1))
    slot_offset = place_ends(jax.random.randint(splits[10], (N_BETA * NS,), 0, BBLK_DEV), jax.random.fold_in(splits[10], 1), 0, BBLK_DEV - 1).astype(jnp.int32)
    beta_slot = place_ends(jax.random.randint(splits[11], (NB // BLK, EB), 0, NS), jax.random.fold_in(splits[11], 1), 0, NS - 1).astype(jnp.int32)
    beta_kind = place_ends(jax.random.randint(splits[12], (NB // BLK, EB), 0, KB), jax.random.fold_in(splits[12], 1), 0, KB - 1).astype(jnp.int32)
    beta_parity = place_ends(jax.random.randint(splits[13], (NB // BLK, EB), 0, 2), jax.random.fold_in(splits[13], 1), 0, 1).astype(jnp.int32)
    mixed_block = place_ends(jax.random.randint(splits[14], (N_BETA,), 0, BBLK_DEV), jax.random.fold_in(splits[14], 1), 0, BBLK_DEV - 1).astype(jnp.int32)
    mixed_kind = place_ends(jax.random.randint(splits[15], (N_BETA,), 0, KB), jax.random.fold_in(splits[15], 1), 0, KB - 1).astype(jnp.int32)
    return dict(coef=coef, alpha_diag=alpha_diag, beta_diag=beta_diag, alpha_tiles=alpha_tiles, beta_tiles=beta_tiles, occupancy=occupancy, alpha_source=alpha_source, alpha_kind=alpha_kind, alpha_parity=alpha_parity, slot_device=slot_device, slot_offset=slot_offset, beta_slot=beta_slot, beta_kind=beta_kind, beta_parity=beta_parity, mixed_block=mixed_block, mixed_kind=mixed_kind)


highest = lax.Precision.HIGHEST


def reference(coef, alpha_diag, beta_diag, alpha_tiles, beta_tiles, occupancy, alpha_source, alpha_kind, alpha_parity, slot_device, slot_offset, beta_slot, beta_kind, beta_parity, mixed_block, mixed_kind):
    beta_blocks = NB // BLK
    allowed = occupancy.astype(jnp.bfloat16)
    grid = coef.reshape(2, N_ALPHA, BLK, beta_blocks, BLK) * allowed[None, :, None, :, None]
    masked = grid.reshape(2, NA, beta_blocks, BLK)
    source_block = slot_device[:, 0] * BBLK_DEV + slot_offset
    active_columns = jnp.arange(N_BETA, dtype=jnp.int32) * BBLK_DEV + mixed_block
    active_grid = jnp.take(masked, active_columns, axis=2).reshape(2, N_ALPHA, BLK, N_BETA, BLK)
    alpha_signs = (1 - 2 * alpha_parity).astype(jnp.float32)

    def target_sum(target_entry):
        sources, kind_ids, sign_row = target_entry
        gathered = jnp.take(active_grid, sources, axis=1).astype(jnp.float32)
        mixed_tiles = sign_row[:, None, None] * jnp.take(alpha_tiles, kind_ids, axis=0).astype(jnp.float32)
        return jnp.einsum("eij,pejbc->pibc", mixed_tiles, gathered, precision=highest)

    mixed_inner = lax.map(target_sum, (alpha_source, alpha_kind, alpha_signs))
    closing = jnp.take(beta_tiles, mixed_kind, axis=0).astype(jnp.float32)
    mixed_term = jnp.einsum("tpibc,bcd->ptibd", mixed_inner, closing, precision=highest).reshape(2, NA, N_BETA, BLK)
    beta_signs = (1 - 2 * beta_parity).astype(jnp.bfloat16)
    block_ids = jnp.arange(beta_blocks, dtype=jnp.int32)

    def block_sigma(block_entry):
        block_id, slot_ids, kind_ids, sign_row = block_entry
        owner = block_id // BBLK_DEV
        sources = jnp.take(source_block, owner * NS + slot_ids)
        gathered = jnp.take(masked, sources, axis=2).reshape(2 * NA, EB * BLK)
        coupling = (sign_row[:, None, None] * jnp.take(beta_tiles, kind_ids, axis=0)).reshape(EB * BLK, BLK)
        same_spin = jnp.dot(gathered, coupling, preferred_element_type=jnp.float32).reshape(2, NA, BLK)
        current = lax.dynamic_index_in_dim(masked, block_id, 2, keepdims=False).astype(jnp.float32)
        energies = alpha_diag[:, None] + lax.dynamic_slice_in_dim(beta_diag, block_id * BLK, BLK)[None, :]
        struck = (block_id % BBLK_DEV == jnp.take(mixed_block, owner)).astype(jnp.float32)
        extra = struck * lax.dynamic_index_in_dim(mixed_term, owner, 2, keepdims=False)
        column_mask = jnp.repeat(lax.dynamic_index_in_dim(occupancy, block_id, 1, keepdims=False), BLK).astype(jnp.float32)
        summed = energies[None] * current + same_spin + extra
        return (summed * column_mask[None, :, None]).astype(jnp.bfloat16)

    stacked = lax.map(block_sigma, (block_ids, beta_slot, beta_kind, beta_signs))
    return stacked.transpose(1, 2, 0, 3).reshape(2, NA, NB)
```

```python
import functools

import jax
import jax.numpy as jnp
from jax import lax
from jax.experimental import pallas as pl
from jax.experimental.pallas import tpu as pltpu
from jax.sharding import PartitionSpec as P

MESH = pl.DeviceIdType.MESH
BLK = 128
NBLK = 16
SLOTS = 16
EB = 16
EA = 4
ROWS = 2 * BLK
F32 = jnp.float32
BF16 = jnp.bfloat16


def kernel(
    X,
    Z,
    Y,
    occ,
    asrc,
    akind,
    apar,
    sdev,
    soff,
    bslot,
    bkind,
    bpar,
    mblk,
    mkind,
    ad,
    bd,
    coef_hbm,
    at_hbm,
    bt_hbm,
    out,
    coef,
    at,
    bt,
    send,
    recv,
    panels,
    share,
    shares,
    adiag,
    mixed,
    codes,
    locs,
    local_sem,
    send_sem,
    recv_sem,
    zsend_sem,
    zrecv_sem,
    xsend_sem,
    xrecv_sem,
):
    NB = 2 * Y
    me_a = lax.axis_index("alpha")
    me_b = lax.axis_index("beta")
    x, z = me_a // Z, lax.rem(me_a, Z)
    y, c = me_b // 2, lax.rem(me_b, 2)

    def block_load(j):
        columns = pl.ds(pl.multiple_of(j * BLK, BLK), BLK)
        return pltpu.make_async_copy(coef_hbm.at[:, columns], coef.at[j], local_sem.at[j])

    tile_loads = [
        pltpu.make_async_copy(at_hbm, at.at[pl.ds(0, 16)], local_sem.at[NBLK]),
        pltpu.make_async_copy(bt_hbm, bt.at[pl.ds(0, 16)], local_sem.at[NBLK + 1]),
    ]

    def load_block(j, _):
        block_load(j).start()
        return 0

    lax.fori_loop(0, NBLK, load_block, 0)
    for load in tile_loads:
        load.start()

    def step_of(k):
        p = k // 2
        dist = (Y - p) // 2
        dy = jnp.where(lax.rem(p, 2) == 1, dist, Y - dist)
        return dy, lax.rem(k, 2)

    def peer(k):
        dy, flip = step_of(k)
        return lax.rem(y + dy, Y) * 2 + lax.rem(c + flip, 2)

    own = NB - 2

    barrier = pltpu.get_barrier_semaphore()

    def greet_beta(i, _):
        pl.semaphore_signal(barrier, 1, device_id=(me_a, lax.rem(me_b + i, NB)), device_id_type=MESH)
        return 0

    lax.fori_loop(1, NB, greet_beta, 0)

    def greet_z(i, _):
        pl.semaphore_signal(barrier, 1, device_id=(x * Z + lax.rem(z + i, Z), me_b), device_id_type=MESH)
        return 0

    lax.fori_loop(1, Z, greet_z, 0)

    def greet_x(i, _):
        pl.semaphore_signal(barrier, 1, device_id=(lax.rem(x + i, X) * Z + z, me_b), device_id_type=MESH)
        return 0

    lax.fori_loop(1, X, greet_x, 0)

    def wanted(d, _):
        code = jnp.int32(0)
        for i in range(SLOTS):
            hit = sdev[d * SLOTS + i] == me_b
            code = jnp.where(hit, code * 32 + soff[d * SLOTS + i] + 1, code)
        codes[d] = code
        return 0

    lax.fori_loop(0, NB, wanted, 0)

    def placed(i, _):
        s = sdev[me_b * SLOTS + i]
        rank = jnp.int32(0)
        for other in range(SLOTS):
            same = (sdev[me_b * SLOTS + other] == s) & (other < i)
            rank = rank + jnp.where(same, 1, 0)
        dy = lax.rem(y - (s >> 1) + Y, Y)
        pos = jnp.where(dy < Y // 2, Y - 1 - 2 * dy, 2 * dy - Y)
        k = pos * 2 + ((s + c) & 1)
        locs[i] = k * 2 + jnp.minimum(rank, 1)
        return 0

    lax.fori_loop(0, SLOTS, placed, 0)

    def await_block(j, _):
        block_load(j).wait()
        return 0

    lax.fori_loop(0, NBLK, await_block, 0)

    def panel_of(block, scale):
        return (coef[block].astype(F32) * scale).astype(BF16)

    active = mblk[0]
    mine = panel_of(active, occ[0, active].astype(F32))
    panels[z] = jnp.concatenate([mine[:BLK], mine[BLK:]], axis=1)

    def pack(k, _):
        code = codes[peer(k)]
        hi, lo = code >> 5, code & 31
        first = jnp.where(hi > 0, hi, lo)
        second = jnp.where(hi > 0, lo, 0)
        for r, named in enumerate((first, second)):
            block = jnp.clip(named - 1, 0, NBLK - 1)
            scale = jnp.where(named > 0, occ[0, block], 0).astype(F32)
            send[2 * k + r] = panel_of(block, scale)
        return 0

    lax.fori_loop(0, NB, pack, 0)

    adiag[...] = jnp.broadcast_to(ad[...], (BLK, BLK)).T

    pl.semaphore_wait(barrier, NB - 1 + Z - 1 + X - 1)

    def exchange(k):
        return pltpu.make_async_remote_copy(
            src_ref=send.at[pl.ds(2 * k, 2)],
            dst_ref=recv.at[pl.ds(2 * k, 2)],
            send_sem=send_sem.at[k],
            recv_sem=recv_sem.at[k],
            device_id=(me_a, peer(k)),
            device_id_type=MESH,
        )

    def panel_copy(i):
        return pltpu.make_async_remote_copy(
            src_ref=panels.at[z],
            dst_ref=panels.at[z],
            send_sem=zsend_sem.at[i],
            recv_sem=zrecv_sem.at[i],
            device_id=(x * Z + lax.rem(z + i, Z), me_b),
            device_id_type=MESH,
        )

    def panel_arrival(i):
        other = lax.rem(z - i + Z, Z)
        return pltpu.make_async_remote_copy(
            src_ref=panels.at[other],
            dst_ref=panels.at[other],
            send_sem=zsend_sem.at[i],
            recv_sem=zrecv_sem.at[i],
            device_id=(x * Z + other, me_b),
            device_id_type=MESH,
        )

    def share_copy(i):
        return pltpu.make_async_remote_copy(
            src_ref=share.at[i],
            dst_ref=shares.at[i],
            send_sem=xsend_sem.at[i],
            recv_sem=xrecv_sem.at[i],
            device_id=(lax.rem(x + i, X) * Z + z, me_b),
            device_id_type=MESH,
        )

    for i in range(1, Z):
        panel_copy(i).start()

    def send_far(k, _):
        exchange(k).start()
        return 0

    lax.fori_loop(0, own, send_far, 0)
    exchange(own + 1).start()
    recv[2 * own] = send[2 * own]
    recv[2 * own + 1] = send[2 * own + 1]

    for load in tile_loads:
        load.wait()

    def negate(i, _):
        at[16 + i] = -at[i]
        bt[16 + i] = -bt[i]
        return 0

    lax.fori_loop(0, 16, negate, 0)
    at[32] = jnp.zeros((BLK, BLK), BF16)

    for i in range(1, Z):
        panel_arrival(i).wait_recv()

    def share_of(i):
        target = lax.rem(x + i, X) * Z + z
        tiles, sources = [], []
        for e in range(EA):
            s = asrc[e, target]
            here = lax.div(s, Z) == x
            tiles.append(at[jnp.where(here, akind[e, target] + 16 * apar[e, target], 32)])
            sources.append(panels[lax.rem(s, Z)])
        return jnp.dot(
            jnp.concatenate(tiles, axis=1), jnp.concatenate(sources, axis=0), preferred_element_type=F32
        )

    for i in range(1, X):
        share[i] = share_of(i).astype(BF16)
        share_copy(i).start()
    inner = share_of(0)
    for i in range(1, X):
        share_copy(i).wait_recv()
        inner = inner + shares[i].astype(F32)
    inner = jnp.concatenate([inner[:, :BLK], inner[:, BLK:]], axis=0)
    coarse = inner.astype(BF16)
    fine = (inner - coarse.astype(F32)).astype(BF16)
    closing = bt[mkind[0]]
    mixed[...] = jnp.dot(
        jnp.concatenate([coarse, fine], axis=1),
        jnp.concatenate([closing, closing], axis=0),
        preferred_element_type=F32,
    )

    def arrive(k, _):
        exchange(k).wait_recv()
        return 0

    lax.fori_loop(0, own, arrive, 0)
    exchange(own + 1).wait_recv()

    def finish(j, _):
        pieces, tiles = [], []
        for e in range(EB):
            pieces.append(recv[locs[bslot[j, e]]])
            tiles.append(bt[bkind[j, e] + 16 * bpar[j, e]])
        same = jnp.dot(
            jnp.concatenate(pieces, axis=1), jnp.concatenate(tiles, axis=0), preferred_element_type=F32
        )
        columns = pl.ds(pl.multiple_of(j * BLK, BLK), BLK)
        energies = adiag[...] + bd[pl.ds(j, 1), :]
        diagonal = jnp.concatenate([energies, energies], axis=0) * coef[j].astype(F32)
        struck = jnp.where(j == active, 1.0, 0.0).astype(F32)
        total = diagonal + same + struck * mixed[...]
        out[:, columns] = (total * occ[0, j].astype(F32)).astype(BF16)
        return 0

    lax.fori_loop(0, NBLK, finish, 0)

    def sent(k, _):
        exchange(k).wait_send()
        return 0

    lax.fori_loop(0, own, sent, 0)
    exchange(own + 1).wait_send()
    for i in range(1, Z):
        panel_copy(i).wait_send()
    for i in range(1, X):
        share_copy(i).wait_send()


def solution(mesh):
    n_alpha, n_beta = mesh.shape["alpha"], mesh.shape["beta"]
    Z = 8 if n_alpha == 32 else 1
    X, Y = n_alpha // Z, n_beta // 2

    def local(
        coef,
        alpha_diag,
        beta_diag,
        alpha_tiles,
        beta_tiles,
        occupancy,
        alpha_source,
        alpha_kind,
        alpha_parity,
        slot_device,
        slot_offset,
        beta_slot,
        beta_kind,
        beta_parity,
        mixed_block,
        mixed_kind,
    ):
        smem = pl.BlockSpec(memory_space=pltpu.SMEM)
        vmem = pl.BlockSpec(memory_space=pltpu.VMEM)
        hbm = pl.BlockSpec(memory_space=pl.ANY)
        columns = coef.shape[-1]
        result = pl.pallas_call(
            functools.partial(kernel, X, Z, Y),
            out_shape=jax.ShapeDtypeStruct((ROWS, columns), BF16),
            in_specs=[smem] * 11 + [vmem] * 2 + [hbm] * 3,
            out_specs=vmem,
            scratch_shapes=[
                pltpu.VMEM((NBLK, ROWS, BLK), BF16),
                pltpu.VMEM((33, BLK, BLK), BF16),
                pltpu.VMEM((32, BLK, BLK), BF16),
                pltpu.VMEM((2 * n_beta, ROWS, BLK), BF16),
                pltpu.VMEM((2 * n_beta, ROWS, BLK), BF16),
                pltpu.VMEM((Z, BLK, ROWS), BF16),
                pltpu.VMEM((X, BLK, ROWS), BF16),
                pltpu.VMEM((X, BLK, ROWS), BF16),
                pltpu.VMEM((BLK, BLK), F32),
                pltpu.VMEM((ROWS, BLK), F32),
                pltpu.SMEM((n_beta,), jnp.int32),
                pltpu.SMEM((SLOTS,), jnp.int32),
                pltpu.SemaphoreType.DMA((NBLK + 2,)),
                pltpu.SemaphoreType.DMA((n_beta,)),
                pltpu.SemaphoreType.DMA((n_beta,)),
                pltpu.SemaphoreType.DMA((Z,)),
                pltpu.SemaphoreType.DMA((Z,)),
                pltpu.SemaphoreType.DMA((X,)),
                pltpu.SemaphoreType.DMA((X,)),
            ],
            compiler_params=pltpu.CompilerParams(
                collective_id=0, has_side_effects=True, vmem_limit_bytes=40 * 1024 * 1024
            ),
            cost_estimate=pl.CostEstimate(flops=2200000000, bytes_accessed=3300000, transcendentals=0),
        )(
            occupancy,
            alpha_source.T,
            alpha_kind.T,
            alpha_parity.T,
            slot_device.reshape(-1),
            slot_offset,
            beta_slot,
            beta_kind,
            beta_parity,
            mixed_block,
            mixed_kind,
            alpha_diag.reshape(1, BLK),
            beta_diag.reshape(NBLK, BLK),
            coef.reshape(ROWS, columns),
            alpha_tiles,
            beta_tiles,
        )
        return result.reshape(coef.shape)

    in_specs = (
        P(None, "alpha", "beta"),
        P("alpha"),
        P("beta"),
        P(),
        P(),
        P("alpha", "beta"),
        P(),
        P(),
        P(),
        P(),
        P(),
        P("beta", None),
        P("beta", None),
        P("beta", None),
        P("beta"),
        P("beta"),
    )
    out_specs = P(None, "alpha", "beta")
    return jax.shard_map(local, mesh=mesh, in_specs=in_specs, out_specs=out_specs, check_vma=False)
```

```python
import functools

import jax
import jax.numpy as jnp
from jax import lax
from jax.experimental import pallas as pl
from jax.experimental.pallas import tpu as pltpu
from jax.sharding import PartitionSpec as P

MESH = pl.DeviceIdType.MESH
BLK = 128
NBLK = 16
SLOTS = 16
EB = 16
EA = 4
ROWS = 2 * BLK
F32 = jnp.float32
BF16 = jnp.bfloat16


def kernel(X, Z, Y, *refs):
    small_hbm, (coef_hbm, at_hbm, bt_hbm, out), small = refs[:13], refs[13:17], refs[17:30]
    occ, asrc, akind, apar, sdev, soff, bslot, bkind, bpar, mblk, mkind, ad, bd = small
    coef, at, bt, send, recv, relay, panels, share, shares, adiag, mixed, codes, locs = refs[30:43]
    (
        small_sem,
        local_sem,
        send_sem,
        recv_sem,
        out_sem,
        in_sem,
        on_sem,
        end_sem,
        zsend_sem,
        zrecv_sem,
        xsend_sem,
        xrecv_sem,
    ) = refs[43:]
    NB = 2 * Y
    me_a = lax.axis_index("alpha")
    me_b = lax.axis_index("beta")
    x, z = me_a // Z, lax.rem(me_a, Z)
    y, c = me_b // 2, lax.rem(me_b, 2)

    small_loads = [
        pltpu.make_async_copy(src, dst, small_sem.at[i]) for i, (src, dst) in enumerate(zip(small_hbm, small))
    ]
    for load in small_loads:
        load.start()

    def block_load(j):
        columns = pl.ds(pl.multiple_of(j * BLK, BLK), BLK)
        return pltpu.make_async_copy(coef_hbm.at[:, columns], coef.at[j], local_sem.at[j])

    tile_loads = [
        pltpu.make_async_copy(at_hbm, at.at[pl.ds(0, 16)], local_sem.at[NBLK]),
        pltpu.make_async_copy(bt_hbm, bt.at[pl.ds(0, 16)], local_sem.at[NBLK + 1]),
    ]

    def load_block(j, _):
        block_load(j).start()
        return 0

    lax.fori_loop(0, NBLK, load_block, 0)
    for load in tile_loads:
        load.start()

    def step_of(k):
        p = k // 2
        dist = (Y - p) // 2
        dy = jnp.where(lax.rem(p, 2) == 1, dist, Y - dist)
        return dy, lax.rem(k, 2)

    def peer(k):
        dy, flip = step_of(k)
        return lax.rem(y + dy, Y) * 2 + lax.rem(c + flip, 2)

    own = NB - 2

    barrier = pltpu.get_barrier_semaphore()

    def greet_beta(i, _):
        pl.semaphore_signal(barrier, 1, device_id=(me_a, lax.rem(me_b + i, NB)), device_id_type=MESH)
        return 0

    lax.fori_loop(1, NB, greet_beta, 0)

    def greet_z(i, _):
        pl.semaphore_signal(barrier, 1, device_id=(x * Z + lax.rem(z + i, Z), me_b), device_id_type=MESH)
        return 0

    lax.fori_loop(1, Z, greet_z, 0)

    def greet_x(i, _):
        pl.semaphore_signal(barrier, 1, device_id=(lax.rem(x + i, X) * Z + z, me_b), device_id_type=MESH)
        return 0

    lax.fori_loop(1, X, greet_x, 0)

    for load in small_loads:
        load.wait()

    def wanted(d, _):
        code = jnp.int32(0)
        for i in range(SLOTS):
            hit = sdev[d * SLOTS + i] == me_b
            code = jnp.where(hit, code * 32 + soff[d * SLOTS + i] + 1, code)
        codes[d] = code
        return 0

    lax.fori_loop(0, NB, wanted, 0)

    def placed(i, _):
        s = sdev[me_b * SLOTS + i]
        rank = jnp.int32(0)
        for other in range(SLOTS):
            same = (sdev[me_b * SLOTS + other] == s) & (other < i)
            rank = rank + jnp.where(same, 1, 0)
        dy = lax.rem(y - (s >> 1) + Y, Y)
        pos = jnp.where(dy < Y // 2, Y - 1 - 2 * dy, 2 * dy - Y)
        k = pos * 2 + ((s + c) & 1)
        rank = jnp.minimum(rank, 1)
        locs[i] = jnp.where(k < 2, k + 2 * rank, 2 * k + rank)
        return 0

    lax.fori_loop(0, SLOTS, placed, 0)

    def await_block(j, _):
        block_load(j).wait()
        return 0

    lax.fori_loop(0, NBLK, await_block, 0)

    def panel_of(block, scale):
        return (coef[block].astype(F32) * scale).astype(BF16)

    active = mblk[0]
    mine = panel_of(active, occ[0, active].astype(F32))
    panels[z] = jnp.concatenate([mine[:BLK], mine[BLK:]], axis=1)

    def pack(k, _):
        code = codes[peer(k)]
        hi, lo = code >> 5, code & 31
        first = jnp.where(hi > 0, hi, lo)
        second = jnp.where(hi > 0, lo, 0)
        for r, named in enumerate((first, second)):
            block = jnp.clip(named - 1, 0, NBLK - 1)
            scale = jnp.where(named > 0, occ[0, block], 0).astype(F32)
            send[jnp.where(k < 2, k + 2 * r, 2 * k + r)] = panel_of(block, scale)
        return 0

    lax.fori_loop(0, NB, pack, 0)

    adiag[...] = jnp.broadcast_to(ad[...], (BLK, BLK)).T

    pl.semaphore_wait(barrier, NB - 1 + Z - 1 + X - 1)

    def exchange(k):
        return pltpu.make_async_remote_copy(
            src_ref=send.at[pl.ds(2 * k, 2)],
            dst_ref=recv.at[pl.ds(2 * k, 2)],
            send_sem=send_sem.at[k],
            recv_sem=recv_sem.at[k],
            device_id=(me_a, peer(k)),
            device_id_type=MESH,
        )

    leg = Y // 4

    def first_leg(w):
        chip = lax.rem(y + (leg if w == 0 else Y - leg), Y)
        return pltpu.make_async_remote_copy(
            src_ref=send.at[pl.ds(2 * w, 2)],
            dst_ref=relay.at[pl.ds(2 * w, 2)],
            send_sem=out_sem.at[w],
            recv_sem=in_sem.at[w],
            device_id=(me_a, chip * 2 + c),
            device_id_type=MESH,
        )

    def second_leg(w, flip):
        chip = lax.rem(y + (leg if w == 0 else Y - leg), Y)
        return pltpu.make_async_remote_copy(
            src_ref=relay.at[2 * w + flip],
            dst_ref=recv.at[2 * w + flip],
            send_sem=on_sem.at[2 * w + flip],
            recv_sem=end_sem.at[2 * w + flip],
            device_id=(me_a, chip * 2 + lax.rem(c + flip, 2)),
            device_id_type=MESH,
        )

    def panel_copy(i):
        return pltpu.make_async_remote_copy(
            src_ref=panels.at[z],
            dst_ref=panels.at[z],
            send_sem=zsend_sem.at[i],
            recv_sem=zrecv_sem.at[i],
            device_id=(x * Z + lax.rem(z + i, Z), me_b),
            device_id_type=MESH,
        )

    def panel_arrival(i):
        other = lax.rem(z - i + Z, Z)
        return pltpu.make_async_remote_copy(
            src_ref=panels.at[other],
            dst_ref=panels.at[other],
            send_sem=zsend_sem.at[i],
            recv_sem=zrecv_sem.at[i],
            device_id=(x * Z + other, me_b),
            device_id_type=MESH,
        )

    def share_copy(i):
        return pltpu.make_async_remote_copy(
            src_ref=share.at[i],
            dst_ref=shares.at[i],
            send_sem=xsend_sem.at[i],
            recv_sem=xrecv_sem.at[i],
            device_id=(lax.rem(x + i, X) * Z + z, me_b),
            device_id_type=MESH,
        )

    for w in range(2):
        first_leg(w).start()
    for i in range(1, Z):
        panel_copy(i).start()

    def send_far(k, _):
        exchange(k).start()
        return 0

    lax.fori_loop(2, own, send_far, 0)
    exchange(own + 1).start()
    recv[2 * own] = send[2 * own]
    recv[2 * own + 1] = send[2 * own + 1]

    for load in tile_loads:
        load.wait()

    def negate(i, _):
        at[16 + i] = -at[i]
        bt[16 + i] = -bt[i]
        return 0

    lax.fori_loop(0, 16, negate, 0)
    at[32] = jnp.zeros((BLK, BLK), BF16)

    for w in range(2):
        first_leg(w).wait_recv()
        for flip in range(2):
            second_leg(w, flip).start()

    for i in range(1, Z):
        panel_arrival(i).wait_recv()

    def share_of(i):
        target = lax.rem(x + i, X) * Z + z
        tiles, sources = [], []
        for e in range(EA):
            s = asrc[e, target]
            here = lax.div(s, Z) == x
            tiles.append(at[jnp.where(here, akind[e, target] + 16 * apar[e, target], 32)])
            sources.append(panels[lax.rem(s, Z)])
        return jnp.dot(
            jnp.concatenate(tiles, axis=1), jnp.concatenate(sources, axis=0), preferred_element_type=F32
        )

    for i in range(1, X):
        share[i] = share_of(i).astype(BF16)
        share_copy(i).start()
    inner = share_of(0)
    for i in range(1, X):
        share_copy(i).wait_recv()
        inner = inner + shares[i].astype(F32)
    inner = jnp.concatenate([inner[:, :BLK], inner[:, BLK:]], axis=0)
    coarse = inner.astype(BF16)
    fine = (inner - coarse.astype(F32)).astype(BF16)
    closing = bt[mkind[0]]
    mixed[...] = jnp.dot(
        jnp.concatenate([coarse, fine], axis=1),
        jnp.concatenate([closing, closing], axis=0),
        preferred_element_type=F32,
    )

    def arrive(k, _):
        exchange(k).wait_recv()
        return 0

    lax.fori_loop(2, own, arrive, 0)
    exchange(own + 1).wait_recv()
    for w in range(2):
        for flip in range(2):
            second_leg(w, flip).wait_recv()

    def finish(j, _):
        pieces, tiles = [], []
        for e in range(EB):
            pieces.append(recv[locs[bslot[j, e]]])
            tiles.append(bt[bkind[j, e] + 16 * bpar[j, e]])
        same = jnp.dot(
            jnp.concatenate(pieces, axis=1), jnp.concatenate(tiles, axis=0), preferred_element_type=F32
        )
        columns = pl.ds(pl.multiple_of(j * BLK, BLK), BLK)
        energies = adiag[...] + bd[pl.ds(j, 1), :]
        diagonal = jnp.concatenate([energies, energies], axis=0) * coef[j].astype(F32)
        struck = jnp.where(j == active, 1.0, 0.0).astype(F32)
        total = diagonal + same + struck * mixed[...]
        out[:, columns] = (total * occ[0, j].astype(F32)).astype(BF16)
        return 0

    lax.fori_loop(0, NBLK, finish, 0)

    def sent(k, _):
        exchange(k).wait_send()
        return 0

    lax.fori_loop(2, own, sent, 0)
    exchange(own + 1).wait_send()
    for w in range(2):
        first_leg(w).wait_send()
        for flip in range(2):
            second_leg(w, flip).wait_send()
    for i in range(1, Z):
        panel_copy(i).wait_send()
    for i in range(1, X):
        share_copy(i).wait_send()


def solution(mesh):
    n_alpha, n_beta = mesh.shape["alpha"], mesh.shape["beta"]
    Z = 8 if n_alpha == 32 else 1
    X, Y = n_alpha // Z, n_beta // 2

    def local(
        coef,
        alpha_diag,
        beta_diag,
        alpha_tiles,
        beta_tiles,
        occupancy,
        alpha_source,
        alpha_kind,
        alpha_parity,
        slot_device,
        slot_offset,
        beta_slot,
        beta_kind,
        beta_parity,
        mixed_block,
        mixed_kind,
    ):
        vmem = pl.BlockSpec(memory_space=pltpu.VMEM)
        hbm = pl.BlockSpec(memory_space=pl.ANY)
        columns = coef.shape[-1]
        small = (
            occupancy,
            alpha_source.T,
            alpha_kind.T,
            alpha_parity.T,
            slot_device.reshape(-1),
            slot_offset,
            beta_slot,
            beta_kind,
            beta_parity,
            mixed_block,
            mixed_kind,
            alpha_diag.reshape(1, BLK),
            beta_diag.reshape(NBLK, BLK),
        )
        result = pl.pallas_call(
            functools.partial(kernel, X, Z, Y),
            out_shape=jax.ShapeDtypeStruct((ROWS, columns), BF16),
            in_specs=[hbm] * (len(small) + 3),
            out_specs=vmem,
            scratch_shapes=[
                *(pltpu.SMEM(v.shape, v.dtype) for v in small[:11]),
                *(pltpu.VMEM(v.shape, v.dtype) for v in small[11:]),
                pltpu.VMEM((NBLK, ROWS, BLK), BF16),
                pltpu.VMEM((33, BLK, BLK), BF16),
                pltpu.VMEM((32, BLK, BLK), BF16),
                pltpu.VMEM((2 * n_beta, ROWS, BLK), BF16),
                pltpu.VMEM((2 * n_beta, ROWS, BLK), BF16),
                pltpu.VMEM((4, ROWS, BLK), BF16),
                pltpu.VMEM((Z, BLK, ROWS), BF16),
                pltpu.VMEM((X, BLK, ROWS), BF16),
                pltpu.VMEM((X, BLK, ROWS), BF16),
                pltpu.VMEM((BLK, BLK), F32),
                pltpu.VMEM((ROWS, BLK), F32),
                pltpu.SMEM((n_beta,), jnp.int32),
                pltpu.SMEM((SLOTS,), jnp.int32),
                pltpu.SemaphoreType.DMA((len(small),)),
                pltpu.SemaphoreType.DMA((NBLK + 2,)),
                pltpu.SemaphoreType.DMA((n_beta,)),
                pltpu.SemaphoreType.DMA((n_beta,)),
                pltpu.SemaphoreType.DMA((2,)),
                pltpu.SemaphoreType.DMA((2,)),
                pltpu.SemaphoreType.DMA((4,)),
                pltpu.SemaphoreType.DMA((4,)),
                pltpu.SemaphoreType.DMA((Z,)),
                pltpu.SemaphoreType.DMA((Z,)),
                pltpu.SemaphoreType.DMA((X,)),
                pltpu.SemaphoreType.DMA((X,)),
            ],
            compiler_params=pltpu.CompilerParams(
                collective_id=0, has_side_effects=True, vmem_limit_bytes=60 * 1024 * 1024
            ),
            cost_estimate=pl.CostEstimate(flops=2200000000, bytes_accessed=3300000, transcendentals=0),
        )(
            *small,
            coef.reshape(ROWS, columns),
            alpha_tiles,
            beta_tiles,
        )
        return result.reshape(coef.shape)

    in_specs = (
        P(None, "alpha", "beta"),
        P("alpha"),
        P("beta"),
        P(),
        P(),
        P("alpha", "beta"),
        P(),
        P(),
        P(),
        P(),
        P(),
        P("beta", None),
        P("beta", None),
        P("beta", None),
        P("beta"),
        P("beta"),
    )
    out_specs = P(None, "alpha", "beta")
    return jax.shard_map(local, mesh=mesh, in_specs=in_specs, out_specs=out_specs, check_vma=False)
```

```python
import functools

import jax
import jax.numpy as jnp
from jax import lax
from jax.experimental import pallas as pl
from jax.experimental.pallas import tpu as pltpu
from jax.sharding import PartitionSpec as P

MESH = pl.DeviceIdType.MESH
BLK = 128
NBLK = 16
SLOTS = 16
EB = 16
EA = 4
ROWS = 2 * BLK
CHUNKS = ((0, 160), (160, 96))
NCH = len(CHUNKS)
F32 = jnp.float32
BF16 = jnp.bfloat16


def kernel(X, Z, Y, *refs):
    small_hbm, (coef_hbm, at_hbm, bt_hbm, out), small = refs[:13], refs[13:17], refs[17:30]
    occ, asrc, akind, apar, sdev, soff, bslot, bkind, bpar, mblk, mkind, ad, bd = small
    coef, at, bt, panels, share, shares, adiag, mixed, locs = refs[30:39]
    send, recv, relay = (refs[39 + NCH * i : 39 + NCH * (i + 1)] for i in range(3))
    (
        small_sem,
        local_sem,
        send_sem,
        recv_sem,
        out_sem,
        in_sem,
        on_sem,
        end_sem,
        zsend_sem,
        zrecv_sem,
        xsend_sem,
        xrecv_sem,
    ) = refs[39 + 3 * NCH :]
    NB = 2 * Y
    me_a = lax.axis_index("alpha")
    me_b = lax.axis_index("beta")
    x, z = me_a // Z, lax.rem(me_a, Z)
    y, c = me_b // 2, lax.rem(me_b, 2)

    small_loads = [
        pltpu.make_async_copy(src, dst, small_sem.at[i]) for i, (src, dst) in enumerate(zip(small_hbm, small))
    ]
    for load in small_loads:
        load.start()

    def block_load(j):
        columns = pl.ds(pl.multiple_of(j * BLK, BLK), BLK)
        return pltpu.make_async_copy(coef_hbm.at[:, columns], coef.at[j], local_sem.at[j])

    tile_loads = [
        pltpu.make_async_copy(at_hbm, at.at[pl.ds(0, 16)], local_sem.at[NBLK]),
        pltpu.make_async_copy(bt_hbm, bt.at[pl.ds(0, 16)], local_sem.at[NBLK + 1]),
    ]

    def load_block(j, _):
        block_load(j).start()
        return 0

    lax.fori_loop(0, NBLK, load_block, 0)
    for load in tile_loads:
        load.start()

    def step_of(k):
        p = k // 2
        dist = (Y - p) // 2
        dy = jnp.where(lax.rem(p, 2) == 1, dist, Y - dist)
        return dy, lax.rem(k, 2)

    def peer(k):
        dy, flip = step_of(k)
        return lax.rem(y + dy, Y) * 2 + lax.rem(c + flip, 2)

    own = NB - 2

    barrier = pltpu.get_barrier_semaphore()

    def greet_beta(i, _):
        pl.semaphore_signal(barrier, 1, device_id=(me_a, lax.rem(me_b + i, NB)), device_id_type=MESH)
        return 0

    lax.fori_loop(1, NB, greet_beta, 0)

    def greet_z(i, _):
        pl.semaphore_signal(barrier, 1, device_id=(x * Z + lax.rem(z + i, Z), me_b), device_id_type=MESH)
        return 0

    lax.fori_loop(1, Z, greet_z, 0)

    def greet_x(i, _):
        pl.semaphore_signal(barrier, 1, device_id=(lax.rem(x + i, X) * Z + z, me_b), device_id_type=MESH)
        return 0

    lax.fori_loop(1, X, greet_x, 0)

    for load in small_loads:
        load.wait()

    def await_block(j, _):
        block_load(j).wait()
        return 0

    lax.fori_loop(0, NBLK, await_block, 0)

    def panel_of(block, allowed):
        panel = coef[block]
        return jnp.where(allowed, panel, jnp.zeros_like(panel))

    active = mblk[0]
    mine = panel_of(active, occ[0, active] > 0)
    panels[z] = jnp.concatenate([mine[:BLK], mine[BLK:]], axis=1)

    def pack(k):
        d = peer(k)
        code = jnp.int32(0)
        for i in range(SLOTS):
            hit = sdev[d * SLOTS + i] == me_b
            code = jnp.where(hit, code * 32 + soff[d * SLOTS + i] + 1, code)
        hi, lo = code >> 5, code & 31
        first = jnp.where(hi > 0, hi, lo)
        second = jnp.where(hi > 0, lo, 0)
        for r, named in enumerate((first, second)):
            block = jnp.clip(named - 1, 0, NBLK - 1)
            panel = panel_of(block, (named > 0) & (occ[0, block] > 0))
            place = jnp.where(k < 2, k + 2 * r, 2 * k + r)
            for h, (row, count) in enumerate(CHUNKS):
                send[h][place] = panel[row : row + count]

    pl.semaphore_wait(barrier, NB - 1 + Z - 1 + X - 1)

    def exchange(h, k):
        return pltpu.make_async_remote_copy(
            src_ref=send[h].at[pl.ds(2 * k, 2)],
            dst_ref=recv[h].at[pl.ds(2 * k, 2)],
            send_sem=send_sem.at[h, k],
            recv_sem=recv_sem.at[h, k],
            device_id=(me_a, peer(k)),
            device_id_type=MESH,
        )

    leg = Y // 4

    def first_leg(h, w):
        chip = lax.rem(y + (leg if w == 0 else Y - leg), Y)
        return pltpu.make_async_remote_copy(
            src_ref=send[h].at[pl.ds(2 * w, 2)],
            dst_ref=relay[h].at[pl.ds(2 * w, 2)],
            send_sem=out_sem.at[h, w],
            recv_sem=in_sem.at[h, w],
            device_id=(me_a, chip * 2 + c),
            device_id_type=MESH,
        )

    def second_leg(h, w, flip):
        chip = lax.rem(y + (leg if w == 0 else Y - leg), Y)
        return pltpu.make_async_remote_copy(
            src_ref=relay[h].at[2 * w + flip],
            dst_ref=recv[h].at[2 * w + flip],
            send_sem=on_sem.at[h, 2 * w + flip],
            recv_sem=end_sem.at[h, 2 * w + flip],
            device_id=(me_a, chip * 2 + lax.rem(c + flip, 2)),
            device_id_type=MESH,
        )

    def panel_copy(i):
        return pltpu.make_async_remote_copy(
            src_ref=panels.at[z],
            dst_ref=panels.at[z],
            send_sem=zsend_sem.at[i],
            recv_sem=zrecv_sem.at[i],
            device_id=(x * Z + lax.rem(z + i, Z), me_b),
            device_id_type=MESH,
        )

    def panel_arrival(i):
        other = lax.rem(z - i + Z, Z)
        return pltpu.make_async_remote_copy(
            src_ref=panels.at[other],
            dst_ref=panels.at[other],
            send_sem=zsend_sem.at[i],
            recv_sem=zrecv_sem.at[i],
            device_id=(x * Z + other, me_b),
            device_id_type=MESH,
        )

    def share_copy(i):
        return pltpu.make_async_remote_copy(
            src_ref=share.at[i],
            dst_ref=shares.at[i],
            send_sem=xsend_sem.at[i],
            recv_sem=xrecv_sem.at[i],
            device_id=(lax.rem(x + i, X) * Z + z, me_b),
            device_id_type=MESH,
        )

    def pack_first(k, _):
        pack(k)
        return 0

    lax.fori_loop(0, 2, pack_first, 0)
    for w in range(2):
        first_leg(0, w).start()
    for i in range(1, Z):
        panel_copy(i).start()

    def pack_and_send(k, _):
        pack(k)
        exchange(0, k).start()
        return 0

    lax.fori_loop(2, own, pack_and_send, 0)
    pack_and_send(own + 1, 0)
    pack(own)
    for h in range(NCH):
        for r in range(2):
            recv[h][2 * own + r] = send[h][2 * own + r]

    def placed(i, _):
        s = sdev[me_b * SLOTS + i]
        rank = jnp.int32(0)
        for other in range(SLOTS):
            same = (sdev[me_b * SLOTS + other] == s) & (other < i)
            rank = rank + jnp.where(same, 1, 0)
        dy = lax.rem(y - (s >> 1) + Y, Y)
        pos = jnp.where(dy < Y // 2, Y - 1 - 2 * dy, 2 * dy - Y)
        k = pos * 2 + ((s + c) & 1)
        rank = jnp.minimum(rank, 1)
        locs[i] = jnp.where(k < 2, k + 2 * rank, 2 * k + rank)
        return 0

    lax.fori_loop(0, SLOTS, placed, 0)

    adiag[...] = jnp.broadcast_to(ad[...], (BLK, BLK)).T

    for load in tile_loads:
        load.wait()

    def negate(i, _):
        at[16 + i] = -at[i]
        bt[16 + i] = -bt[i]
        return 0

    lax.fori_loop(0, 16, negate, 0)
    at[32] = jnp.zeros((BLK, BLK), BF16)

    def pass_on(h):
        for w in range(2):
            first_leg(h, w).wait_recv()
            for flip in range(2):
                second_leg(h, w, flip).start()

    pass_on(0)

    for i in range(1, Z):
        panel_arrival(i).wait_recv()

    def share_of(i):
        target = lax.rem(x + i, X) * Z + z
        tiles, sources = [], []
        for e in range(EA):
            s = asrc[e, target]
            here = lax.div(s, Z) == x
            tiles.append(at[jnp.where(here, akind[e, target] + 16 * apar[e, target], 32)])
            sources.append(panels[lax.rem(s, Z)])
        return jnp.dot(
            jnp.concatenate(tiles, axis=1), jnp.concatenate(sources, axis=0), preferred_element_type=F32
        )

    for i in range(1, X):
        share[i] = share_of(i).astype(BF16)
        share_copy(i).start()
    inner = share_of(0)
    for i in range(1, X):
        share_copy(i).wait_recv()
        inner = inner + shares[i].astype(F32)
    inner = jnp.concatenate([inner[:, :BLK], inner[:, BLK:]], axis=0)
    coarse = inner.astype(BF16)
    fine = (inner - coarse.astype(F32)).astype(BF16)
    closing = bt[mkind[0]]
    mixed[...] = jnp.dot(
        jnp.concatenate([coarse, fine], axis=1),
        jnp.concatenate([closing, closing], axis=0),
        preferred_element_type=F32,
    )

    for h in range(1, NCH):
        for w in range(2):
            first_leg(h - 1, w).wait_send()
            first_leg(h, w).start()

        def follow(k, _):
            exchange(h - 1, k).wait_send()
            exchange(h, k).start()
            return 0

        lax.fori_loop(2, own, follow, 0)
        follow(own + 1, 0)
        pass_on(h)

    def finish(h):
        row, count = CHUNKS[h]
        rows = pl.ds(row, count)

        def arrive(k, _):
            exchange(h, k).wait_recv()
            return 0

        lax.fori_loop(2, own, arrive, 0)
        arrive(own + 1, 0)
        for w in range(2):
            for flip in range(2):
                second_leg(h, w, flip).wait_recv()

        def block(j, _):
            pieces, tiles = [], []
            for e in range(EB):
                pieces.append(recv[h][locs[bslot[j, e]]])
                tiles.append(bt[bkind[j, e] + 16 * bpar[j, e]])
            same = jnp.dot(
                jnp.concatenate(pieces, axis=1), jnp.concatenate(tiles, axis=0), preferred_element_type=F32
            )
            columns = pl.ds(pl.multiple_of(j * BLK, BLK), BLK)
            parts = []
            for start in range(row, row + count, 32):
                parts.append(adiag[pl.ds(start % BLK, 32), :])
            energies = jnp.concatenate(parts, axis=0) + bd[pl.ds(j, 1), :]
            struck = jnp.where(j == active, 1.0, 0.0).astype(F32)
            total = energies * coef[j, rows, :].astype(F32) + same + struck * mixed[rows, :]
            out[rows, columns] = (total * occ[0, j].astype(F32)).astype(BF16)
            return 0

        lax.fori_loop(0, NBLK, block, 0)

    for h in range(NCH):
        finish(h)

    last = NCH - 1

    def sent(k, _):
        exchange(last, k).wait_send()
        return 0

    lax.fori_loop(2, own, sent, 0)
    sent(own + 1, 0)
    for w in range(2):
        first_leg(last, w).wait_send()
        for h in range(NCH):
            for flip in range(2):
                second_leg(h, w, flip).wait_send()
    for i in range(1, Z):
        panel_copy(i).wait_send()
    for i in range(1, X):
        share_copy(i).wait_send()


def solution(mesh):
    n_alpha, n_beta = mesh.shape["alpha"], mesh.shape["beta"]
    Z = 8 if n_alpha == 32 else 1
    X, Y = n_alpha // Z, n_beta // 2

    def local(
        coef,
        alpha_diag,
        beta_diag,
        alpha_tiles,
        beta_tiles,
        occupancy,
        alpha_source,
        alpha_kind,
        alpha_parity,
        slot_device,
        slot_offset,
        beta_slot,
        beta_kind,
        beta_parity,
        mixed_block,
        mixed_kind,
    ):
        vmem = pl.BlockSpec(memory_space=pltpu.VMEM)
        hbm = pl.BlockSpec(memory_space=pl.ANY)
        columns = coef.shape[-1]
        small = (
            occupancy,
            alpha_source.T,
            alpha_kind.T,
            alpha_parity.T,
            slot_device.reshape(-1),
            slot_offset,
            beta_slot,
            beta_kind,
            beta_parity,
            mixed_block,
            mixed_kind,
            alpha_diag.reshape(1, BLK),
            beta_diag.reshape(NBLK, BLK),
        )
        result = pl.pallas_call(
            functools.partial(kernel, X, Z, Y),
            out_shape=jax.ShapeDtypeStruct((ROWS, columns), BF16),
            in_specs=[hbm] * (len(small) + 3),
            out_specs=vmem,
            scratch_shapes=[
                *(pltpu.SMEM(v.shape, v.dtype) for v in small[:11]),
                *(pltpu.VMEM(v.shape, v.dtype) for v in small[11:]),
                pltpu.VMEM((NBLK, ROWS, BLK), BF16),
                pltpu.VMEM((33, BLK, BLK), BF16),
                pltpu.VMEM((32, BLK, BLK), BF16),
                pltpu.VMEM((Z, BLK, ROWS), BF16),
                pltpu.VMEM((X, BLK, ROWS), BF16),
                pltpu.VMEM((X, BLK, ROWS), BF16),
                pltpu.VMEM((BLK, BLK), F32),
                pltpu.VMEM((ROWS, BLK), F32),
                pltpu.SMEM((SLOTS,), jnp.int32),
                *(pltpu.VMEM((2 * n_beta, count, BLK), BF16) for _, count in CHUNKS),
                *(pltpu.VMEM((2 * n_beta, count, BLK), BF16) for _, count in CHUNKS),
                *(pltpu.VMEM((4, count, BLK), BF16) for _, count in CHUNKS),
                pltpu.SemaphoreType.DMA((len(small),)),
                pltpu.SemaphoreType.DMA((NBLK + 2,)),
                pltpu.SemaphoreType.DMA((NCH, n_beta)),
                pltpu.SemaphoreType.DMA((NCH, n_beta)),
                pltpu.SemaphoreType.DMA((NCH, 2)),
                pltpu.SemaphoreType.DMA((NCH, 2)),
                pltpu.SemaphoreType.DMA((NCH, 4)),
                pltpu.SemaphoreType.DMA((NCH, 4)),
                pltpu.SemaphoreType.DMA((Z,)),
                pltpu.SemaphoreType.DMA((Z,)),
                pltpu.SemaphoreType.DMA((X,)),
                pltpu.SemaphoreType.DMA((X,)),
            ],
            compiler_params=pltpu.CompilerParams(
                collective_id=0, has_side_effects=True, vmem_limit_bytes=60 * 1024 * 1024
            ),
            cost_estimate=pl.CostEstimate(flops=2200000000, bytes_accessed=3300000, transcendentals=0),
        )(
            *small,
            coef.reshape(ROWS, columns),
            alpha_tiles,
            beta_tiles,
        )
        return result.reshape(coef.shape)

    in_specs = (
        P(None, "alpha", "beta"),
        P("alpha"),
        P("beta"),
        P(),
        P(),
        P("alpha", "beta"),
        P(),
        P(),
        P(),
        P(),
        P(),
        P("beta", None),
        P("beta", None),
        P("beta", None),
        P("beta"),
        P("beta"),
    )
    out_specs = P(None, "alpha", "beta")
    return jax.shard_map(local, mesh=mesh, in_specs=in_specs, out_specs=out_specs, check_vma=False)
```

```python
import functools

import jax
import jax.numpy as jnp
from jax import lax
from jax.experimental import pallas as pl
from jax.experimental.pallas import tpu as pltpu
from jax.sharding import PartitionSpec as P

MESH = pl.DeviceIdType.MESH
BLK = 128
NBLK = 16
SLOTS = 16
EB = 16
EA = 4
ROWS = 2 * BLK
CHUNKS = ((0, 160), (160, 96))
NCH = len(CHUNKS)
F32 = jnp.float32
BF16 = jnp.bfloat16


def kernel(X, Z, Y, *refs):
    small_hbm, (coef_hbm, at_hbm, bt_hbm, out), small = refs[:13], refs[13:17], refs[17:30]
    occ, asrc, akind, apar, sdev, soff, bslot, bkind, bpar, mblk, mkind, ad, bd = small
    coef, at, bt, panels, share, shares, adiag, mixed, locs = refs[30:39]
    send, recv, relay = (refs[39 + NCH * i : 39 + NCH * (i + 1)] for i in range(3))
    (
        small_sem,
        local_sem,
        send_sem,
        recv_sem,
        out_sem,
        in_sem,
        on_sem,
        end_sem,
        zsend_sem,
        zrecv_sem,
        xsend_sem,
        xrecv_sem,
    ) = refs[39 + 3 * NCH :]
    NB = 2 * Y
    me_a = lax.axis_index("alpha")
    me_b = lax.axis_index("beta")
    x, z = me_a // Z, lax.rem(me_a, Z)
    y, c = me_b // 2, lax.rem(me_b, 2)

    small_loads = [
        pltpu.make_async_copy(src, dst, small_sem.at[i]) for i, (src, dst) in enumerate(zip(small_hbm, small))
    ]
    for load in small_loads:
        load.start()

    def block_load(j):
        columns = pl.ds(pl.multiple_of(j * BLK, BLK), BLK)
        return pltpu.make_async_copy(coef_hbm.at[:, columns], coef.at[j], local_sem.at[j])

    tile_loads = [
        pltpu.make_async_copy(at_hbm, at.at[pl.ds(0, 16)], local_sem.at[NBLK]),
        pltpu.make_async_copy(bt_hbm, bt.at[pl.ds(0, 16)], local_sem.at[NBLK + 1]),
    ]

    def load_block(j, _):
        block_load(j).start()
        return 0

    lax.fori_loop(0, NBLK, load_block, 0)
    for load in tile_loads:
        load.start()

    def step_of(k):
        p = k // 2
        dist = (Y - p) // 2
        dy = jnp.where(lax.rem(p, 2) == 1, dist, Y - dist)
        return dy, lax.rem(k, 2)

    def peer(k):
        dy, flip = step_of(k)
        return lax.rem(y + dy, Y) * 2 + lax.rem(c + flip, 2)

    own = NB - 2

    barrier = pltpu.get_barrier_semaphore()

    def greet_beta(i, _):
        pl.semaphore_signal(barrier, 1, device_id=(me_a, lax.rem(me_b + i, NB)), device_id_type=MESH)
        return 0

    lax.fori_loop(1, NB, greet_beta, 0)

    has_next, has_prev = z < Z - 1, z > 0

    @pl.when(has_next)
    def _():
        pl.semaphore_signal(barrier, 1, device_id=(me_a + 1, me_b), device_id_type=MESH)

    @pl.when(has_prev)
    def _():
        pl.semaphore_signal(barrier, 1, device_id=(me_a - 1, me_b), device_id_type=MESH)

    def greet_x(i, _):
        pl.semaphore_signal(barrier, 1, device_id=(lax.rem(x + i, X) * Z + z, me_b), device_id_type=MESH)
        return 0

    lax.fori_loop(1, X, greet_x, 0)

    for load in small_loads:
        load.wait()

    def await_block(j, _):
        block_load(j).wait()
        return 0

    lax.fori_loop(0, NBLK, await_block, 0)

    def panel_of(block, allowed):
        panel = coef[block]
        return jnp.where(allowed, panel, jnp.zeros_like(panel))

    active = mblk[0]
    mine = panel_of(active, occ[0, active] > 0)
    panels[z] = jnp.concatenate([mine[:BLK], mine[BLK:]], axis=1)

    def pack(k):
        d = peer(k)
        code = jnp.int32(0)
        for i in range(SLOTS):
            hit = sdev[d * SLOTS + i] == me_b
            code = jnp.where(hit, code * 32 + soff[d * SLOTS + i] + 1, code)
        hi, lo = code >> 5, code & 31
        first = jnp.where(hi > 0, hi, lo)
        second = jnp.where(hi > 0, lo, 0)
        for r, named in enumerate((first, second)):
            block = jnp.clip(named - 1, 0, NBLK - 1)
            panel = panel_of(block, (named > 0) & (occ[0, block] > 0))
            place = jnp.where(k < 2, k + 2 * r, 2 * k + r)
            for h, (row, count) in enumerate(CHUNKS):
                send[h][place] = panel[row : row + count]

    pl.semaphore_wait(barrier, NB - 1 + X - 1 + jnp.where(has_next, 1, 0) + jnp.where(has_prev, 1, 0))

    def exchange(h, k):
        return pltpu.make_async_remote_copy(
            src_ref=send[h].at[pl.ds(2 * k, 2)],
            dst_ref=recv[h].at[pl.ds(2 * k, 2)],
            send_sem=send_sem.at[h, k],
            recv_sem=recv_sem.at[h, k],
            device_id=(me_a, peer(k)),
            device_id_type=MESH,
        )

    leg = Y // 4

    def first_leg(h, w):
        chip = lax.rem(y + (leg if w == 0 else Y - leg), Y)
        return pltpu.make_async_remote_copy(
            src_ref=send[h].at[pl.ds(2 * w, 2)],
            dst_ref=relay[h].at[pl.ds(2 * w, 2)],
            send_sem=out_sem.at[h, w],
            recv_sem=in_sem.at[h, w],
            device_id=(me_a, chip * 2 + c),
            device_id_type=MESH,
        )

    def second_leg(h, w, flip):
        chip = lax.rem(y + (leg if w == 0 else Y - leg), Y)
        return pltpu.make_async_remote_copy(
            src_ref=relay[h].at[2 * w + flip],
            dst_ref=recv[h].at[2 * w + flip],
            send_sem=on_sem.at[h, 2 * w + flip],
            recv_sem=end_sem.at[h, 2 * w + flip],
            device_id=(me_a, chip * 2 + lax.rem(c + flip, 2)),
            device_id_type=MESH,
        )

    def panel_copy(way, s):
        origin, to = (z - s + 1, me_a + 1) if way == 0 else (z + s - 1, me_a - 1)
        origin = jnp.clip(origin, 0, Z - 1)
        return pltpu.make_async_remote_copy(
            src_ref=panels.at[origin],
            dst_ref=panels.at[origin],
            send_sem=zsend_sem.at[way, s],
            recv_sem=zrecv_sem.at[way, s],
            device_id=(to, me_b),
            device_id_type=MESH,
        )

    def panel_leaves(way, s):
        return (z - s + 1 >= 0) & has_next if way == 0 else (z + s - 1 < Z) & has_prev

    def panel_arrives(way, s):
        return z - s >= 0 if way == 0 else z + s < Z

    def start_panels(s):
        for way in range(2):

            @pl.when(panel_leaves(way, s))
            def _():
                panel_copy(way, s).start()

    def await_panels(s):
        for way in range(2):

            @pl.when(panel_arrives(way, s))
            def _():
                origin = jnp.clip(z - s if way == 0 else z + s, 0, Z - 1)
                pltpu.make_async_remote_copy(
                    src_ref=panels.at[origin],
                    dst_ref=panels.at[origin],
                    send_sem=zsend_sem.at[way, s],
                    recv_sem=zrecv_sem.at[way, s],
                    device_id=(jnp.where(has_next, me_a + 1, me_a - 1), me_b),
                    device_id_type=MESH,
                ).wait_recv()

    def sent_panels(s):
        for way in range(2):

            @pl.when(panel_leaves(way, s))
            def _():
                panel_copy(way, s).wait_send()

    def share_copy(i):
        return pltpu.make_async_remote_copy(
            src_ref=share.at[i],
            dst_ref=shares.at[i],
            send_sem=xsend_sem.at[i],
            recv_sem=xrecv_sem.at[i],
            device_id=(lax.rem(x + i, X) * Z + z, me_b),
            device_id_type=MESH,
        )

    def pack_first(k, _):
        pack(k)
        return 0

    lax.fori_loop(0, 2, pack_first, 0)
    for w in range(2):
        first_leg(0, w).start()
    if Z > 1:
        start_panels(1)

    def pack_and_send(k, _):
        pack(k)
        exchange(0, k).start()
        return 0

    lax.fori_loop(2, own, pack_and_send, 0)
    pack_and_send(own + 1, 0)
    pack(own)
    for h in range(NCH):
        for r in range(2):
            recv[h][2 * own + r] = send[h][2 * own + r]

    def placed(i, _):
        s = sdev[me_b * SLOTS + i]
        rank = jnp.int32(0)
        for other in range(SLOTS):
            same = (sdev[me_b * SLOTS + other] == s) & (other < i)
            rank = rank + jnp.where(same, 1, 0)
        dy = lax.rem(y - (s >> 1) + Y, Y)
        pos = jnp.where(dy < Y // 2, Y - 1 - 2 * dy, 2 * dy - Y)
        k = pos * 2 + ((s + c) & 1)
        rank = jnp.minimum(rank, 1)
        locs[i] = jnp.where(k < 2, k + 2 * rank, 2 * k + rank)
        return 0

    lax.fori_loop(0, SLOTS, placed, 0)

    adiag[...] = jnp.broadcast_to(ad[...], (BLK, BLK)).T

    for load in tile_loads:
        load.wait()

    def negate(i, _):
        at[16 + i] = -at[i]
        bt[16 + i] = -bt[i]
        return 0

    lax.fori_loop(0, 16, negate, 0)
    at[32] = jnp.zeros((BLK, BLK), BF16)

    def pass_on(h):
        for w in range(2):
            first_leg(h, w).wait_recv()
            for flip in range(2):
                second_leg(h, w, flip).start()

    pass_on(0)

    def next_panels(s, _):
        await_panels(s)

        @pl.when(s < Z - 1)
        def _():
            start_panels(s + 1)

        return 0

    lax.fori_loop(1, Z, next_panels, 0)

    def share_of(i):
        target = lax.rem(x + i, X) * Z + z
        tiles, sources = [], []
        for e in range(EA):
            s = asrc[e, target]
            here = lax.div(s, Z) == x
            tiles.append(at[jnp.where(here, akind[e, target] + 16 * apar[e, target], 32)])
            sources.append(panels[lax.rem(s, Z)])
        return jnp.dot(
            jnp.concatenate(tiles, axis=1), jnp.concatenate(sources, axis=0), preferred_element_type=F32
        )

    for i in range(1, X):
        share[i] = share_of(i).astype(BF16)
        share_copy(i).start()
    inner = share_of(0)
    for i in range(1, X):
        share_copy(i).wait_recv()
        inner = inner + shares[i].astype(F32)
    inner = jnp.concatenate([inner[:, :BLK], inner[:, BLK:]], axis=0)
    coarse = inner.astype(BF16)
    fine = (inner - coarse.astype(F32)).astype(BF16)
    closing = bt[mkind[0]]
    mixed[...] = jnp.dot(
        jnp.concatenate([coarse, fine], axis=1),
        jnp.concatenate([closing, closing], axis=0),
        preferred_element_type=F32,
    )

    for h in range(1, NCH):
        for w in range(2):
            first_leg(h - 1, w).wait_send()
            first_leg(h, w).start()

        def follow(k, _):
            exchange(h - 1, k).wait_send()
            exchange(h, k).start()
            return 0

        lax.fori_loop(2, own, follow, 0)
        follow(own + 1, 0)
        pass_on(h)

    def finish(h):
        row, count = CHUNKS[h]
        rows = pl.ds(row, count)

        def arrive(k, _):
            exchange(h, k).wait_recv()
            return 0

        lax.fori_loop(2, own, arrive, 0)
        arrive(own + 1, 0)
        for w in range(2):
            for flip in range(2):
                second_leg(h, w, flip).wait_recv()

        def block(j, _):
            pieces, tiles = [], []
            for e in range(EB):
                pieces.append(recv[h][locs[bslot[j, e]]])
                tiles.append(bt[bkind[j, e] + 16 * bpar[j, e]])
            same = jnp.dot(
                jnp.concatenate(pieces, axis=1), jnp.concatenate(tiles, axis=0), preferred_element_type=F32
            )
            columns = pl.ds(pl.multiple_of(j * BLK, BLK), BLK)
            parts = []
            for start in range(row, row + count, 32):
                parts.append(adiag[pl.ds(start % BLK, 32), :])
            energies = jnp.concatenate(parts, axis=0) + bd[pl.ds(j, 1), :]
            struck = jnp.where(j == active, 1.0, 0.0).astype(F32)
            total = energies * coef[j, rows, :].astype(F32) + same + struck * mixed[rows, :]
            out[rows, columns] = (total * occ[0, j].astype(F32)).astype(BF16)
            return 0

        lax.fori_loop(0, NBLK, block, 0)

    for h in range(NCH):
        finish(h)

    last = NCH - 1

    def sent(k, _):
        exchange(last, k).wait_send()
        return 0

    lax.fori_loop(2, own, sent, 0)
    sent(own + 1, 0)
    for w in range(2):
        first_leg(last, w).wait_send()
        for h in range(NCH):
            for flip in range(2):
                second_leg(h, w, flip).wait_send()
    def left_panels(s, _):
        sent_panels(s)
        return 0

    lax.fori_loop(1, Z, left_panels, 0)
    for i in range(1, X):
        share_copy(i).wait_send()


def solution(mesh):
    n_alpha, n_beta = mesh.shape["alpha"], mesh.shape["beta"]
    Z = 8 if n_alpha == 32 else 1
    X, Y = n_alpha // Z, n_beta // 2

    def local(
        coef,
        alpha_diag,
        beta_diag,
        alpha_tiles,
        beta_tiles,
        occupancy,
        alpha_source,
        alpha_kind,
        alpha_parity,
        slot_device,
        slot_offset,
        beta_slot,
        beta_kind,
        beta_parity,
        mixed_block,
        mixed_kind,
    ):
        vmem = pl.BlockSpec(memory_space=pltpu.VMEM)
        hbm = pl.BlockSpec(memory_space=pl.ANY)
        columns = coef.shape[-1]
        small = (
            occupancy,
            alpha_source.T,
            alpha_kind.T,
            alpha_parity.T,
            slot_device.reshape(-1),
            slot_offset,
            beta_slot,
            beta_kind,
            beta_parity,
            mixed_block,
            mixed_kind,
            alpha_diag.reshape(1, BLK),
            beta_diag.reshape(NBLK, BLK),
        )
        result = pl.pallas_call(
            functools.partial(kernel, X, Z, Y),
            out_shape=jax.ShapeDtypeStruct((ROWS, columns), BF16),
            in_specs=[hbm] * (len(small) + 3),
            out_specs=vmem,
            scratch_shapes=[
                *(pltpu.SMEM(v.shape, v.dtype) for v in small[:11]),
                *(pltpu.VMEM(v.shape, v.dtype) for v in small[11:]),
                pltpu.VMEM((NBLK, ROWS, BLK), BF16),
                pltpu.VMEM((33, BLK, BLK), BF16),
                pltpu.VMEM((32, BLK, BLK), BF16),
                pltpu.VMEM((Z, BLK, ROWS), BF16),
                pltpu.VMEM((X, BLK, ROWS), BF16),
                pltpu.VMEM((X, BLK, ROWS), BF16),
                pltpu.VMEM((BLK, BLK), F32),
                pltpu.VMEM((ROWS, BLK), F32),
                pltpu.SMEM((SLOTS,), jnp.int32),
                *(pltpu.VMEM((2 * n_beta, count, BLK), BF16) for _, count in CHUNKS),
                *(pltpu.VMEM((2 * n_beta, count, BLK), BF16) for _, count in CHUNKS),
                *(pltpu.VMEM((4, count, BLK), BF16) for _, count in CHUNKS),
                pltpu.SemaphoreType.DMA((len(small),)),
                pltpu.SemaphoreType.DMA((NBLK + 2,)),
                pltpu.SemaphoreType.DMA((NCH, n_beta)),
                pltpu.SemaphoreType.DMA((NCH, n_beta)),
                pltpu.SemaphoreType.DMA((NCH, 2)),
                pltpu.SemaphoreType.DMA((NCH, 2)),
                pltpu.SemaphoreType.DMA((NCH, 4)),
                pltpu.SemaphoreType.DMA((NCH, 4)),
                pltpu.SemaphoreType.DMA((2, Z)),
                pltpu.SemaphoreType.DMA((2, Z)),
                pltpu.SemaphoreType.DMA((X,)),
                pltpu.SemaphoreType.DMA((X,)),
            ],
            compiler_params=pltpu.CompilerParams(
                collective_id=0, has_side_effects=True, vmem_limit_bytes=60 * 1024 * 1024
            ),
            cost_estimate=pl.CostEstimate(flops=2200000000, bytes_accessed=3300000, transcendentals=0),
        )(
            *small,
            coef.reshape(ROWS, columns),
            alpha_tiles,
            beta_tiles,
        )
        return result.reshape(coef.shape)

    in_specs = (
        P(None, "alpha", "beta"),
        P("alpha"),
        P("beta"),
        P(),
        P(),
        P("alpha", "beta"),
        P(),
        P(),
        P(),
        P(),
        P(),
        P("beta", None),
        P("beta", None),
        P("beta", None),
        P("beta"),
        P("beta"),
    )
    out_specs = P(None, "alpha", "beta")
    return jax.shard_map(local, mesh=mesh, in_specs=in_specs, out_specs=out_specs, check_vma=False)
```

```python
import functools

import jax
import jax.numpy as jnp
from jax import lax
from jax.experimental import pallas as pl
from jax.experimental.pallas import tpu as pltpu
from jax.sharding import PartitionSpec as P

MESH = pl.DeviceIdType.MESH
BLK = 128
NBLK = 16
SLOTS = 16
EB = 16
EA = 4
ROWS = 2 * BLK
CHUNKS = ((0, 160), (160, 96))
NCH = len(CHUNKS)
F32 = jnp.float32
BF16 = jnp.bfloat16


def kernel(X, Z, Y, *refs):
    small_hbm, (coef_hbm, at_hbm, bt_hbm, out), small = refs[:13], refs[13:17], refs[17:30]
    occ, asrc, akind, apar, sdev, soff, bslot, bkind, bpar, mblk, mkind, ad, bd = small
    coef, at, bt, panels, share, shares, adiag, mixed, locs = refs[30:39]
    send, recv, relay = (refs[39 + NCH * i : 39 + NCH * (i + 1)] for i in range(3))
    (
        small_sem,
        local_sem,
        send_sem,
        recv_sem,
        out_sem,
        in_sem,
        on_sem,
        end_sem,
        zsend_sem,
        zrecv_sem,
        xsend_sem,
        xrecv_sem,
    ) = refs[39 + 3 * NCH :]
    NB = 2 * Y
    me_a = lax.axis_index("alpha")
    me_b = lax.axis_index("beta")
    x, z = me_a // Z, lax.rem(me_a, Z)
    y, c = me_b // 2, lax.rem(me_b, 2)

    small_loads = [
        pltpu.make_async_copy(src, dst, small_sem.at[i]) for i, (src, dst) in enumerate(zip(small_hbm, small))
    ]
    for load in small_loads:
        load.start()

    def block_load(j):
        columns = pl.ds(pl.multiple_of(j * BLK, BLK), BLK)
        return pltpu.make_async_copy(coef_hbm.at[:, columns], coef.at[j], local_sem.at[j])

    tile_loads = [
        pltpu.make_async_copy(at_hbm, at.at[pl.ds(0, 16)], local_sem.at[NBLK]),
        pltpu.make_async_copy(bt_hbm, bt.at[pl.ds(0, 16)], local_sem.at[NBLK + 1]),
    ]

    def load_block(j, _):
        block_load(j).start()
        return 0

    lax.fori_loop(0, NBLK, load_block, 0)
    for load in tile_loads:
        load.start()

    def step_of(k):
        p = k // 2
        dist = (Y - p) // 2
        dy = jnp.where(lax.rem(p, 2) == 1, dist, Y - dist)
        return dy, lax.rem(k, 2)

    def peer(k):
        dy, flip = step_of(k)
        return lax.rem(y + dy, Y) * 2 + lax.rem(c + flip, 2)

    own = NB - 2

    barrier = pltpu.get_barrier_semaphore()

    def greet_beta(i, _):
        pl.semaphore_signal(barrier, 1, device_id=(me_a, lax.rem(me_b + i, NB)), device_id_type=MESH)
        return 0

    lax.fori_loop(1, NB, greet_beta, 0)

    has_next, has_prev = z < Z - 1, z > 0

    @pl.when(has_next)
    def _():
        pl.semaphore_signal(barrier, 1, device_id=(me_a + 1, me_b), device_id_type=MESH)

    @pl.when(has_prev)
    def _():
        pl.semaphore_signal(barrier, 1, device_id=(me_a - 1, me_b), device_id_type=MESH)

    def greet_x(i, _):
        pl.semaphore_signal(barrier, 1, device_id=(lax.rem(x + i, X) * Z + z, me_b), device_id_type=MESH)
        return 0

    lax.fori_loop(1, X, greet_x, 0)

    for load in small_loads:
        load.wait()

    def await_block(j, _):
        block_load(j).wait()
        return 0

    lax.fori_loop(0, NBLK, await_block, 0)

    def panel_of(block, allowed):
        panel = coef[block]
        return jnp.where(allowed, panel, jnp.zeros_like(panel))

    active = mblk[0]
    mine = panel_of(active, occ[0, active] > 0)
    panels[z] = jnp.concatenate([mine[:BLK], mine[BLK:]], axis=1)

    def pack(k):
        d = peer(k)
        code = jnp.int32(0)
        for i in range(SLOTS):
            hit = sdev[d * SLOTS + i] == me_b
            code = jnp.where(hit, code * 32 + soff[d * SLOTS + i] + 1, code)
        hi, lo = code >> 5, code & 31
        first = jnp.where(hi > 0, hi, lo)
        second = jnp.where(hi > 0, lo, 0)
        for r, named in enumerate((first, second)):
            block = jnp.clip(named - 1, 0, NBLK - 1)
            panel = panel_of(block, (named > 0) & (occ[0, block] > 0))
            place = jnp.where(k < 2, k + 2 * r, 2 * k + r)
            for h, (row, count) in enumerate(CHUNKS):
                send[h][place] = panel[row : row + count]

    pl.semaphore_wait(barrier, NB - 1 + X - 1 + jnp.where(has_next, 1, 0) + jnp.where(has_prev, 1, 0))

    def exchange(h, k):
        return pltpu.make_async_remote_copy(
            src_ref=send[h].at[pl.ds(2 * k, 2)],
            dst_ref=recv[h].at[pl.ds(2 * k, 2)],
            send_sem=send_sem.at[h, k],
            recv_sem=recv_sem.at[h, k],
            device_id=(me_a, peer(k)),
            device_id_type=MESH,
        )

    leg = Y // 4

    def first_leg(h, w):
        chip = lax.rem(y + (leg if w == 0 else Y - leg), Y)
        return pltpu.make_async_remote_copy(
            src_ref=send[h].at[pl.ds(2 * w, 2)],
            dst_ref=relay[h].at[pl.ds(2 * w, 2)],
            send_sem=out_sem.at[h, w],
            recv_sem=in_sem.at[h, w],
            device_id=(me_a, chip * 2 + c),
            device_id_type=MESH,
        )

    def second_leg(h, w, flip):
        chip = lax.rem(y + (leg if w == 0 else Y - leg), Y)
        return pltpu.make_async_remote_copy(
            src_ref=relay[h].at[2 * w + flip],
            dst_ref=recv[h].at[2 * w + flip],
            send_sem=on_sem.at[h, 2 * w + flip],
            recv_sem=end_sem.at[h, 2 * w + flip],
            device_id=(me_a, chip * 2 + lax.rem(c + flip, 2)),
            device_id_type=MESH,
        )

    def panel_copy(way, s):
        origin, to = (z - s + 1, me_a + 1) if way == 0 else (z + s - 1, me_a - 1)
        origin = jnp.clip(origin, 0, Z - 1)
        return pltpu.make_async_remote_copy(
            src_ref=panels.at[origin],
            dst_ref=panels.at[origin],
            send_sem=zsend_sem.at[way, s],
            recv_sem=zrecv_sem.at[way, s],
            device_id=(to, me_b),
            device_id_type=MESH,
        )

    def panel_leaves(way, s):
        return (z - s + 1 >= 0) & has_next if way == 0 else (z + s - 1 < Z) & has_prev

    def panel_arrives(way, s):
        return z - s >= 0 if way == 0 else z + s < Z

    def start_panels(s):
        for way in range(2):

            @pl.when(panel_leaves(way, s))
            def _():
                panel_copy(way, s).start()

    def await_panels(s):
        for way in range(2):

            @pl.when(panel_arrives(way, s))
            def _():
                origin = jnp.clip(z - s if way == 0 else z + s, 0, Z - 1)
                pltpu.make_async_remote_copy(
                    src_ref=panels.at[origin],
                    dst_ref=panels.at[origin],
                    send_sem=zsend_sem.at[way, s],
                    recv_sem=zrecv_sem.at[way, s],
                    device_id=(jnp.where(has_next, me_a + 1, me_a - 1), me_b),
                    device_id_type=MESH,
                ).wait_recv()

    def sent_panels(s):
        for way in range(2):

            @pl.when(panel_leaves(way, s))
            def _():
                panel_copy(way, s).wait_send()

    def share_copy(i):
        return pltpu.make_async_remote_copy(
            src_ref=share.at[i],
            dst_ref=shares.at[i],
            send_sem=xsend_sem.at[i],
            recv_sem=xrecv_sem.at[i],
            device_id=(lax.rem(x + i, X) * Z + z, me_b),
            device_id_type=MESH,
        )

    def pack_first(k, _):
        pack(k)
        return 0

    lax.fori_loop(0, 2, pack_first, 0)
    for h in range(NCH):
        for w in range(2):
            first_leg(h, w).start()
    if Z > 1:
        start_panels(1)

    def pack_and_send(k, _):
        pack(k)
        exchange(0, k).start()
        return 0

    lax.fori_loop(2, own, pack_and_send, 0)
    pack_and_send(own + 1, 0)

    def send_later(k, _):
        for h in range(1, NCH):
            exchange(h, k).start()
        return 0

    lax.fori_loop(2, own, send_later, 0)
    send_later(own + 1, 0)
    pack(own)
    for h in range(NCH):
        for r in range(2):
            recv[h][2 * own + r] = send[h][2 * own + r]

    def placed(i, _):
        s = sdev[me_b * SLOTS + i]
        rank = jnp.int32(0)
        for other in range(SLOTS):
            same = (sdev[me_b * SLOTS + other] == s) & (other < i)
            rank = rank + jnp.where(same, 1, 0)
        dy = lax.rem(y - (s >> 1) + Y, Y)
        pos = jnp.where(dy < Y // 2, Y - 1 - 2 * dy, 2 * dy - Y)
        k = pos * 2 + ((s + c) & 1)
        rank = jnp.minimum(rank, 1)
        locs[i] = jnp.where(k < 2, k + 2 * rank, 2 * k + rank)
        return 0

    lax.fori_loop(0, SLOTS, placed, 0)

    adiag[...] = jnp.broadcast_to(ad[...], (BLK, BLK)).T

    for load in tile_loads:
        load.wait()

    def negate(i, _):
        at[16 + i] = -at[i]
        bt[16 + i] = -bt[i]
        return 0

    lax.fori_loop(0, 16, negate, 0)
    at[32] = jnp.zeros((BLK, BLK), BF16)

    def pass_on(h):
        for w in range(2):
            first_leg(h, w).wait_recv()
            for flip in range(2):
                second_leg(h, w, flip).start()

    pass_on(0)

    def next_panels(s, _):
        await_panels(s)

        @pl.when(s < Z - 1)
        def _():
            start_panels(s + 1)

        return 0

    lax.fori_loop(1, Z, next_panels, 0)

    def share_of(i):
        target = lax.rem(x + i, X) * Z + z
        tiles, sources = [], []
        for e in range(EA):
            s = asrc[e, target]
            here = lax.div(s, Z) == x
            tiles.append(at[jnp.where(here, akind[e, target] + 16 * apar[e, target], 32)])
            sources.append(panels[lax.rem(s, Z)])
        return jnp.dot(
            jnp.concatenate(tiles, axis=1), jnp.concatenate(sources, axis=0), preferred_element_type=F32
        )

    for i in range(1, X):
        share[i] = share_of(i).astype(BF16)
        share_copy(i).start()
    inner = share_of(0)
    for i in range(1, X):
        share_copy(i).wait_recv()
        inner = inner + shares[i].astype(F32)
    inner = jnp.concatenate([inner[:, :BLK], inner[:, BLK:]], axis=0)
    coarse = inner.astype(BF16)
    fine = (inner - coarse.astype(F32)).astype(BF16)
    closing = bt[mkind[0]]
    mixed[...] = jnp.dot(
        jnp.concatenate([coarse, fine], axis=1),
        jnp.concatenate([closing, closing], axis=0),
        preferred_element_type=F32,
    )

    for h in range(1, NCH):
        pass_on(h)

    def finish(h):
        row, count = CHUNKS[h]
        rows = pl.ds(row, count)

        def arrive(k, _):
            exchange(h, k).wait_recv()
            return 0

        lax.fori_loop(2, own, arrive, 0)
        arrive(own + 1, 0)
        for w in range(2):
            for flip in range(2):
                second_leg(h, w, flip).wait_recv()

        def block(j, _):
            pieces, tiles = [], []
            for e in range(EB):
                pieces.append(recv[h][locs[bslot[j, e]]])
                tiles.append(bt[bkind[j, e] + 16 * bpar[j, e]])
            same = jnp.dot(
                jnp.concatenate(pieces, axis=1), jnp.concatenate(tiles, axis=0), preferred_element_type=F32
            )
            columns = pl.ds(pl.multiple_of(j * BLK, BLK), BLK)
            parts = []
            for start in range(row, row + count, 32):
                parts.append(adiag[pl.ds(start % BLK, 32), :])
            energies = jnp.concatenate(parts, axis=0) + bd[pl.ds(j, 1), :]
            struck = jnp.where(j == active, 1.0, 0.0).astype(F32)
            total = energies * coef[j, rows, :].astype(F32) + same + struck * mixed[rows, :]
            out[rows, columns] = (total * occ[0, j].astype(F32)).astype(BF16)
            return 0

        lax.fori_loop(0, NBLK, block, 0)

    for h in range(NCH):
        finish(h)

    def sent(k, _):
        for h in range(NCH):
            exchange(h, k).wait_send()
        return 0

    lax.fori_loop(2, own, sent, 0)
    sent(own + 1, 0)
    for h in range(NCH):
        for w in range(2):
            first_leg(h, w).wait_send()
            for flip in range(2):
                second_leg(h, w, flip).wait_send()

    def left_panels(s, _):
        sent_panels(s)
        return 0

    lax.fori_loop(1, Z, left_panels, 0)
    for i in range(1, X):
        share_copy(i).wait_send()


def hand_over(result, out):
    out[...] = result[...]


def solution(mesh):
    n_alpha, n_beta = mesh.shape["alpha"], mesh.shape["beta"]
    Z = 8 if n_alpha == 32 else 1
    X, Y = n_alpha // Z, n_beta // 2

    def local(
        coef,
        alpha_diag,
        beta_diag,
        alpha_tiles,
        beta_tiles,
        occupancy,
        alpha_source,
        alpha_kind,
        alpha_parity,
        slot_device,
        slot_offset,
        beta_slot,
        beta_kind,
        beta_parity,
        mixed_block,
        mixed_kind,
    ):
        vmem = pl.BlockSpec(memory_space=pltpu.VMEM)
        hbm = pl.BlockSpec(memory_space=pl.ANY)
        columns = coef.shape[-1]
        small = (
            occupancy,
            alpha_source.T,
            alpha_kind.T,
            alpha_parity.T,
            slot_device.reshape(-1),
            slot_offset,
            beta_slot,
            beta_kind,
            beta_parity,
            mixed_block,
            mixed_kind,
            alpha_diag.reshape(1, BLK),
            beta_diag.reshape(NBLK, BLK),
        )
        result = pl.pallas_call(
            functools.partial(kernel, X, Z, Y),
            out_shape=jax.ShapeDtypeStruct((ROWS, columns), BF16),
            in_specs=[hbm] * (len(small) + 3),
            out_specs=vmem,
            scratch_shapes=[
                *(pltpu.SMEM(v.shape, v.dtype) for v in small[:11]),
                *(pltpu.VMEM(v.shape, v.dtype) for v in small[11:]),
                pltpu.VMEM((NBLK, ROWS, BLK), BF16),
                pltpu.VMEM((33, BLK, BLK), BF16),
                pltpu.VMEM((32, BLK, BLK), BF16),
                pltpu.VMEM((Z, BLK, ROWS), BF16),
                pltpu.VMEM((X, BLK, ROWS), BF16),
                pltpu.VMEM((X, BLK, ROWS), BF16),
                pltpu.VMEM((BLK, BLK), F32),
                pltpu.VMEM((ROWS, BLK), F32),
                pltpu.SMEM((SLOTS,), jnp.int32),
                *(pltpu.VMEM((2 * n_beta, count, BLK), BF16) for _, count in CHUNKS),
                *(pltpu.VMEM((2 * n_beta, count, BLK), BF16) for _, count in CHUNKS),
                *(pltpu.VMEM((4, count, BLK), BF16) for _, count in CHUNKS),
                pltpu.SemaphoreType.DMA((len(small),)),
                pltpu.SemaphoreType.DMA((NBLK + 2,)),
                pltpu.SemaphoreType.DMA((NCH, n_beta)),
                pltpu.SemaphoreType.DMA((NCH, n_beta)),
                pltpu.SemaphoreType.DMA((NCH, 2)),
                pltpu.SemaphoreType.DMA((NCH, 2)),
                pltpu.SemaphoreType.DMA((NCH, 4)),
                pltpu.SemaphoreType.DMA((NCH, 4)),
                pltpu.SemaphoreType.DMA((2, Z)),
                pltpu.SemaphoreType.DMA((2, Z)),
                pltpu.SemaphoreType.DMA((X,)),
                pltpu.SemaphoreType.DMA((X,)),
            ],
            compiler_params=pltpu.CompilerParams(
                collective_id=0, has_side_effects=True, vmem_limit_bytes=60 * 1024 * 1024
            ),
            cost_estimate=pl.CostEstimate(flops=2200000000, bytes_accessed=3300000, transcendentals=0),
        )(
            *small,
            coef.reshape(ROWS, columns),
            alpha_tiles,
            beta_tiles,
        )
        strip = pl.BlockSpec((ROWS // 4, columns), lambda i: (i, 0))
        result = pl.pallas_call(
            hand_over,
            out_shape=jax.ShapeDtypeStruct((ROWS, columns), BF16),
            grid=(4,),
            in_specs=[strip],
            out_specs=strip,
            compiler_params=pltpu.CompilerParams(vmem_limit_bytes=60 * 1024 * 1024),
            cost_estimate=pl.CostEstimate(flops=0, bytes_accessed=2097152, transcendentals=0),
        )(result)
        return result.reshape(coef.shape)

    in_specs = (
        P(None, "alpha", "beta"),
        P("alpha"),
        P("beta"),
        P(),
        P(),
        P("alpha", "beta"),
        P(),
        P(),
        P(),
        P(),
        P(),
        P("beta", None),
        P("beta", None),
        P("beta", None),
        P("beta"),
        P("beta"),
    )
    out_specs = P(None, "alpha", "beta")
    return jax.shard_map(local, mesh=mesh, in_specs=in_specs, out_specs=out_specs, check_vma=False)
```

```python
import functools

import jax
import jax.numpy as jnp
from jax import lax
from jax.experimental import pallas as pl
from jax.experimental.pallas import tpu as pltpu
from jax.sharding import PartitionSpec as P

MESH = pl.DeviceIdType.MESH
BLK = 128
NBLK = 16
SLOTS = 16
EB = 16
EA = 4
ROWS = 2 * BLK
ORDERS = {
    4: ((1, 2), (1, 1), (2, 2)),
    8: ((1, 4), (1, 3), (1, 2), (2, 4), (2, 3), (1, 1), (3, 4), (2, 2), (3, 3), (4, 4)),
}
IN_FLIGHT = 3
F32 = jnp.float32
BF16 = jnp.bfloat16


def kernel(X, Z, Y, *refs):
    small_hbm, (coef_hbm, at_hbm, bt_hbm, out), small = refs[:13], refs[13:17], refs[17:30]
    occ, asrc, akind, apar, sdev, soff, bslot, bkind, bpar, mblk, mkind, ad, bd = small
    coef, at, bt, panels, share, shares, adiag, mixed, locs, send, recv, passing = refs[30:42]
    (
        small_sem,
        local_sem,
        send_sem,
        recv_sem,
        side_sem,
        zsend_sem,
        zrecv_sem,
        xsend_sem,
        xrecv_sem,
    ) = refs[42:]
    NB = 2 * Y
    me_a = lax.axis_index("alpha")
    me_b = lax.axis_index("beta")
    x, z = me_a // Z, lax.rem(me_a, Z)
    y, c = me_b // 2, lax.rem(me_b, 2)

    small_loads = [
        pltpu.make_async_copy(src, dst, small_sem.at[i]) for i, (src, dst) in enumerate(zip(small_hbm, small))
    ]
    for load in small_loads:
        load.start()

    def block_load(j):
        columns = pl.ds(pl.multiple_of(j * BLK, BLK), BLK)
        return pltpu.make_async_copy(coef_hbm.at[:, columns], coef.at[j], local_sem.at[j])

    tile_loads = [
        pltpu.make_async_copy(at_hbm, at.at[pl.ds(0, 16)], local_sem.at[NBLK]),
        pltpu.make_async_copy(bt_hbm, bt.at[pl.ds(0, 16)], local_sem.at[NBLK + 1]),
    ]

    def load_block(j, _):
        block_load(j).start()
        return 0

    lax.fori_loop(0, NBLK, load_block, 0)
    for load in tile_loads:
        load.start()

    def peer(p, flip):
        dist = (Y - p) // 2
        dy = jnp.where(lax.rem(p, 2) == 1, dist, Y - dist)
        return lax.rem(y + dy, Y) * 2 + lax.rem(c + flip, 2)

    M = Y // 2
    own = Y - 1
    order = ORDERS[Y]
    up, down = lax.rem(y + 1, Y) * 2, lax.rem(y + Y - 1, Y) * 2

    barrier = pltpu.get_barrier_semaphore()

    for neighbour in (up, up + 1, down, down + 1, y * 2 + 1 - c):
        pl.semaphore_signal(barrier, 1, device_id=(me_a, neighbour), device_id_type=MESH)

    has_next, has_prev = z < Z - 1, z > 0

    @pl.when(has_next)
    def _():
        pl.semaphore_signal(barrier, 1, device_id=(me_a + 1, me_b), device_id_type=MESH)

    @pl.when(has_prev)
    def _():
        pl.semaphore_signal(barrier, 1, device_id=(me_a - 1, me_b), device_id_type=MESH)

    def greet_x(i, _):
        pl.semaphore_signal(barrier, 1, device_id=(lax.rem(x + i, X) * Z + z, me_b), device_id_type=MESH)
        return 0

    lax.fori_loop(1, X, greet_x, 0)

    for load in small_loads:
        load.wait()

    def await_block(j, _):
        block_load(j).wait()
        return 0

    lax.fori_loop(0, NBLK, await_block, 0)

    def panel_of(block, allowed):
        panel = coef[block]
        return jnp.where(allowed, panel, jnp.zeros_like(panel))

    active = mblk[0]
    mine = panel_of(active, occ[0, active] > 0)
    panels[z] = jnp.concatenate([mine[:BLK], mine[BLK:]], axis=1)

    def pack(p):
        def one(flip, _):
            d = peer(p, flip)
            code = jnp.int32(0)
            for i in range(SLOTS):
                hit = sdev[d * SLOTS + i] == me_b
                code = jnp.where(hit, code * 32 + soff[d * SLOTS + i] + 1, code)
            hi, lo = code >> 5, code & 31
            first = jnp.where(hi > 0, hi, lo)
            second = jnp.where(hi > 0, lo, 0)
            for r, named in enumerate((first, second)):
                block = jnp.clip(named - 1, 0, NBLK - 1)
                panel = panel_of(block, (named > 0) & (occ[0, block] > 0))
                send[(flip + 2 * r) if p == 0 else (4 * p + 2 * flip + r)] = panel
            return 0

        lax.fori_loop(0, 2, one, 0)

    pl.semaphore_wait(barrier, 5 + X - 1 + jnp.where(has_next, 1, 0) + jnp.where(has_prev, 1, 0))

    places, count = {}, 0
    for hop in range(1, M):
        for dist in range(M, hop, -1):
            places[hop, dist] = count
            count += 2 if dist == M else 4

    def message(way, i):
        hop, dist = order[i]
        p = 0 if dist == M else Y - 1 - 2 * dist if way == 0 else Y - 2 * dist
        size = 2 if dist == M else 4
        first = 2 * way if dist == M else 4 * p
        chip = up if way == 0 else down

        def leg(src, at_, dst, to_at, length, core, flip):
            return pltpu.make_async_remote_copy(
                src_ref=src.at[pl.ds(at_, length)],
                dst_ref=dst.at[pl.ds(to_at, length)],
                send_sem=send_sem.at[way, i, flip],
                recv_sem=recv_sem.at[way, i, flip],
                device_id=(me_a, chip + core),
                device_id_type=MESH,
            )

        src, begin = (send, first) if hop == 1 else (passing.at[way], places[hop - 1, dist])
        if hop < dist:
            return [leg(src, begin, passing.at[way], places[hop, dist], size, c, 0)]
        half = size // 2
        return [
            leg(src, begin + half * flip, recv, first + half * flip, half, lax.rem(c + flip, 2), flip)
            for flip in range(2)
        ]

    def side_copy():
        return pltpu.make_async_remote_copy(
            src_ref=send.at[pl.ds(4 * own + 2, 2)],
            dst_ref=recv.at[pl.ds(4 * own + 2, 2)],
            send_sem=side_sem.at[0],
            recv_sem=side_sem.at[1],
            device_id=(me_a, y * 2 + 1 - c),
            device_id_type=MESH,
        )

    def advance(i):
        for way in range(2):
            hop, dist = order[i]
            if hop > 1:
                for copy in message(way, order.index((hop - 1, dist))):
                    copy.wait_recv()
            if i >= IN_FLIGHT:
                for copy in message(way, i - IN_FLIGHT):
                    copy.wait_send()
            for copy in message(way, i):
                copy.start()

    def panel_copy(way, s):
        origin, to = (z - s + 1, me_a + 1) if way == 0 else (z + s - 1, me_a - 1)
        origin = jnp.clip(origin, 0, Z - 1)
        return pltpu.make_async_remote_copy(
            src_ref=panels.at[origin],
            dst_ref=panels.at[origin],
            send_sem=zsend_sem.at[way, s],
            recv_sem=zrecv_sem.at[way, s],
            device_id=(to, me_b),
            device_id_type=MESH,
        )

    def panel_leaves(way, s):
        return (z - s + 1 >= 0) & has_next if way == 0 else (z + s - 1 < Z) & has_prev

    def panel_arrives(way, s):
        return z - s >= 0 if way == 0 else z + s < Z

    def start_panels(s):
        for way in range(2):

            @pl.when(panel_leaves(way, s))
            def _():
                panel_copy(way, s).start()

    def await_panels(s):
        for way in range(2):

            @pl.when(panel_arrives(way, s))
            def _():
                origin = jnp.clip(z - s if way == 0 else z + s, 0, Z - 1)
                pltpu.make_async_remote_copy(
                    src_ref=panels.at[origin],
                    dst_ref=panels.at[origin],
                    send_sem=zsend_sem.at[way, s],
                    recv_sem=zrecv_sem.at[way, s],
                    device_id=(jnp.where(has_next, me_a + 1, me_a - 1), me_b),
                    device_id_type=MESH,
                ).wait_recv()

    def sent_panels(s):
        for way in range(2):

            @pl.when(panel_leaves(way, s))
            def _():
                panel_copy(way, s).wait_send()

    def share_copy(i):
        return pltpu.make_async_remote_copy(
            src_ref=share.at[i],
            dst_ref=shares.at[i],
            send_sem=xsend_sem.at[i],
            recv_sem=xrecv_sem.at[i],
            device_id=(lax.rem(x + i, X) * Z + z, me_b),
            device_id_type=MESH,
        )

    def next_panels(s):
        if s < Z:
            await_panels(s)
        if s + 1 < Z:
            start_panels(s + 1)

    started = 0
    for p in range(Y):
        pack(p)
        if p == 0 and Z > 1:
            start_panels(1)
        if p % 2 == 0 and started < IN_FLIGHT and order[started][0] == 1:
            advance(started)
            started += 1
    side_copy().start()
    for r in range(2):
        recv[4 * own + r] = send[4 * own + r]

    def placed(i, _):
        s = sdev[me_b * SLOTS + i]
        rank = jnp.int32(0)
        for other in range(SLOTS):
            same = (sdev[me_b * SLOTS + other] == s) & (other < i)
            rank = rank + jnp.where(same, 1, 0)
        dy = lax.rem(y - (s >> 1) + Y, Y)
        p = jnp.where(dy < Y // 2, Y - 1 - 2 * dy, 2 * dy - Y)
        flip = (s + c) & 1
        rank = jnp.minimum(rank, 1)
        locs[i] = jnp.where(p == 0, flip + 2 * rank, 4 * p + 2 * flip + rank)
        return 0

    lax.fori_loop(0, SLOTS, placed, 0)

    adiag[...] = jnp.broadcast_to(ad[...], (BLK, BLK)).T

    for load in tile_loads:
        load.wait()

    def negate(i, _):
        at[16 + i] = -at[i]
        bt[16 + i] = -bt[i]
        return 0

    lax.fori_loop(0, 16, negate, 0)
    at[32] = jnp.zeros((BLK, BLK), BF16)

    step = 1
    for i in range(started, len(order)):
        next_panels(step)
        step += 1
        advance(i)
    for s in range(step, Z):
        next_panels(s)

    def share_of(i):
        target = lax.rem(x + i, X) * Z + z
        tiles, sources = [], []
        for e in range(EA):
            s = asrc[e, target]
            here = lax.div(s, Z) == x
            tiles.append(at[jnp.where(here, akind[e, target] + 16 * apar[e, target], 32)])
            sources.append(panels[lax.rem(s, Z)])
        return jnp.dot(
            jnp.concatenate(tiles, axis=1), jnp.concatenate(sources, axis=0), preferred_element_type=F32
        )

    for i in range(1, X):
        share[i] = share_of(i).astype(BF16)
        share_copy(i).start()
    inner = share_of(0)
    for i in range(1, X):
        share_copy(i).wait_recv()
        inner = inner + shares[i].astype(F32)
    inner = jnp.concatenate([inner[:, :BLK], inner[:, BLK:]], axis=0)
    coarse = inner.astype(BF16)
    fine = (inner - coarse.astype(F32)).astype(BF16)
    closing = bt[mkind[0]]
    mixed[...] = jnp.dot(
        jnp.concatenate([coarse, fine], axis=1),
        jnp.concatenate([closing, closing], axis=0),
        preferred_element_type=F32,
    )

    side_copy().wait_recv()
    for i, (hop, dist) in enumerate(order):
        if hop == dist:
            for way in range(2):
                for copy in message(way, i):
                    copy.wait_recv()

    def finish(j, _):
        pieces, tiles = [], []
        for e in range(EB):
            pieces.append(recv[locs[bslot[j, e]]])
            tiles.append(bt[bkind[j, e] + 16 * bpar[j, e]])
        same = jnp.dot(
            jnp.concatenate(pieces, axis=1), jnp.concatenate(tiles, axis=0), preferred_element_type=F32
        )
        columns = pl.ds(pl.multiple_of(j * BLK, BLK), BLK)
        energies = adiag[...] + bd[pl.ds(j, 1), :]
        struck = jnp.where(j == active, 1.0, 0.0).astype(F32)
        total = jnp.concatenate([energies, energies], axis=0) * coef[j].astype(F32) + same + struck * mixed[...]
        out[:, columns] = (total * occ[0, j].astype(F32)).astype(BF16)
        return 0

    lax.fori_loop(0, NBLK, finish, 0)

    side_copy().wait_send()
    for i in range(max(0, len(order) - IN_FLIGHT), len(order)):
        for way in range(2):
            for copy in message(way, i):
                copy.wait_send()

    def left_panels(s, _):
        sent_panels(s)
        return 0

    lax.fori_loop(1, Z, left_panels, 0)
    for i in range(1, X):
        share_copy(i).wait_send()


def solution(mesh):
    n_alpha, n_beta = mesh.shape["alpha"], mesh.shape["beta"]
    Z = 8 if n_alpha == 32 else 1
    X, Y = n_alpha // Z, n_beta // 2
    waiting = sum(2 if 2 * dist == Y else 4 for hop, dist in ORDERS[Y] if hop < dist)

    def local(
        coef,
        alpha_diag,
        beta_diag,
        alpha_tiles,
        beta_tiles,
        occupancy,
        alpha_source,
        alpha_kind,
        alpha_parity,
        slot_device,
        slot_offset,
        beta_slot,
        beta_kind,
        beta_parity,
        mixed_block,
        mixed_kind,
    ):
        vmem = pl.BlockSpec(memory_space=pltpu.VMEM)
        hbm = pl.BlockSpec(memory_space=pl.ANY)
        columns = coef.shape[-1]
        small = (
            occupancy,
            alpha_source.T,
            alpha_kind.T,
            alpha_parity.T,
            slot_device.reshape(-1),
            slot_offset,
            beta_slot,
            beta_kind,
            beta_parity,
            mixed_block,
            mixed_kind,
            alpha_diag.reshape(1, BLK),
            beta_diag.reshape(NBLK, BLK),
        )
        result = pl.pallas_call(
            functools.partial(kernel, X, Z, Y),
            out_shape=jax.ShapeDtypeStruct((ROWS, columns), BF16),
            in_specs=[hbm] * (len(small) + 3),
            out_specs=vmem,
            scratch_shapes=[
                *(pltpu.SMEM(v.shape, v.dtype) for v in small[:11]),
                *(pltpu.VMEM(v.shape, v.dtype) for v in small[11:]),
                pltpu.VMEM((NBLK, ROWS, BLK), BF16),
                pltpu.VMEM((33, BLK, BLK), BF16),
                pltpu.VMEM((32, BLK, BLK), BF16),
                pltpu.VMEM((Z, BLK, ROWS), BF16),
                pltpu.VMEM((X, BLK, ROWS), BF16),
                pltpu.VMEM((X, BLK, ROWS), BF16),
                pltpu.VMEM((BLK, BLK), F32),
                pltpu.VMEM((ROWS, BLK), F32),
                pltpu.SMEM((SLOTS,), jnp.int32),
                pltpu.VMEM((2 * n_beta, ROWS, BLK), BF16),
                pltpu.VMEM((2 * n_beta, ROWS, BLK), BF16),
                pltpu.VMEM((2, waiting, ROWS, BLK), BF16),
                pltpu.SemaphoreType.DMA((len(small),)),
                pltpu.SemaphoreType.DMA((NBLK + 2,)),
                pltpu.SemaphoreType.DMA((2, len(ORDERS[Y]), 2)),
                pltpu.SemaphoreType.DMA((2, len(ORDERS[Y]), 2)),
                pltpu.SemaphoreType.DMA((2,)),
                pltpu.SemaphoreType.DMA((2, Z)),
                pltpu.SemaphoreType.DMA((2, Z)),
                pltpu.SemaphoreType.DMA((X,)),
                pltpu.SemaphoreType.DMA((X,)),
            ],
            compiler_params=pltpu.CompilerParams(
                collective_id=0, has_side_effects=True, vmem_limit_bytes=60 * 1024 * 1024
            ),
            cost_estimate=pl.CostEstimate(flops=2200000000, bytes_accessed=3300000, transcendentals=0),
        )(
            *small,
            coef.reshape(ROWS, columns),
            alpha_tiles,
            beta_tiles,
        )
        return result.reshape(coef.shape)

    in_specs = (
        P(None, "alpha", "beta"),
        P("alpha"),
        P("beta"),
        P(),
        P(),
        P("alpha", "beta"),
        P(),
        P(),
        P(),
        P(),
        P(),
        P("beta", None),
        P("beta", None),
        P("beta", None),
        P("beta"),
        P("beta"),
    )
    out_specs = P(None, "alpha", "beta")
    return jax.shard_map(local, mesh=mesh, in_specs=in_specs, out_specs=out_specs, check_vma=False)
```

```python
import functools

import jax
import jax.numpy as jnp
from jax import lax
from jax.experimental import pallas as pl
from jax.experimental.pallas import tpu as pltpu
from jax.sharding import PartitionSpec as P

MESH = pl.DeviceIdType.MESH
BLK = 128
NBLK = 16
SLOTS = 16
EB = 16
EA = 4
ROWS = 2 * BLK
ORDERS = {
    4: ((1, 2), (1, 1), (2, 2)),
    8: ((1, 4), (1, 3), (1, 2), (2, 4), (2, 3), (1, 1), (3, 4), (2, 2), (3, 3), (4, 4)),
}
IN_FLIGHT = 3
F32 = jnp.float32
BF16 = jnp.bfloat16


def kernel(X, Z, Y, *refs):
    small_hbm, (coef_hbm, at_hbm, bt_hbm, out), small = refs[:13], refs[13:17], refs[17:30]
    occ, asrc, akind, apar, sdev, soff, bslot, bkind, bpar, mblk, mkind, ad, bd = small
    coef, at, bt, panels, share, shares, adiag, mixed, locs, send, recv, passing, wide, products = refs[30:44]
    (
        small_sem,
        local_sem,
        send_sem,
        recv_sem,
        side_sem,
        zsend_sem,
        zrecv_sem,
        xsend_sem,
        xrecv_sem,
    ) = refs[44:]
    NB = 2 * Y
    me_a = lax.axis_index("alpha")
    me_b = lax.axis_index("beta")
    x, z = me_a // Z, lax.rem(me_a, Z)
    y, c = me_b // 2, lax.rem(me_b, 2)

    small_loads = [
        pltpu.make_async_copy(src, dst, small_sem.at[i]) for i, (src, dst) in enumerate(zip(small_hbm, small))
    ]
    for load in small_loads:
        load.start()

    def block_load(j):
        columns = pl.ds(pl.multiple_of(j * BLK, BLK), BLK)
        return pltpu.make_async_copy(coef_hbm.at[:, columns], coef.at[j], local_sem.at[j])

    tile_loads = [
        pltpu.make_async_copy(at_hbm, at.at[pl.ds(0, 16)], local_sem.at[NBLK]),
        pltpu.make_async_copy(bt_hbm, bt, local_sem.at[NBLK + 1]),
    ]

    def load_block(j, _):
        block_load(j).start()
        return 0

    lax.fori_loop(0, NBLK, load_block, 0)
    for load in tile_loads:
        load.start()

    def peer(p, flip):
        dist = (Y - p) // 2
        dy = jnp.where(lax.rem(p, 2) == 1, dist, Y - dist)
        return lax.rem(y + dy, Y) * 2 + lax.rem(c + flip, 2)

    M = Y // 2
    own = Y - 1
    order = ORDERS[Y]
    up, down = lax.rem(y + 1, Y) * 2, lax.rem(y + Y - 1, Y) * 2

    barrier = pltpu.get_barrier_semaphore()

    for neighbour in (up, up + 1, down, down + 1, y * 2 + 1 - c):
        pl.semaphore_signal(barrier, 1, device_id=(me_a, neighbour), device_id_type=MESH)

    has_next, has_prev = z < Z - 1, z > 0

    @pl.when(has_next)
    def _():
        pl.semaphore_signal(barrier, 1, device_id=(me_a + 1, me_b), device_id_type=MESH)

    @pl.when(has_prev)
    def _():
        pl.semaphore_signal(barrier, 1, device_id=(me_a - 1, me_b), device_id_type=MESH)

    def greet_x(i, _):
        pl.semaphore_signal(barrier, 1, device_id=(lax.rem(x + i, X) * Z + z, me_b), device_id_type=MESH)
        return 0

    lax.fori_loop(1, X, greet_x, 0)

    for load in small_loads:
        load.wait()

    def await_block(j, _):
        block_load(j).wait()
        return 0

    lax.fori_loop(0, NBLK, await_block, 0)

    def panel_of(block, allowed):
        panel = coef[block]
        return jnp.where(allowed, panel, jnp.zeros_like(panel))

    active = mblk[0]
    mine = panel_of(active, occ[0, active] > 0)
    panels[z] = jnp.concatenate([mine[:BLK], mine[BLK:]], axis=1)

    def pack(p):
        def one(flip, _):
            d = peer(p, flip)
            code = jnp.int32(0)
            for i in range(SLOTS):
                hit = sdev[d * SLOTS + i] == me_b
                code = jnp.where(hit, code * 32 + soff[d * SLOTS + i] + 1, code)
            hi, lo = code >> 5, code & 31
            first = jnp.where(hi > 0, hi, lo)
            second = jnp.where(hi > 0, lo, 0)
            for r, named in enumerate((first, second)):
                block = jnp.clip(named - 1, 0, NBLK - 1)
                panel = panel_of(block, (named > 0) & (occ[0, block] > 0))
                place = (flip + 2 * r) if p == 0 else (4 * p + 2 * flip + r)
                for h in range(2):
                    send[h, place] = panel[h * BLK : (h + 1) * BLK]
            return 0

        lax.fori_loop(0, 2, one, 0)

    pl.semaphore_wait(barrier, 5 + X - 1 + jnp.where(has_next, 1, 0) + jnp.where(has_prev, 1, 0))

    places, count = {}, 0
    for hop in range(1, M):
        for dist in range(M, hop, -1):
            places[hop, dist] = count
            count += 2 if dist == M else 4

    L = len(order)

    def message(way, g):
        h, i = divmod(g, L)
        hop, dist = order[i]
        p = 0 if dist == M else Y - 1 - 2 * dist if way == 0 else Y - 2 * dist
        size = 2 if dist == M else 4
        first = 2 * way if dist == M else 4 * p
        chip = up if way == 0 else down

        def leg(src, at_, dst, to_at, length, core, flip):
            return pltpu.make_async_remote_copy(
                src_ref=src.at[pl.ds(at_, length)],
                dst_ref=dst.at[pl.ds(to_at, length)],
                send_sem=send_sem.at[way, g, flip],
                recv_sem=recv_sem.at[way, g, flip],
                device_id=(me_a, chip + core),
                device_id_type=MESH,
            )

        src, begin = (send.at[h], first) if hop == 1 else (passing.at[h, way], places[hop - 1, dist])
        if hop < dist:
            return [leg(src, begin, passing.at[h, way], places[hop, dist], size, c, 0)]
        half = size // 2
        return [
            leg(src, begin + half * flip, recv.at[h], first + half * flip, half, lax.rem(c + flip, 2), flip)
            for flip in range(2)
        ]

    def side_copy():
        return pltpu.make_async_remote_copy(
            src_ref=send.at[:, pl.ds(4 * own + 2, 2)],
            dst_ref=recv.at[:, pl.ds(4 * own + 2, 2)],
            send_sem=side_sem.at[0],
            recv_sem=side_sem.at[1],
            device_id=(me_a, y * 2 + 1 - c),
            device_id_type=MESH,
        )

    def advance(g):
        h, i = divmod(g, L)
        hop, dist = order[i]
        for way in range(2):
            if hop > 1:
                for copy in message(way, h * L + order.index((hop - 1, dist))):
                    copy.wait_recv()
            if g >= IN_FLIGHT:
                for copy in message(way, g - IN_FLIGHT):
                    copy.wait_send()
            for copy in message(way, g):
                copy.start()

    def expand(h, first, count):
        def two(n, _):
            start = first + 2 * n
            rows = recv[h, pl.ds(start, 2)].reshape(ROWS, BLK)

            def pair(q, _):
                result = jnp.dot(rows, wide[q], preferred_element_type=F32)
                for a in range(2):
                    for b in range(2):
                        products[start + a, 2 * q + b] = result[a * BLK : (a + 1) * BLK, b * BLK : (b + 1) * BLK]
                return 0

            lax.fori_loop(0, 8, pair, 0, unroll=4)
            return 0

        lax.fori_loop(0, count // 2, two, 0)

    def land(g):
        h, i = divmod(g, L)
        hop, dist = order[i]
        for way in range(2):
            for copy in message(way, g):
                copy.wait_recv()
        if dist == M:
            expand(h, 0, 4)
        else:
            expand(h, 4 * (Y - 1 - 2 * dist), 8)

    def panel_copy(way, s):
        origin, to = (z - s + 1, me_a + 1) if way == 0 else (z + s - 1, me_a - 1)
        origin = jnp.clip(origin, 0, Z - 1)
        return pltpu.make_async_remote_copy(
            src_ref=panels.at[origin],
            dst_ref=panels.at[origin],
            send_sem=zsend_sem.at[way, s],
            recv_sem=zrecv_sem.at[way, s],
            device_id=(to, me_b),
            device_id_type=MESH,
        )

    def panel_leaves(way, s):
        return (z - s + 1 >= 0) & has_next if way == 0 else (z + s - 1 < Z) & has_prev

    def panel_arrives(way, s):
        return z - s >= 0 if way == 0 else z + s < Z

    def start_panels(s):
        for way in range(2):

            @pl.when(panel_leaves(way, s))
            def _():
                panel_copy(way, s).start()

    def await_panels(s):
        for way in range(2):

            @pl.when(panel_arrives(way, s))
            def _():
                origin = jnp.clip(z - s if way == 0 else z + s, 0, Z - 1)
                pltpu.make_async_remote_copy(
                    src_ref=panels.at[origin],
                    dst_ref=panels.at[origin],
                    send_sem=zsend_sem.at[way, s],
                    recv_sem=zrecv_sem.at[way, s],
                    device_id=(jnp.where(has_next, me_a + 1, me_a - 1), me_b),
                    device_id_type=MESH,
                ).wait_recv()

    def sent_panels(s):
        for way in range(2):

            @pl.when(panel_leaves(way, s))
            def _():
                panel_copy(way, s).wait_send()

    def share_copy(i):
        return pltpu.make_async_remote_copy(
            src_ref=share.at[i],
            dst_ref=shares.at[i],
            send_sem=xsend_sem.at[i],
            recv_sem=xrecv_sem.at[i],
            device_id=(lax.rem(x + i, X) * Z + z, me_b),
            device_id_type=MESH,
        )

    def next_panels(s):
        if s < Z:
            await_panels(s)
        if s + 1 < Z:
            start_panels(s + 1)

    started = 0
    for p in range(Y):
        pack(p)
        if p == 0 and Z > 1:
            start_panels(1)
        if p % 2 == 0 and started < IN_FLIGHT and order[started][0] == 1:
            advance(started)
            started += 1
    side_copy().start()
    recv[:, pl.ds(4 * own, 2)] = send[:, pl.ds(4 * own, 2)]

    def placed(i, _):
        s = sdev[me_b * SLOTS + i]
        rank = jnp.int32(0)
        for other in range(SLOTS):
            same = (sdev[me_b * SLOTS + other] == s) & (other < i)
            rank = rank + jnp.where(same, 1, 0)
        dy = lax.rem(y - (s >> 1) + Y, Y)
        p = jnp.where(dy < Y // 2, Y - 1 - 2 * dy, 2 * dy - Y)
        flip = (s + c) & 1
        rank = jnp.minimum(rank, 1)
        locs[i] = jnp.where(p == 0, flip + 2 * rank, 4 * p + 2 * flip + rank)
        return 0

    lax.fori_loop(0, SLOTS, placed, 0)

    adiag[...] = jnp.broadcast_to(ad[...], (BLK, BLK)).T

    for load in tile_loads:
        load.wait()

    def negate(i, _):
        at[16 + i] = -at[i]
        return 0

    lax.fori_loop(0, 16, negate, 0)
    at[32] = jnp.zeros((BLK, BLK), BF16)

    def widen(q, _):
        wide[q] = jnp.concatenate([bt[2 * q], bt[2 * q + 1]], axis=1)
        return 0

    lax.fori_loop(0, 8, widen, 0)

    def share_of(i):
        target = lax.rem(x + i, X) * Z + z
        tiles, sources = [], []
        for e in range(EA):
            s = asrc[e, target]
            here = lax.div(s, Z) == x
            tiles.append(at[jnp.where(here, akind[e, target] + 16 * apar[e, target], 32)])
            sources.append(panels[lax.rem(s, Z)])
        return jnp.dot(
            jnp.concatenate(tiles, axis=1), jnp.concatenate(sources, axis=0), preferred_element_type=F32
        )

    def give_shares():
        for i in range(1, X):
            share[i] = share_of(i).astype(BF16)
            share_copy(i).start()

    def close_mixed():
        inner = share_of(0)
        for i in range(1, X):
            share_copy(i).wait_recv()
            inner = inner + shares[i].astype(F32)
        inner = jnp.concatenate([inner[:, :BLK], inner[:, BLK:]], axis=0)
        coarse = inner.astype(BF16)
        fine = (inner - coarse.astype(F32)).astype(BF16)
        closing = bt[mkind[0]]
        mixed[...] = jnp.dot(
            jnp.concatenate([coarse, fine], axis=1),
            jnp.concatenate([closing, closing], axis=0),
            preferred_element_type=F32,
        )

    def finish(h):
        rows = pl.ds(h * BLK, BLK)

        def block(j, _):
            columns = pl.ds(pl.multiple_of(j * BLK, BLK), BLK)
            struck = jnp.where(j == active, 1.0, 0.0).astype(F32)
            total = (adiag[...] + bd[pl.ds(j, 1), :]) * coef[j, rows, :].astype(F32) + struck * mixed[rows, :]
            for e in range(EB):
                sign = (1 - 2 * bpar[j, e]).astype(F32)
                total = total + sign * products[locs[bslot[j, e]], bkind[j, e]]
            out[rows, columns] = (total * occ[0, j].astype(F32)).astype(BF16)
            return 0

        lax.fori_loop(0, NBLK, block, 0)

    beside = {}
    step = 1
    for g in range(started, started + Z - 1):
        beside[g] = functools.partial(next_panels, step)
        step += 1
    after_z = max(L, started + Z - 1)
    beside[after_z + 3] = give_shares
    beside[after_z + 4] = close_mixed
    beside[after_z + 5] = functools.partial(finish, 0)

    waiting_to_land = [g for g in range(2 * L) if order[g % L][0] == order[g % L][1]]
    finished = False
    for g in range(started, 2 * L + IN_FLIGHT):
        if g < 2 * L:
            advance(g)
        if g == started:
            expand(0, 4 * own, 2)
        if g == started + 1:
            side_copy().wait_recv()
            expand(0, 4 * own + 2, 2)
        while waiting_to_land and waiting_to_land[0] + IN_FLIGHT <= g and (waiting_to_land[0] < L or finished):
            land(waiting_to_land.pop(0))
        if g in beside:
            beside.pop(g)()
            if g == after_z + 5:
                finished = True
                expand(1, 4 * own, 4)
    while beside:
        g = min(beside)
        beside.pop(g)()
        if g == after_z + 5:
            expand(1, 4 * own, 4)
    for g in waiting_to_land:
        land(g)
    finish(1)

    side_copy().wait_send()
    for g in range(2 * L - IN_FLIGHT, 2 * L):
        for way in range(2):
            for copy in message(way, g):
                copy.wait_send()

    def left_panels(s, _):
        sent_panels(s)
        return 0

    lax.fori_loop(1, Z, left_panels, 0)
    for i in range(1, X):
        share_copy(i).wait_send()


def solution(mesh):
    n_alpha, n_beta = mesh.shape["alpha"], mesh.shape["beta"]
    Z = 8 if n_alpha == 32 else 1
    X, Y = n_alpha // Z, n_beta // 2
    waiting = sum(2 if 2 * dist == Y else 4 for hop, dist in ORDERS[Y] if hop < dist)

    def local(
        coef,
        alpha_diag,
        beta_diag,
        alpha_tiles,
        beta_tiles,
        occupancy,
        alpha_source,
        alpha_kind,
        alpha_parity,
        slot_device,
        slot_offset,
        beta_slot,
        beta_kind,
        beta_parity,
        mixed_block,
        mixed_kind,
    ):
        vmem = pl.BlockSpec(memory_space=pltpu.VMEM)
        hbm = pl.BlockSpec(memory_space=pl.ANY)
        columns = coef.shape[-1]
        small = (
            occupancy,
            alpha_source.T,
            alpha_kind.T,
            alpha_parity.T,
            slot_device.reshape(-1),
            slot_offset,
            beta_slot,
            beta_kind,
            beta_parity,
            mixed_block,
            mixed_kind,
            alpha_diag.reshape(1, BLK),
            beta_diag.reshape(NBLK, BLK),
        )
        result = pl.pallas_call(
            functools.partial(kernel, X, Z, Y),
            out_shape=jax.ShapeDtypeStruct((ROWS, columns), BF16),
            in_specs=[hbm] * (len(small) + 3),
            out_specs=vmem,
            scratch_shapes=[
                *(pltpu.SMEM(v.shape, v.dtype) for v in small[:11]),
                *(pltpu.VMEM(v.shape, v.dtype) for v in small[11:]),
                pltpu.VMEM((NBLK, ROWS, BLK), BF16),
                pltpu.VMEM((33, BLK, BLK), BF16),
                pltpu.VMEM((16, BLK, BLK), BF16),
                pltpu.VMEM((Z, BLK, ROWS), BF16),
                pltpu.VMEM((X, BLK, ROWS), BF16),
                pltpu.VMEM((X, BLK, ROWS), BF16),
                pltpu.VMEM((BLK, BLK), F32),
                pltpu.VMEM((ROWS, BLK), F32),
                pltpu.SMEM((SLOTS,), jnp.int32),
                pltpu.VMEM((2, 2 * n_beta, BLK, BLK), BF16),
                pltpu.VMEM((2, 2 * n_beta, BLK, BLK), BF16),
                pltpu.VMEM((2, 2, waiting, BLK, BLK), BF16),
                pltpu.VMEM((8, BLK, 2 * BLK), BF16),
                pltpu.VMEM((2 * n_beta, 16, BLK, BLK), F32),
                pltpu.SemaphoreType.DMA((len(small),)),
                pltpu.SemaphoreType.DMA((NBLK + 2,)),
                pltpu.SemaphoreType.DMA((2, 2 * len(ORDERS[Y]), 2)),
                pltpu.SemaphoreType.DMA((2, 2 * len(ORDERS[Y]), 2)),
                pltpu.SemaphoreType.DMA((2,)),
                pltpu.SemaphoreType.DMA((2, Z)),
                pltpu.SemaphoreType.DMA((2, Z)),
                pltpu.SemaphoreType.DMA((X,)),
                pltpu.SemaphoreType.DMA((X,)),
            ],
            compiler_params=pltpu.CompilerParams(
                collective_id=0, has_side_effects=True, vmem_limit_bytes=60 * 1024 * 1024
            ),
            cost_estimate=pl.CostEstimate(flops=2200000000, bytes_accessed=3300000, transcendentals=0),
        )(
            *small,
            coef.reshape(ROWS, columns),
            alpha_tiles,
            beta_tiles,
        )
        return result.reshape(coef.shape)

    in_specs = (
        P(None, "alpha", "beta"),
        P("alpha"),
        P("beta"),
        P(),
        P(),
        P("alpha", "beta"),
        P(),
        P(),
        P(),
        P(),
        P(),
        P("beta", None),
        P("beta", None),
        P("beta", None),
        P("beta"),
        P("beta"),
    )
    out_specs = P(None, "alpha", "beta")
    return jax.shard_map(local, mesh=mesh, in_specs=in_specs, out_specs=out_specs, check_vma=False)
```

```python
import functools

import jax
import jax.numpy as jnp
from jax import lax
from jax.experimental import pallas as pl
from jax.experimental.pallas import tpu as pltpu
from jax.sharding import PartitionSpec as P

MESH = pl.DeviceIdType.MESH
BLK = 128
NBLK = 16
SLOTS = 16
EB = 16
EA = 4
ROWS = 2 * BLK
ORDERS = {
    4: ((1, 2), (1, 1), (2, 2)),
    8: ((1, 4), (1, 3), (1, 2), (2, 4), (2, 3), (1, 1), (3, 4), (2, 2), (3, 3), (4, 4)),
}
IN_FLIGHT = 3
F32 = jnp.float32
BF16 = jnp.bfloat16


def kernel(X, Z, Y, *refs):
    small_hbm, (coef_hbm, at_hbm, bt_hbm, out), small = refs[:13], refs[13:17], refs[17:30]
    occ, asrc, akind, apar, sdev, soff, bslot, bkind, bpar, mblk, mkind, ad, bd = small
    coef, at, bt, panels, share, shares, adiag, mixed, locs, send, recv, passing, wide, products, stash = refs[30:45]
    (
        small_sem,
        local_sem,
        send_sem,
        recv_sem,
        side_sem,
        zsend_sem,
        zrecv_sem,
        xsend_sem,
        xrecv_sem,
    ) = refs[45:]
    NB = 2 * Y
    me_a = lax.axis_index("alpha")
    me_b = lax.axis_index("beta")
    x, z = me_a // Z, lax.rem(me_a, Z)
    y, c = me_b // 2, lax.rem(me_b, 2)

    small_loads = [
        pltpu.make_async_copy(src, dst, small_sem.at[i]) for i, (src, dst) in enumerate(zip(small_hbm, small))
    ]
    for load in small_loads:
        load.start()

    def block_load(j):
        columns = pl.ds(pl.multiple_of(j * BLK, BLK), BLK)
        return pltpu.make_async_copy(coef_hbm.at[:, columns], coef.at[j], local_sem.at[j])

    tile_loads = [
        pltpu.make_async_copy(at_hbm, at.at[pl.ds(0, 16)], local_sem.at[NBLK]),
        pltpu.make_async_copy(bt_hbm, bt, local_sem.at[NBLK + 1]),
    ]

    def load_block(j, _):
        block_load(j).start()
        return 0

    lax.fori_loop(0, NBLK, load_block, 0)
    for load in tile_loads:
        load.start()

    def peer(p, flip):
        dist = (Y - p) // 2
        dy = jnp.where(lax.rem(p, 2) == 1, dist, Y - dist)
        return lax.rem(y + dy, Y) * 2 + lax.rem(c + flip, 2)

    M = Y // 2
    own = Y - 1
    order = ORDERS[Y]
    up, down = lax.rem(y + 1, Y) * 2, lax.rem(y + Y - 1, Y) * 2

    barrier = pltpu.get_barrier_semaphore()

    for neighbour in (up, up + 1, down, down + 1, y * 2 + 1 - c):
        pl.semaphore_signal(barrier, 1, device_id=(me_a, neighbour), device_id_type=MESH)

    has_next, has_prev = z < Z - 1, z > 0

    @pl.when(has_next)
    def _():
        pl.semaphore_signal(barrier, 1, device_id=(me_a + 1, me_b), device_id_type=MESH)

    @pl.when(has_prev)
    def _():
        pl.semaphore_signal(barrier, 1, device_id=(me_a - 1, me_b), device_id_type=MESH)

    def greet_x(i, _):
        pl.semaphore_signal(barrier, 1, device_id=(lax.rem(x + i, X) * Z + z, me_b), device_id_type=MESH)
        return 0

    lax.fori_loop(1, X, greet_x, 0)

    for load in small_loads:
        load.wait()

    def await_block(j, _):
        block_load(j).wait()
        return 0

    lax.fori_loop(0, NBLK, await_block, 0)

    def panel_of(block, allowed):
        panel = coef[block]
        return jnp.where(allowed, panel, jnp.zeros_like(panel))

    active = mblk[0]
    mine = panel_of(active, occ[0, active] > 0)
    panels[z] = jnp.concatenate([mine[:BLK], mine[BLK:]], axis=1)

    def pack(p):
        def one(flip, _):
            d = peer(p, flip)
            code = jnp.int32(0)
            for i in range(SLOTS):
                hit = sdev[d * SLOTS + i] == me_b
                code = jnp.where(hit, code * 32 + soff[d * SLOTS + i] + 1, code)
            hi, lo = code >> 5, code & 31
            first = jnp.where(hi > 0, hi, lo)
            second = jnp.where(hi > 0, lo, 0)
            for r, named in enumerate((first, second)):
                block = jnp.clip(named - 1, 0, NBLK - 1)
                panel = panel_of(block, (named > 0) & (occ[0, block] > 0))
                place = (flip + 2 * r) if p == 0 else (4 * p + 2 * flip + r)
                for h in range(2):
                    send[h, place] = panel[h * BLK : (h + 1) * BLK]
            return 0

        lax.fori_loop(0, 2, one, 0)

    pl.semaphore_wait(barrier, 5 + X - 1 + jnp.where(has_next, 1, 0) + jnp.where(has_prev, 1, 0))

    places, count = {}, 0
    for hop in range(1, M):
        for dist in range(M, hop, -1):
            places[hop, dist] = count
            count += 2 if dist == M else 4

    L = len(order)

    def message(way, g):
        h, i = divmod(g, L)
        hop, dist = order[i]
        p = 0 if dist == M else Y - 1 - 2 * dist if way == 0 else Y - 2 * dist
        size = 2 if dist == M else 4
        first = 2 * way if dist == M else 4 * p
        chip = up if way == 0 else down

        def leg(src, at_, dst, to_at, length, core, flip):
            return pltpu.make_async_remote_copy(
                src_ref=src.at[pl.ds(at_, length)],
                dst_ref=dst.at[pl.ds(to_at, length)],
                send_sem=send_sem.at[way, g, flip],
                recv_sem=recv_sem.at[way, g, flip],
                device_id=(me_a, chip + core),
                device_id_type=MESH,
            )

        src, begin = (send.at[h], first) if hop == 1 else (passing.at[h, way], places[hop - 1, dist])
        if hop < dist:
            return [leg(src, begin, passing.at[h, way], places[hop, dist], size, c, 0)]
        half = size // 2
        return [
            leg(src, begin + half * flip, recv.at[h], first + half * flip, half, lax.rem(c + flip, 2), flip)
            for flip in range(2)
        ]

    def side_copy():
        return pltpu.make_async_remote_copy(
            src_ref=send.at[:, pl.ds(4 * own + 2, 2)],
            dst_ref=recv.at[:, pl.ds(4 * own + 2, 2)],
            send_sem=side_sem.at[0],
            recv_sem=side_sem.at[1],
            device_id=(me_a, y * 2 + 1 - c),
            device_id_type=MESH,
        )

    def advance(g):
        h, i = divmod(g, L)
        hop, dist = order[i]
        for way in range(2):
            if hop > 1:
                for copy in message(way, h * L + order.index((hop - 1, dist))):
                    copy.wait_recv()
            if g >= IN_FLIGHT:
                for copy in message(way, g - IN_FLIGHT):
                    copy.wait_send()
            for copy in message(way, g):
                copy.start()

    def expand(h, first, count):
        def two(n, _):
            start = first + 2 * n
            rows = recv[h, pl.ds(start, 2)].reshape(ROWS, BLK)

            def pair(q, _):
                result = jnp.dot(rows, wide[q], preferred_element_type=F32)
                for a in range(2):
                    for b in range(2):
                        products[start + a, 2 * q + b] = result[a * BLK : (a + 1) * BLK, b * BLK : (b + 1) * BLK]
                return 0

            lax.fori_loop(0, 8, pair, 0, unroll=4)
            return 0

        lax.fori_loop(0, count // 2, two, 0)

    def land(g):
        h, i = divmod(g, L)
        hop, dist = order[i]
        for way in range(2):
            for copy in message(way, g):
                copy.wait_recv()
        if dist == M:
            expand(h, 0, 4)
        else:
            expand(h, 4 * (Y - 1 - 2 * dist), 8)

    def panel_copy(way, s):
        origin, to = (z - s + 1, me_a + 1) if way == 0 else (z + s - 1, me_a - 1)
        origin = jnp.clip(origin, 0, Z - 1)
        return pltpu.make_async_remote_copy(
            src_ref=panels.at[origin],
            dst_ref=panels.at[origin],
            send_sem=zsend_sem.at[way, s],
            recv_sem=zrecv_sem.at[way, s],
            device_id=(to, me_b),
            device_id_type=MESH,
        )

    def panel_leaves(way, s):
        return (z - s + 1 >= 0) & has_next if way == 0 else (z + s - 1 < Z) & has_prev

    def panel_arrives(way, s):
        return z - s >= 0 if way == 0 else z + s < Z

    def start_panels(s):
        for way in range(2):

            @pl.when(panel_leaves(way, s))
            def _():
                panel_copy(way, s).start()

    def await_panels(s):
        for way in range(2):

            @pl.when(panel_arrives(way, s))
            def _():
                origin = jnp.clip(z - s if way == 0 else z + s, 0, Z - 1)
                pltpu.make_async_remote_copy(
                    src_ref=panels.at[origin],
                    dst_ref=panels.at[origin],
                    send_sem=zsend_sem.at[way, s],
                    recv_sem=zrecv_sem.at[way, s],
                    device_id=(jnp.where(has_next, me_a + 1, me_a - 1), me_b),
                    device_id_type=MESH,
                ).wait_recv()

    def sent_panels(s):
        for way in range(2):

            @pl.when(panel_leaves(way, s))
            def _():
                panel_copy(way, s).wait_send()

    def share_copy(i):
        return pltpu.make_async_remote_copy(
            src_ref=share.at[i],
            dst_ref=shares.at[i],
            send_sem=xsend_sem.at[i],
            recv_sem=xrecv_sem.at[i],
            device_id=(lax.rem(x + i, X) * Z + z, me_b),
            device_id_type=MESH,
        )

    def next_panels(s):
        if s < Z:
            await_panels(s)
        if s + 1 < Z:
            start_panels(s + 1)

    started = 0
    for p in range(Y):
        pack(p)
        if p == 0 and Z > 1:
            start_panels(1)
        if p % 2 == 0 and started < IN_FLIGHT and order[started][0] == 1:
            advance(started)
            started += 1
    side_copy().start()
    recv[:, pl.ds(4 * own, 2)] = send[:, pl.ds(4 * own, 2)]

    def placed(i, _):
        s = sdev[me_b * SLOTS + i]
        rank = jnp.int32(0)
        for other in range(SLOTS):
            same = (sdev[me_b * SLOTS + other] == s) & (other < i)
            rank = rank + jnp.where(same, 1, 0)
        dy = lax.rem(y - (s >> 1) + Y, Y)
        p = jnp.where(dy < Y // 2, Y - 1 - 2 * dy, 2 * dy - Y)
        flip = (s + c) & 1
        rank = jnp.minimum(rank, 1)
        locs[i] = jnp.where(p == 0, flip + 2 * rank, 4 * p + 2 * flip + rank)
        return 0

    lax.fori_loop(0, SLOTS, placed, 0)

    adiag[...] = jnp.broadcast_to(ad[...], (BLK, BLK)).T

    for load in tile_loads:
        load.wait()

    def negate(i, _):
        at[16 + i] = -at[i]
        return 0

    lax.fori_loop(0, 16, negate, 0)
    at[32] = jnp.zeros((BLK, BLK), BF16)

    def widen(q, _):
        wide[q] = jnp.concatenate([bt[2 * q], bt[2 * q + 1]], axis=1)
        return 0

    lax.fori_loop(0, 8, widen, 0)

    def share_of(i):
        target = lax.rem(x + i, X) * Z + z
        tiles, sources = [], []
        for e in range(EA):
            s = asrc[e, target]
            here = lax.div(s, Z) == x
            tiles.append(at[jnp.where(here, akind[e, target] + 16 * apar[e, target], 32)])
            sources.append(panels[lax.rem(s, Z)])
        return jnp.dot(
            jnp.concatenate(tiles, axis=1), jnp.concatenate(sources, axis=0), preferred_element_type=F32
        )

    def give_shares():
        for i in range(1, X):
            share[i] = share_of(i).astype(BF16)
            share_copy(i).start()

    def close_mixed():
        inner = share_of(0)
        for i in range(1, X):
            share_copy(i).wait_recv()
            inner = inner + shares[i].astype(F32)
        inner = jnp.concatenate([inner[:, :BLK], inner[:, BLK:]], axis=0)
        coarse = inner.astype(BF16)
        fine = (inner - coarse.astype(F32)).astype(BF16)
        closing = bt[mkind[0]]
        mixed[...] = jnp.dot(
            jnp.concatenate([coarse, fine], axis=1),
            jnp.concatenate([closing, closing], axis=0),
            preferred_element_type=F32,
        )

    def finish(h):
        rows = pl.ds(h * BLK, BLK)

        def block(j, _):
            columns = pl.ds(pl.multiple_of(j * BLK, BLK), BLK)
            struck = jnp.where(j == active, 1.0, 0.0).astype(F32)
            total = (adiag[...] + bd[pl.ds(j, 1), :]) * coef[j, rows, :].astype(F32)
            if h == 1:
                total = total + struck * mixed[rows, :]
            for e in range(EB):
                sign = (1 - 2 * bpar[j, e]).astype(F32)
                total = total + sign * products[locs[bslot[j, e]], bkind[j, e]]
            if h == 0:
                stash[...] = stash[...] + struck * total
            out[rows, columns] = (total * occ[0, j].astype(F32)).astype(BF16)
            return 0

        lax.fori_loop(0, NBLK, block, 0)

    def amend():
        rows = pl.ds(0, BLK)
        whole = ((stash[...] + mixed[rows, :]) * occ[0, active].astype(F32)).astype(BF16)

        def block(j, _):
            columns = pl.ds(pl.multiple_of(j * BLK, BLK), BLK)
            out[rows, columns] = jnp.where(j == active, whole, out[rows, columns])
            return 0

        lax.fori_loop(0, NBLK, block, 0)

    def first_plane():
        stash[...] = jnp.zeros((BLK, BLK), F32)
        finish(0)
        expand(1, 4 * own, 4)

    beside = []
    for n, (hop, dist) in enumerate(order):
        if hop == dist:
            beside.append((n + IN_FLIGHT, functools.partial(land, n)))
            beside.append((L + n + IN_FLIGHT, functools.partial(land, L + n)))
    beside.append((started, functools.partial(expand, 0, 4 * own, 2)))

    def beside_core():
        side_copy().wait_recv()
        expand(0, 4 * own + 2, 2)

    beside.append((started + 1, beside_core))
    beside.append((L + IN_FLIGHT - 1, first_plane))
    for s in range(1, Z):
        beside.append((started + 2 * (s - 1), functools.partial(next_panels, s)))
    late = 2 * L - 2
    beside.append((late - 2, give_shares))
    beside.append((late, close_mixed))
    beside.append((late + 1, amend))
    beside.sort(key=lambda entry: entry[0])
    for g in range(started, 2 * L):
        advance(g)
        while beside and beside[0][0] <= g:
            beside.pop(0)[1]()
    for _, work in beside:
        work()
    finish(1)

    side_copy().wait_send()
    for g in range(2 * L - IN_FLIGHT, 2 * L):
        for way in range(2):
            for copy in message(way, g):
                copy.wait_send()

    def left_panels(s, _):
        sent_panels(s)
        return 0

    lax.fori_loop(1, Z, left_panels, 0)
    for i in range(1, X):
        share_copy(i).wait_send()


def solution(mesh):
    n_alpha, n_beta = mesh.shape["alpha"], mesh.shape["beta"]
    Z = 8 if n_alpha == 32 else 1
    X, Y = n_alpha // Z, n_beta // 2
    waiting = sum(2 if 2 * dist == Y else 4 for hop, dist in ORDERS[Y] if hop < dist)

    def local(
        coef,
        alpha_diag,
        beta_diag,
        alpha_tiles,
        beta_tiles,
        occupancy,
        alpha_source,
        alpha_kind,
        alpha_parity,
        slot_device,
        slot_offset,
        beta_slot,
        beta_kind,
        beta_parity,
        mixed_block,
        mixed_kind,
    ):
        vmem = pl.BlockSpec(memory_space=pltpu.VMEM)
        hbm = pl.BlockSpec(memory_space=pl.ANY)
        columns = coef.shape[-1]
        small = (
            occupancy,
            alpha_source.T,
            alpha_kind.T,
            alpha_parity.T,
            slot_device.reshape(-1),
            slot_offset,
            beta_slot,
            beta_kind,
            beta_parity,
            mixed_block,
            mixed_kind,
            alpha_diag.reshape(1, BLK),
            beta_diag.reshape(NBLK, BLK),
        )
        result = pl.pallas_call(
            functools.partial(kernel, X, Z, Y),
            out_shape=jax.ShapeDtypeStruct((ROWS, columns), BF16),
            in_specs=[hbm] * (len(small) + 3),
            out_specs=vmem,
            scratch_shapes=[
                *(pltpu.SMEM(v.shape, v.dtype) for v in small[:11]),
                *(pltpu.VMEM(v.shape, v.dtype) for v in small[11:]),
                pltpu.VMEM((NBLK, ROWS, BLK), BF16),
                pltpu.VMEM((33, BLK, BLK), BF16),
                pltpu.VMEM((16, BLK, BLK), BF16),
                pltpu.VMEM((Z, BLK, ROWS), BF16),
                pltpu.VMEM((X, BLK, ROWS), BF16),
                pltpu.VMEM((X, BLK, ROWS), BF16),
                pltpu.VMEM((BLK, BLK), F32),
                pltpu.VMEM((ROWS, BLK), F32),
                pltpu.SMEM((SLOTS,), jnp.int32),
                pltpu.VMEM((2, 2 * n_beta, BLK, BLK), BF16),
                pltpu.VMEM((2, 2 * n_beta, BLK, BLK), BF16),
                pltpu.VMEM((2, 2, waiting, BLK, BLK), BF16),
                pltpu.VMEM((8, BLK, 2 * BLK), BF16),
                pltpu.VMEM((2 * n_beta, 16, BLK, BLK), F32),
                pltpu.VMEM((BLK, BLK), F32),
                pltpu.SemaphoreType.DMA((len(small),)),
                pltpu.SemaphoreType.DMA((NBLK + 2,)),
                pltpu.SemaphoreType.DMA((2, 2 * len(ORDERS[Y]), 2)),
                pltpu.SemaphoreType.DMA((2, 2 * len(ORDERS[Y]), 2)),
                pltpu.SemaphoreType.DMA((2,)),
                pltpu.SemaphoreType.DMA((2, Z)),
                pltpu.SemaphoreType.DMA((2, Z)),
                pltpu.SemaphoreType.DMA((X,)),
                pltpu.SemaphoreType.DMA((X,)),
            ],
            compiler_params=pltpu.CompilerParams(
                collective_id=0, has_side_effects=True, vmem_limit_bytes=60 * 1024 * 1024
            ),
            cost_estimate=pl.CostEstimate(flops=2200000000, bytes_accessed=3300000, transcendentals=0),
        )(
            *small,
            coef.reshape(ROWS, columns),
            alpha_tiles,
            beta_tiles,
        )
        return result.reshape(coef.shape)

    in_specs = (
        P(None, "alpha", "beta"),
        P("alpha"),
        P("beta"),
        P(),
        P(),
        P("alpha", "beta"),
        P(),
        P(),
        P(),
        P(),
        P(),
        P("beta", None),
        P("beta", None),
        P("beta", None),
        P("beta"),
        P("beta"),
    )
    out_specs = P(None, "alpha", "beta")
    return jax.shard_map(local, mesh=mesh, in_specs=in_specs, out_specs=out_specs, check_vma=False)
```

```python
import functools

import jax
import jax.numpy as jnp
from jax import lax
from jax.experimental import pallas as pl
from jax.experimental.pallas import tpu as pltpu
from jax.sharding import PartitionSpec as P

MESH = pl.DeviceIdType.MESH
BLK = 128
NBLK = 16
SLOTS = 16
EB = 16
EA = 4
ROWS = 2 * BLK
ORDERS = {
    4: ((1, 2), (1, 1), (2, 2)),
    8: ((1, 4), (1, 3), (1, 2), (2, 4), (2, 3), (1, 1), (3, 4), (2, 2), (3, 3), (4, 4)),
}
IN_FLIGHT = 3
F32 = jnp.float32
BF16 = jnp.bfloat16


def kernel(X, Z, Y, *refs):
    small_hbm, (coef_hbm, at_hbm, bt_hbm, out_hbm), small = refs[:13], refs[13:17], refs[17:30]
    occ, sdev, soff, mblk, mkind, asrc, akind, apar, bslot, bkind, bpar, ad, bd = small
    coef, at, bt, panels, share, shares, adiag, mixed, locs, send, recv, passing, wide, products, stash, out = refs[30:46]
    (
        small_sem,
        out_sem,
        local_sem,
        send_sem,
        recv_sem,
        side_sem,
        zsend_sem,
        zrecv_sem,
        xsend_sem,
        xrecv_sem,
    ) = refs[46:]
    NB = 2 * Y
    me_a = lax.axis_index("alpha")
    me_b = lax.axis_index("beta")
    x, z = me_a // Z, lax.rem(me_a, Z)
    y, c = me_b // 2, lax.rem(me_b, 2)

    def peer(p, flip):
        dist = (Y - p) // 2
        dy = jnp.where(lax.rem(p, 2) == 1, dist, Y - dist)
        return lax.rem(y + dy, Y) * 2 + lax.rem(c + flip, 2)

    M = Y // 2
    own = Y - 1
    order = ORDERS[Y]
    up, down = lax.rem(y + 1, Y) * 2, lax.rem(y + Y - 1, Y) * 2

    barrier = pltpu.get_barrier_semaphore()

    for neighbour in (up, up + 1, down, down + 1, y * 2 + 1 - c):
        pl.semaphore_signal(barrier, 1, device_id=(me_a, neighbour), device_id_type=MESH)

    has_next, has_prev = z < Z - 1, z > 0

    @pl.when(has_next)
    def _():
        pl.semaphore_signal(barrier, 1, device_id=(me_a + 1, me_b), device_id_type=MESH)

    @pl.when(has_prev)
    def _():
        pl.semaphore_signal(barrier, 1, device_id=(me_a - 1, me_b), device_id_type=MESH)

    def greet_x(i, _):
        pl.semaphore_signal(barrier, 1, device_id=(lax.rem(x + i, X) * Z + z, me_b), device_id_type=MESH)
        return 0

    lax.fori_loop(1, X, greet_x, 0)

    small_loads = [
        pltpu.make_async_copy(src, dst, small_sem.at[i]) for i, (src, dst) in enumerate(zip(small_hbm, small))
    ]
    for load in small_loads[:4]:
        load.start()

    def block_load(j):
        columns = pl.ds(pl.multiple_of(j * BLK, BLK), BLK)
        return pltpu.make_async_copy(coef_hbm.at[:, columns], coef.at[j], local_sem.at[j])

    tile_loads = [
        pltpu.make_async_copy(at_hbm, at.at[pl.ds(0, 16)], local_sem.at[NBLK]),
        pltpu.make_async_copy(bt_hbm, bt, local_sem.at[NBLK + 1]),
    ]

    def load_block(j, _):
        block_load(j).start()
        return 0

    lax.fori_loop(0, NBLK, load_block, 0)
    for load in small_loads[4:] + tile_loads:
        load.start()
    for load in small_loads[:4]:
        load.wait()

    def await_block(j, _):
        block_load(j).wait()
        return 0

    lax.fori_loop(0, NBLK, await_block, 0)

    def panel_of(block, allowed):
        panel = coef[block]
        return jnp.where(allowed, panel, jnp.zeros_like(panel))

    active = mblk[0]
    mine = panel_of(active, occ[0, active] > 0)
    panels[z] = jnp.concatenate([mine[:BLK], mine[BLK:]], axis=1)

    def pack(p):
        def one(flip, _):
            d = peer(p, flip)
            code = jnp.int32(0)
            for i in range(SLOTS):
                hit = sdev[d * SLOTS + i] == me_b
                code = jnp.where(hit, code * 32 + soff[d * SLOTS + i] + 1, code)
            hi, lo = code >> 5, code & 31
            first = jnp.where(hi > 0, hi, lo)
            second = jnp.where(hi > 0, lo, 0)
            for r, named in enumerate((first, second)):
                block = jnp.clip(named - 1, 0, NBLK - 1)
                panel = panel_of(block, (named > 0) & (occ[0, block] > 0))
                place = (flip + 2 * r) if p == 0 else (4 * p + 2 * flip + r)
                for h in range(2):
                    send[h, place] = panel[h * BLK : (h + 1) * BLK]
            return 0

        lax.fori_loop(0, 2, one, 0)

    pack(0)
    pl.semaphore_wait(barrier, 5 + X - 1 + jnp.where(has_next, 1, 0) + jnp.where(has_prev, 1, 0))

    places, count = {}, 0
    for hop in range(1, M):
        for dist in range(M, hop, -1):
            places[hop, dist] = count
            count += 2 if dist == M else 4

    L = len(order)

    def message(way, g):
        h, i = divmod(g, L)
        hop, dist = order[i]
        p = 0 if dist == M else Y - 1 - 2 * dist if way == 0 else Y - 2 * dist
        size = 2 if dist == M else 4
        first = 2 * way if dist == M else 4 * p
        chip = up if way == 0 else down

        def leg(src, at_, dst, to_at, length, core, flip):
            return pltpu.make_async_remote_copy(
                src_ref=src.at[pl.ds(at_, length)],
                dst_ref=dst.at[pl.ds(to_at, length)],
                send_sem=send_sem.at[way, g, flip],
                recv_sem=recv_sem.at[way, g, flip],
                device_id=(me_a, chip + core),
                device_id_type=MESH,
            )

        src, begin = (send.at[h], first) if hop == 1 else (passing.at[h, way], places[hop - 1, dist])
        if hop < dist:
            return [leg(src, begin, passing.at[h, way], places[hop, dist], size, c, 0)]
        half = size // 2
        return [
            leg(src, begin + half * flip, recv.at[h], first + half * flip, half, lax.rem(c + flip, 2), flip)
            for flip in range(2)
        ]

    def side_copy():
        return pltpu.make_async_remote_copy(
            src_ref=send.at[:, pl.ds(4 * own + 2, 2)],
            dst_ref=recv.at[:, pl.ds(4 * own + 2, 2)],
            send_sem=side_sem.at[0],
            recv_sem=side_sem.at[1],
            device_id=(me_a, y * 2 + 1 - c),
            device_id_type=MESH,
        )

    def advance(g):
        h, i = divmod(g, L)
        hop, dist = order[i]
        for way in range(2):
            if hop > 1:
                for copy in message(way, h * L + order.index((hop - 1, dist))):
                    copy.wait_recv()
            if g >= IN_FLIGHT:
                for copy in message(way, g - IN_FLIGHT):
                    copy.wait_send()
            for copy in message(way, g):
                copy.start()

    def expand(h, first, count):
        def two(n, _):
            start = first + 2 * n
            rows = recv[h, pl.ds(start, 2)].reshape(ROWS, BLK)

            def pair(q, _):
                result = jnp.dot(rows, wide[q], preferred_element_type=F32)
                for a in range(2):
                    for b in range(2):
                        products[start + a, 2 * q + b] = result[a * BLK : (a + 1) * BLK, b * BLK : (b + 1) * BLK]
                return 0

            lax.fori_loop(0, 8, pair, 0, unroll=4)
            return 0

        lax.fori_loop(0, count // 2, two, 0)

    def land(g):
        h, i = divmod(g, L)
        hop, dist = order[i]
        for way in range(2):
            for copy in message(way, g):
                copy.wait_recv()
        if dist == M:
            expand(h, 0, 4)
        else:
            expand(h, 4 * (Y - 1 - 2 * dist), 8)

    def panel_copy(way, s):
        origin, to = (z - s + 1, me_a + 1) if way == 0 else (z + s - 1, me_a - 1)
        origin = jnp.clip(origin, 0, Z - 1)
        return pltpu.make_async_remote_copy(
            src_ref=panels.at[origin],
            dst_ref=panels.at[origin],
            send_sem=zsend_sem.at[way, s],
            recv_sem=zrecv_sem.at[way, s],
            device_id=(to, me_b),
            device_id_type=MESH,
        )

    def panel_leaves(way, s):
        return (z - s + 1 >= 0) & has_next if way == 0 else (z + s - 1 < Z) & has_prev

    def panel_arrives(way, s):
        return z - s >= 0 if way == 0 else z + s < Z

    def start_panels(s):
        for way in range(2):

            @pl.when(panel_leaves(way, s))
            def _():
                panel_copy(way, s).start()

    def await_panels(s):
        for way in range(2):

            @pl.when(panel_arrives(way, s))
            def _():
                origin = jnp.clip(z - s if way == 0 else z + s, 0, Z - 1)
                pltpu.make_async_remote_copy(
                    src_ref=panels.at[origin],
                    dst_ref=panels.at[origin],
                    send_sem=zsend_sem.at[way, s],
                    recv_sem=zrecv_sem.at[way, s],
                    device_id=(jnp.where(has_next, me_a + 1, me_a - 1), me_b),
                    device_id_type=MESH,
                ).wait_recv()

    def sent_panels(s):
        for way in range(2):

            @pl.when(panel_leaves(way, s))
            def _():
                panel_copy(way, s).wait_send()

    def share_copy(i):
        return pltpu.make_async_remote_copy(
            src_ref=share.at[i],
            dst_ref=shares.at[i],
            send_sem=xsend_sem.at[i],
            recv_sem=xrecv_sem.at[i],
            device_id=(lax.rem(x + i, X) * Z + z, me_b),
            device_id_type=MESH,
        )

    def next_panels(s):
        if s < Z:
            await_panels(s)
        if s + 1 < Z:
            start_panels(s + 1)

    started = 0
    for p in range(Y):
        if p > 0:
            pack(p)
        if p == 0 and Z > 1:
            start_panels(1)
        if p % 2 == 0 and started < IN_FLIGHT and order[started][0] == 1:
            advance(started)
            started += 1
    side_copy().start()
    recv[:, pl.ds(4 * own, 2)] = send[:, pl.ds(4 * own, 2)]

    for load in small_loads[4:]:
        load.wait()

    def placed(i, _):
        s = sdev[me_b * SLOTS + i]
        rank = jnp.int32(0)
        for other in range(SLOTS):
            same = (sdev[me_b * SLOTS + other] == s) & (other < i)
            rank = rank + jnp.where(same, 1, 0)
        dy = lax.rem(y - (s >> 1) + Y, Y)
        p = jnp.where(dy < Y // 2, Y - 1 - 2 * dy, 2 * dy - Y)
        flip = (s + c) & 1
        rank = jnp.minimum(rank, 1)
        locs[i] = jnp.where(p == 0, flip + 2 * rank, 4 * p + 2 * flip + rank)
        return 0

    lax.fori_loop(0, SLOTS, placed, 0)

    adiag[...] = jnp.broadcast_to(ad[...], (BLK, BLK)).T

    for load in tile_loads:
        load.wait()

    def negate(i, _):
        at[16 + i] = -at[i]
        return 0

    lax.fori_loop(0, 16, negate, 0)
    at[32] = jnp.zeros((BLK, BLK), BF16)

    def widen(q, _):
        wide[q] = jnp.concatenate([bt[2 * q], bt[2 * q + 1]], axis=1)
        return 0

    lax.fori_loop(0, 8, widen, 0)

    def share_of(i):
        target = lax.rem(x + i, X) * Z + z
        tiles, sources = [], []
        for e in range(EA):
            s = asrc[e, target]
            here = lax.div(s, Z) == x
            tiles.append(at[jnp.where(here, akind[e, target] + 16 * apar[e, target], 32)])
            sources.append(panels[lax.rem(s, Z)])
        return jnp.dot(
            jnp.concatenate(tiles, axis=1), jnp.concatenate(sources, axis=0), preferred_element_type=F32
        )

    def give_shares():
        for i in range(1, X):
            share[i] = share_of(i).astype(BF16)
            share_copy(i).start()

    def close_mixed():
        inner = share_of(0)
        for i in range(1, X):
            share_copy(i).wait_recv()
            inner = inner + shares[i].astype(F32)
        inner = jnp.concatenate([inner[:, :BLK], inner[:, BLK:]], axis=0)
        coarse = inner.astype(BF16)
        fine = (inner - coarse.astype(F32)).astype(BF16)
        closing = bt[mkind[0]]
        mixed[...] = jnp.dot(
            jnp.concatenate([coarse, fine], axis=1),
            jnp.concatenate([closing, closing], axis=0),
            preferred_element_type=F32,
        )

    QUARTER = NBLK // 4

    def written(h, part):
        view = (pl.ds(h * BLK, BLK), pl.ds(part * QUARTER * BLK, QUARTER * BLK))
        return pltpu.make_async_copy(out.at[view], out_hbm.at[view], out_sem.at[h, part])

    def finish(h):
        rows = pl.ds(h * BLK, BLK)

        def block(j, _):
            columns = pl.ds(pl.multiple_of(j * BLK, BLK), BLK)
            struck = jnp.where(j == active, 1.0, 0.0).astype(F32)
            total = (adiag[...] + bd[pl.ds(j, 1), :]) * coef[j, rows, :].astype(F32)
            if h == 1:
                total = total + struck * mixed[rows, :]
            for e in range(EB):
                sign = (1 - 2 * bpar[j, e]).astype(F32)
                total = total + sign * products[locs[bslot[j, e]], bkind[j, e]]
            if h == 0:
                stash[...] = stash[...] + struck * total
            out[rows, columns] = (total * occ[0, j].astype(F32)).astype(BF16)
            return 0

        for part in range(4):
            lax.fori_loop(part * QUARTER, (part + 1) * QUARTER, block, 0)
            if h == 1:
                written(1, part).start()

    def amend():
        rows = pl.ds(0, BLK)
        whole = ((stash[...] + mixed[rows, :]) * occ[0, active].astype(F32)).astype(BF16)

        def block(j, _):
            columns = pl.ds(pl.multiple_of(j * BLK, BLK), BLK)
            out[rows, columns] = jnp.where(j == active, whole, out[rows, columns])
            return 0

        lax.fori_loop(0, NBLK, block, 0)
        for part in range(4):
            written(0, part).start()

    def first_plane():
        stash[...] = jnp.zeros((BLK, BLK), F32)
        finish(0)
        expand(1, 4 * own, 4)

    beside = []
    for n, (hop, dist) in enumerate(order):
        if hop == dist:
            beside.append((n + IN_FLIGHT, functools.partial(land, n)))
            beside.append((L + n + IN_FLIGHT, functools.partial(land, L + n)))
    beside.append((started, functools.partial(expand, 0, 4 * own, 2)))

    def beside_core():
        side_copy().wait_recv()
        expand(0, 4 * own + 2, 2)

    beside.append((started + 1, beside_core))
    beside.append((L + IN_FLIGHT - 1, first_plane))
    for s in range(1, Z):
        beside.append((started + 2 * (s - 1), functools.partial(next_panels, s)))
    late = 2 * L - 2
    beside.append((late - 2, give_shares))
    beside.append((late, close_mixed))
    beside.append((late + 1, amend))
    beside.sort(key=lambda entry: entry[0])
    for g in range(started, 2 * L):
        advance(g)
        while beside and beside[0][0] <= g:
            beside.pop(0)[1]()
    for _, work in beside:
        work()
    finish(1)

    side_copy().wait_send()
    for h in range(2):
        for part in range(4):
            written(h, part).wait()
    for g in range(2 * L - IN_FLIGHT, 2 * L):
        for way in range(2):
            for copy in message(way, g):
                copy.wait_send()

    def left_panels(s, _):
        sent_panels(s)
        return 0

    lax.fori_loop(1, Z, left_panels, 0)
    for i in range(1, X):
        share_copy(i).wait_send()


def solution(mesh):
    n_alpha, n_beta = mesh.shape["alpha"], mesh.shape["beta"]
    Z = 8 if n_alpha == 32 else 1
    X, Y = n_alpha // Z, n_beta // 2
    waiting = sum(2 if 2 * dist == Y else 4 for hop, dist in ORDERS[Y] if hop < dist)

    def local(
        coef,
        alpha_diag,
        beta_diag,
        alpha_tiles,
        beta_tiles,
        occupancy,
        alpha_source,
        alpha_kind,
        alpha_parity,
        slot_device,
        slot_offset,
        beta_slot,
        beta_kind,
        beta_parity,
        mixed_block,
        mixed_kind,
    ):
        hbm = pl.BlockSpec(memory_space=pl.ANY)
        columns = coef.shape[-1]
        small = (
            occupancy,
            slot_device.reshape(-1),
            slot_offset,
            mixed_block,
            mixed_kind,
            alpha_source.T,
            alpha_kind.T,
            alpha_parity.T,
            beta_slot,
            beta_kind,
            beta_parity,
            alpha_diag.reshape(1, BLK),
            beta_diag.reshape(NBLK, BLK),
        )
        result = pl.pallas_call(
            functools.partial(kernel, X, Z, Y),
            out_shape=jax.ShapeDtypeStruct((ROWS, columns), BF16),
            in_specs=[hbm] * (len(small) + 3),
            out_specs=hbm,
            scratch_shapes=[
                *(pltpu.SMEM(v.shape, v.dtype) for v in small[:11]),
                *(pltpu.VMEM(v.shape, v.dtype) for v in small[11:]),
                pltpu.VMEM((NBLK, ROWS, BLK), BF16),
                pltpu.VMEM((33, BLK, BLK), BF16),
                pltpu.VMEM((16, BLK, BLK), BF16),
                pltpu.VMEM((Z, BLK, ROWS), BF16),
                pltpu.VMEM((X, BLK, ROWS), BF16),
                pltpu.VMEM((X, BLK, ROWS), BF16),
                pltpu.VMEM((BLK, BLK), F32),
                pltpu.VMEM((ROWS, BLK), F32),
                pltpu.SMEM((SLOTS,), jnp.int32),
                pltpu.VMEM((2, 2 * n_beta, BLK, BLK), BF16),
                pltpu.VMEM((2, 2 * n_beta, BLK, BLK), BF16),
                pltpu.VMEM((2, 2, waiting, BLK, BLK), BF16),
                pltpu.VMEM((8, BLK, 2 * BLK), BF16),
                pltpu.VMEM((2 * n_beta, 16, BLK, BLK), F32),
                pltpu.VMEM((BLK, BLK), F32),
                pltpu.VMEM((ROWS, columns), BF16),
                pltpu.SemaphoreType.DMA((len(small),)),
                pltpu.SemaphoreType.DMA((2, 4)),
                pltpu.SemaphoreType.DMA((NBLK + 2,)),
                pltpu.SemaphoreType.DMA((2, 2 * len(ORDERS[Y]), 2)),
                pltpu.SemaphoreType.DMA((2, 2 * len(ORDERS[Y]), 2)),
                pltpu.SemaphoreType.DMA((2,)),
                pltpu.SemaphoreType.DMA((2, Z)),
                pltpu.SemaphoreType.DMA((2, Z)),
                pltpu.SemaphoreType.DMA((X,)),
                pltpu.SemaphoreType.DMA((X,)),
            ],
            compiler_params=pltpu.CompilerParams(
                collective_id=0, has_side_effects=True, vmem_limit_bytes=60 * 1024 * 1024
            ),
            cost_estimate=pl.CostEstimate(flops=2200000000, bytes_accessed=3300000, transcendentals=0),
        )(
            *small,
            coef.reshape(ROWS, columns),
            alpha_tiles,
            beta_tiles,
        )
        return result.reshape(coef.shape)

    in_specs = (
        P(None, "alpha", "beta"),
        P("alpha"),
        P("beta"),
        P(),
        P(),
        P("alpha", "beta"),
        P(),
        P(),
        P(),
        P(),
        P(),
        P("beta", None),
        P("beta", None),
        P("beta", None),
        P("beta"),
        P("beta"),
    )
    out_specs = P(None, "alpha", "beta")
    return jax.shard_map(local, mesh=mesh, in_specs=in_specs, out_specs=out_specs, check_vma=False)
```

```python
import functools

import jax
import jax.numpy as jnp
from jax import lax
from jax.experimental import pallas as pl
from jax.experimental.pallas import tpu as pltpu
from jax.sharding import PartitionSpec as P

MESH = pl.DeviceIdType.MESH
BLK = 128
NBLK = 16
SLOTS = 16
EB = 16
EA = 4
ROWS = 2 * BLK
ORDERS = {
    4: ((1, 2), (1, 1), (2, 2)),
    8: ((1, 4), (1, 3), (1, 2), (2, 4), (2, 3), (2, 2), (1, 1), (3, 4), (3, 3), (4, 4)),
}
IN_FLIGHT = 3
F32 = jnp.float32
BF16 = jnp.bfloat16


def kernel(X, Z, Y, *refs):
    small_hbm, (coef_hbm, at_hbm, bt_hbm, out_hbm), small = refs[:13], refs[13:17], refs[17:30]
    occ, sdev, soff, mblk, mkind, asrc, akind, apar, bslot, bkind, bpar, ad, bd = small
    coef, at, bt, panels, share, shares, adiag, mixed, locs, send, recv, passing, wide, products, stash, out, plan, signs = refs[30:48]
    (
        small_sem,
        out_sem,
        local_sem,
        send_sem,
        recv_sem,
        side_sem,
        zsend_sem,
        zrecv_sem,
        xsend_sem,
        xrecv_sem,
    ) = refs[48:]
    NB = 2 * Y
    me_a = lax.axis_index("alpha")
    me_b = lax.axis_index("beta")
    x, z = me_a // Z, lax.rem(me_a, Z)
    y, c = me_b // 2, lax.rem(me_b, 2)

    def peer(p, flip):
        dist = (Y - p) // 2
        dy = jnp.where(lax.rem(p, 2) == 1, dist, Y - dist)
        return lax.rem(y + dy, Y) * 2 + lax.rem(c + flip, 2)

    M = Y // 2
    own = Y - 1
    order = ORDERS[Y]
    up, down = lax.rem(y + 1, Y) * 2, lax.rem(y + Y - 1, Y) * 2

    barrier = pltpu.get_barrier_semaphore()

    for neighbour in (up, up + 1, down, down + 1, y * 2 + 1 - c):
        pl.semaphore_signal(barrier, 1, device_id=(me_a, neighbour), device_id_type=MESH)

    has_next, has_prev = z < Z - 1, z > 0

    @pl.when(has_next)
    def _():
        pl.semaphore_signal(barrier, 1, device_id=(me_a + 1, me_b), device_id_type=MESH)

    @pl.when(has_prev)
    def _():
        pl.semaphore_signal(barrier, 1, device_id=(me_a - 1, me_b), device_id_type=MESH)

    def greet_x(i, _):
        pl.semaphore_signal(barrier, 1, device_id=(lax.rem(x + i, X) * Z + z, me_b), device_id_type=MESH)
        return 0

    lax.fori_loop(1, X, greet_x, 0)

    small_loads = [
        pltpu.make_async_copy(src, dst, small_sem.at[i]) for i, (src, dst) in enumerate(zip(small_hbm, small))
    ]
    for load in small_loads[:4]:
        load.start()

    def block_load(j):
        columns = pl.ds(pl.multiple_of(j * BLK, BLK), BLK)
        return pltpu.make_async_copy(coef_hbm.at[:, columns], coef.at[j], local_sem.at[j])

    tile_loads = [
        pltpu.make_async_copy(at_hbm, at.at[pl.ds(0, 16)], local_sem.at[NBLK]),
        pltpu.make_async_copy(bt_hbm, bt, local_sem.at[NBLK + 1]),
    ]

    def load_block(j, _):
        block_load(j).start()
        return 0

    lax.fori_loop(0, NBLK, load_block, 0)
    for load in small_loads[4:] + tile_loads:
        load.start()
    for load in small_loads[:4]:
        load.wait()

    def await_block(j, _):
        block_load(j).wait()
        return 0

    lax.fori_loop(0, NBLK, await_block, 0)

    def panel_of(block, allowed):
        panel = coef[block]
        return jnp.where(allowed, panel, jnp.zeros_like(panel))

    active = mblk[0]
    mine = panel_of(active, occ[0, active] > 0)
    panels[z] = jnp.concatenate([mine[:BLK], mine[BLK:]], axis=1)

    def pack(p):
        def one(flip, _):
            d = peer(p, flip)
            code = jnp.int32(0)
            for i in range(SLOTS):
                hit = sdev[d * SLOTS + i] == me_b
                code = jnp.where(hit, code * 32 + soff[d * SLOTS + i] + 1, code)
            hi, lo = code >> 5, code & 31
            first = jnp.where(hi > 0, hi, lo)
            second = jnp.where(hi > 0, lo, 0)
            for r, named in enumerate((first, second)):
                block = jnp.clip(named - 1, 0, NBLK - 1)
                panel = panel_of(block, (named > 0) & (occ[0, block] > 0))
                place = (flip + 2 * r) if p == 0 else (4 * p + 2 * flip + r)
                for h in range(2):
                    send[h, place] = panel[h * BLK : (h + 1) * BLK]
            return 0

        lax.fori_loop(0, 2, one, 0)

    pack(0)
    pl.semaphore_wait(barrier, 5 + X - 1 + jnp.where(has_next, 1, 0) + jnp.where(has_prev, 1, 0))

    places, count = {}, 0
    for hop in range(1, M):
        for dist in range(M, hop, -1):
            places[hop, dist] = count
            count += 2 if dist == M else 4

    L = len(order)

    def message(way, g):
        h, i = divmod(g, L)
        hop, dist = order[i]
        p = 0 if dist == M else Y - 1 - 2 * dist if way == 0 else Y - 2 * dist
        size = 2 if dist == M else 4
        first = 2 * way if dist == M else 4 * p
        chip = up if way == 0 else down

        def leg(src, at_, dst, to_at, length, core, flip):
            return pltpu.make_async_remote_copy(
                src_ref=src.at[pl.ds(at_, length)],
                dst_ref=dst.at[pl.ds(to_at, length)],
                send_sem=send_sem.at[way, g, flip],
                recv_sem=recv_sem.at[way, g, flip],
                device_id=(me_a, chip + core),
                device_id_type=MESH,
            )

        src, begin = (send.at[h], first) if hop == 1 else (passing.at[h, way], places[hop - 1, dist])
        if hop < dist:
            return [leg(src, begin, passing.at[h, way], places[hop, dist], size, c, 0)]
        half = size // 2
        return [
            leg(src, begin + half * flip, recv.at[h], first + half * flip, half, lax.rem(c + flip, 2), flip)
            for flip in range(2)
        ]

    def side_copy():
        return pltpu.make_async_remote_copy(
            src_ref=send.at[:, pl.ds(4 * own + 2, 2)],
            dst_ref=recv.at[:, pl.ds(4 * own + 2, 2)],
            send_sem=side_sem.at[0],
            recv_sem=side_sem.at[1],
            device_id=(me_a, y * 2 + 1 - c),
            device_id_type=MESH,
        )

    def advance(g):
        h, i = divmod(g, L)
        hop, dist = order[i]
        for way in range(2):
            if hop > 1:
                for copy in message(way, h * L + order.index((hop - 1, dist))):
                    copy.wait_recv()
            if g >= IN_FLIGHT:
                for copy in message(way, g - IN_FLIGHT):
                    copy.wait_send()
            for copy in message(way, g):
                copy.start()

    def expand(h, first, count):
        def two(n, _):
            start = first + 2 * n
            rows = recv[h, pl.ds(start, 2)].reshape(ROWS, BLK)

            def pair(q, _):
                result = jnp.dot(rows, wide[q], preferred_element_type=F32)
                for a in range(2):
                    for b in range(2):
                        products[(start + a) * 16 + 2 * q + b] = result[a * BLK : (a + 1) * BLK, b * BLK : (b + 1) * BLK]
                return 0

            lax.fori_loop(0, 8, pair, 0, unroll=4)
            return 0

        lax.fori_loop(0, count // 2, two, 0)

    def land(g):
        h, i = divmod(g, L)
        hop, dist = order[i]
        for way in range(2):
            for copy in message(way, g):
                copy.wait_recv()
        if dist == M:
            expand(h, 0, 4)
        else:
            expand(h, 4 * (Y - 1 - 2 * dist), 8)

    def panel_copy(way, s):
        origin, to = (z - s + 1, me_a + 1) if way == 0 else (z + s - 1, me_a - 1)
        origin = jnp.clip(origin, 0, Z - 1)
        return pltpu.make_async_remote_copy(
            src_ref=panels.at[origin],
            dst_ref=panels.at[origin],
            send_sem=zsend_sem.at[way, s],
            recv_sem=zrecv_sem.at[way, s],
            device_id=(to, me_b),
            device_id_type=MESH,
        )

    def panel_leaves(way, s):
        return (z - s + 1 >= 0) & has_next if way == 0 else (z + s - 1 < Z) & has_prev

    def panel_arrives(way, s):
        return z - s >= 0 if way == 0 else z + s < Z

    def start_panels(s):
        for way in range(2):

            @pl.when(panel_leaves(way, s))
            def _():
                panel_copy(way, s).start()

    def await_panels(s):
        for way in range(2):

            @pl.when(panel_arrives(way, s))
            def _():
                origin = jnp.clip(z - s if way == 0 else z + s, 0, Z - 1)
                pltpu.make_async_remote_copy(
                    src_ref=panels.at[origin],
                    dst_ref=panels.at[origin],
                    send_sem=zsend_sem.at[way, s],
                    recv_sem=zrecv_sem.at[way, s],
                    device_id=(jnp.where(has_next, me_a + 1, me_a - 1), me_b),
                    device_id_type=MESH,
                ).wait_recv()

    def sent_panels(s):
        for way in range(2):

            @pl.when(panel_leaves(way, s))
            def _():
                panel_copy(way, s).wait_send()

    def share_copy(i):
        return pltpu.make_async_remote_copy(
            src_ref=share.at[i],
            dst_ref=shares.at[i],
            send_sem=xsend_sem.at[i],
            recv_sem=xrecv_sem.at[i],
            device_id=(lax.rem(x + i, X) * Z + z, me_b),
            device_id_type=MESH,
        )

    def next_panels(s):
        if s < Z:
            await_panels(s)
        if s + 1 < Z:
            start_panels(s + 1)

    started = 0
    for p in range(Y):
        if p > 0:
            pack(p)
        if p == 0 and Z > 1:
            start_panels(1)
        if p % 2 == 0 and started < IN_FLIGHT and order[started][0] == 1:
            advance(started)
            started += 1
    side_copy().start()
    recv[:, pl.ds(4 * own, 2)] = send[:, pl.ds(4 * own, 2)]

    for load in small_loads[4:]:
        load.wait()

    def placed(i, _):
        s = sdev[me_b * SLOTS + i]
        rank = jnp.int32(0)
        for other in range(SLOTS):
            same = (sdev[me_b * SLOTS + other] == s) & (other < i)
            rank = rank + jnp.where(same, 1, 0)
        dy = lax.rem(y - (s >> 1) + Y, Y)
        p = jnp.where(dy < Y // 2, Y - 1 - 2 * dy, 2 * dy - Y)
        flip = (s + c) & 1
        rank = jnp.minimum(rank, 1)
        locs[i] = jnp.where(p == 0, flip + 2 * rank, 4 * p + 2 * flip + rank)
        return 0

    lax.fori_loop(0, SLOTS, placed, 0)

    adiag[...] = jnp.broadcast_to(ad[...], (BLK, BLK)).T

    for load in tile_loads:
        load.wait()

    def negate(i, _):
        at[16 + i] = -at[i]
        return 0

    lax.fori_loop(0, 16, negate, 0)
    at[32] = jnp.zeros((BLK, BLK), BF16)

    def widen(q, _):
        wide[q] = jnp.concatenate([bt[2 * q], bt[2 * q + 1]], axis=1)
        return 0

    lax.fori_loop(0, 8, widen, 0)

    def share_of(i):
        target = lax.rem(x + i, X) * Z + z
        tiles, sources = [], []
        for e in range(EA):
            s = asrc[e, target]
            here = lax.div(s, Z) == x
            tiles.append(at[jnp.where(here, akind[e, target] + 16 * apar[e, target], 32)])
            sources.append(panels[lax.rem(s, Z)])
        return jnp.dot(
            jnp.concatenate(tiles, axis=1), jnp.concatenate(sources, axis=0), preferred_element_type=F32
        )

    def give_shares():
        for i in range(1, X):
            share[i] = share_of(i).astype(BF16)
            share_copy(i).start()

    def close_mixed():
        inner = share_of(0)
        for i in range(1, X):
            share_copy(i).wait_recv()
            inner = inner + shares[i].astype(F32)
        inner = jnp.concatenate([inner[:, :BLK], inner[:, BLK:]], axis=0)
        coarse = inner.astype(BF16)
        fine = (inner - coarse.astype(F32)).astype(BF16)
        closing = bt[mkind[0]]
        mixed[...] = jnp.dot(
            jnp.concatenate([coarse, fine], axis=1),
            jnp.concatenate([closing, closing], axis=0),
            preferred_element_type=F32,
        )

    QUARTER = NBLK // 4

    def written(h, part):
        view = (pl.ds(h * BLK, BLK), pl.ds(part * QUARTER * BLK, QUARTER * BLK))
        return pltpu.make_async_copy(out.at[view], out_hbm.at[view], out_sem.at[h, part])

    def finish(h):
        rows = pl.ds(h * BLK, BLK)

        def block(j, _):
            columns = pl.ds(pl.multiple_of(j * BLK, BLK), BLK)
            struck = jnp.where(j == active, 1.0, 0.0).astype(F32)
            total = (adiag[...] + bd[pl.ds(j, 1), :]) * coef[j, rows, :].astype(F32)
            if h == 1:
                total = total + struck * mixed[rows, :]
            for e in range(EB):
                total = total + signs[j * EB + e] * products[plan[j * EB + e]]
            if h == 0:
                stash[...] = stash[...] + struck * total
            out[rows, columns] = (total * occ[0, j].astype(F32)).astype(BF16)
            return 0

        for part in range(4):
            lax.fori_loop(part * QUARTER, (part + 1) * QUARTER, block, 0)
            if h == 1:
                written(1, part).start()

    def amend():
        rows = pl.ds(0, BLK)
        whole = ((stash[...] + mixed[rows, :]) * occ[0, active].astype(F32)).astype(BF16)

        def block(j, _):
            columns = pl.ds(pl.multiple_of(j * BLK, BLK), BLK)
            out[rows, columns] = jnp.where(j == active, whole, out[rows, columns])
            return 0

        lax.fori_loop(0, NBLK, block, 0)
        for part in range(4):
            written(0, part).start()

    def look_up():
        def one(j, _):
            for e in range(EB):
                plan[j * EB + e] = locs[bslot[j, e]] * 16 + bkind[j, e]
                signs[j * EB + e] = (1 - 2 * bpar[j, e]).astype(F32)
            return 0

        lax.fori_loop(0, NBLK, one, 0)

    def first_plane():
        stash[...] = jnp.zeros((BLK, BLK), F32)
        finish(0)
        expand(1, 4 * own, 4)

    beside = []
    for n, (hop, dist) in enumerate(order):
        if hop == dist:
            beside.append((n + IN_FLIGHT, functools.partial(land, n)))
            beside.append((L + n + IN_FLIGHT, functools.partial(land, L + n)))
    beside.append((started, functools.partial(expand, 0, 4 * own, 2)))

    def beside_core():
        side_copy().wait_recv()
        expand(0, 4 * own + 2, 2)

    beside.append((started + 1, beside_core))
    beside.append((started + 1, look_up))
    beside.append((L + IN_FLIGHT - 1, first_plane))
    for s in range(1, Z):
        beside.append((started + 2 * (s - 1), functools.partial(next_panels, s)))
    late = 2 * L - 2
    beside.append((late - 2, give_shares))
    beside.append((late, close_mixed))
    beside.append((late + 1, amend))
    beside.sort(key=lambda entry: entry[0])
    for g in range(started, 2 * L):
        advance(g)
        while beside and beside[0][0] <= g:
            beside.pop(0)[1]()
    for _, work in beside:
        work()
    finish(1)

    side_copy().wait_send()
    for h in range(2):
        for part in range(4):
            written(h, part).wait()
    for g in range(2 * L - IN_FLIGHT, 2 * L):
        for way in range(2):
            for copy in message(way, g):
                copy.wait_send()

    def left_panels(s, _):
        sent_panels(s)
        return 0

    lax.fori_loop(1, Z, left_panels, 0)
    for i in range(1, X):
        share_copy(i).wait_send()


def solution(mesh):
    n_alpha, n_beta = mesh.shape["alpha"], mesh.shape["beta"]
    Z = 8 if n_alpha == 32 else 1
    X, Y = n_alpha // Z, n_beta // 2
    waiting = sum(2 if 2 * dist == Y else 4 for hop, dist in ORDERS[Y] if hop < dist)

    def local(
        coef,
        alpha_diag,
        beta_diag,
        alpha_tiles,
        beta_tiles,
        occupancy,
        alpha_source,
        alpha_kind,
        alpha_parity,
        slot_device,
        slot_offset,
        beta_slot,
        beta_kind,
        beta_parity,
        mixed_block,
        mixed_kind,
    ):
        hbm = pl.BlockSpec(memory_space=pl.ANY)
        columns = coef.shape[-1]
        small = (
            occupancy,
            slot_device.reshape(-1),
            slot_offset,
            mixed_block,
            mixed_kind,
            alpha_source.T,
            alpha_kind.T,
            alpha_parity.T,
            beta_slot,
            beta_kind,
            beta_parity,
            alpha_diag.reshape(1, BLK),
            beta_diag.reshape(NBLK, BLK),
        )
        result = pl.pallas_call(
            functools.partial(kernel, X, Z, Y),
            out_shape=jax.ShapeDtypeStruct((ROWS, columns), BF16),
            in_specs=[hbm] * (len(small) + 3),
            out_specs=hbm,
            scratch_shapes=[
                *(pltpu.SMEM(v.shape, v.dtype) for v in small[:11]),
                *(pltpu.VMEM(v.shape, v.dtype) for v in small[11:]),
                pltpu.VMEM((NBLK, ROWS, BLK), BF16),
                pltpu.VMEM((33, BLK, BLK), BF16),
                pltpu.VMEM((16, BLK, BLK), BF16),
                pltpu.VMEM((Z, BLK, ROWS), BF16),
                pltpu.VMEM((X, BLK, ROWS), BF16),
                pltpu.VMEM((X, BLK, ROWS), BF16),
                pltpu.VMEM((BLK, BLK), F32),
                pltpu.VMEM((ROWS, BLK), F32),
                pltpu.SMEM((SLOTS,), jnp.int32),
                pltpu.VMEM((2, 2 * n_beta, BLK, BLK), BF16),
                pltpu.VMEM((2, 2 * n_beta, BLK, BLK), BF16),
                pltpu.VMEM((2, 2, waiting, BLK, BLK), BF16),
                pltpu.VMEM((8, BLK, 2 * BLK), BF16),
                pltpu.VMEM((2 * n_beta * 16, BLK, BLK), F32),
                pltpu.VMEM((BLK, BLK), F32),
                pltpu.VMEM((ROWS, columns), BF16),
                pltpu.SMEM((NBLK * EB,), jnp.int32),
                pltpu.SMEM((NBLK * EB,), F32),
                pltpu.SemaphoreType.DMA((len(small),)),
                pltpu.SemaphoreType.DMA((2, 4)),
                pltpu.SemaphoreType.DMA((NBLK + 2,)),
                pltpu.SemaphoreType.DMA((2, 2 * len(ORDERS[Y]), 2)),
                pltpu.SemaphoreType.DMA((2, 2 * len(ORDERS[Y]), 2)),
                pltpu.SemaphoreType.DMA((2,)),
                pltpu.SemaphoreType.DMA((2, Z)),
                pltpu.SemaphoreType.DMA((2, Z)),
                pltpu.SemaphoreType.DMA((X,)),
                pltpu.SemaphoreType.DMA((X,)),
            ],
            compiler_params=pltpu.CompilerParams(
                collective_id=0, has_side_effects=True, vmem_limit_bytes=60 * 1024 * 1024
            ),
            cost_estimate=pl.CostEstimate(flops=2200000000, bytes_accessed=3300000, transcendentals=0),
        )(
            *small,
            coef.reshape(ROWS, columns),
            alpha_tiles,
            beta_tiles,
        )
        return result.reshape(coef.shape)

    in_specs = (
        P(None, "alpha", "beta"),
        P("alpha"),
        P("beta"),
        P(),
        P(),
        P("alpha", "beta"),
        P(),
        P(),
        P(),
        P(),
        P(),
        P("beta", None),
        P("beta", None),
        P("beta", None),
        P("beta"),
        P("beta"),
    )
    out_specs = P(None, "alpha", "beta")
    return jax.shard_map(local, mesh=mesh, in_specs=in_specs, out_specs=out_specs, check_vma=False)
```

```python
import functools

import jax
import jax.numpy as jnp
from jax import lax
from jax.experimental import pallas as pl
from jax.experimental.pallas import tpu as pltpu
from jax.sharding import PartitionSpec as P

MESH = pl.DeviceIdType.MESH
BLK = 128
NBLK = 16
SLOTS = 16
EB = 16
EA = 4
ROWS = 2 * BLK
ORDERS = {
    4: ((1, 2), (1, 1), (2, 2)),
    8: ((1, 4), (1, 3), (1, 2), (2, 4), (2, 3), (2, 2), (1, 1), (3, 4), (3, 3), (4, 4)),
}
IN_FLIGHT = 5
F32 = jnp.float32
BF16 = jnp.bfloat16


def kernel(X, Z, Y, *refs):
    small_hbm, (coef_hbm, at_hbm, bt_hbm, out_hbm), small = refs[:13], refs[13:17], refs[17:30]
    occ, sdev, soff, mblk, mkind, asrc, akind, apar, bslot, bkind, bpar, ad, bd = small
    coef, at, bt, panels, share, shares, adiag, mixed, locs, send, recv, passing, wide, products, stash, out, plan, signs = refs[30:48]
    (
        small_sem,
        out_sem,
        local_sem,
        send_sem,
        recv_sem,
        side_sem,
        zsend_sem,
        zrecv_sem,
        xsend_sem,
        xrecv_sem,
    ) = refs[48:]
    NB = 2 * Y
    me_a = lax.axis_index("alpha")
    me_b = lax.axis_index("beta")
    x, z = me_a // Z, lax.rem(me_a, Z)
    y, c = me_b // 2, lax.rem(me_b, 2)

    def peer(p, flip):
        dist = (Y - p) // 2
        dy = jnp.where(lax.rem(p, 2) == 1, dist, Y - dist)
        return lax.rem(y + dy, Y) * 2 + lax.rem(c + flip, 2)

    M = Y // 2
    own = Y - 1
    order = ORDERS[Y]
    up, down = lax.rem(y + 1, Y) * 2, lax.rem(y + Y - 1, Y) * 2

    barrier = pltpu.get_barrier_semaphore()

    for neighbour in (up, up + 1, down, down + 1, y * 2 + 1 - c):
        pl.semaphore_signal(barrier, 1, device_id=(me_a, neighbour), device_id_type=MESH)

    has_next, has_prev = z < Z - 1, z > 0

    @pl.when(has_next)
    def _():
        pl.semaphore_signal(barrier, 1, device_id=(me_a + 1, me_b), device_id_type=MESH)

    @pl.when(has_prev)
    def _():
        pl.semaphore_signal(barrier, 1, device_id=(me_a - 1, me_b), device_id_type=MESH)

    def greet_x(i, _):
        pl.semaphore_signal(barrier, 1, device_id=(lax.rem(x + i, X) * Z + z, me_b), device_id_type=MESH)
        return 0

    lax.fori_loop(1, X, greet_x, 0)

    small_loads = [
        pltpu.make_async_copy(src, dst, small_sem.at[i]) for i, (src, dst) in enumerate(zip(small_hbm, small))
    ]
    for load in small_loads[:4]:
        load.start()

    def block_load(j):
        columns = pl.ds(pl.multiple_of(j * BLK, BLK), BLK)
        return pltpu.make_async_copy(coef_hbm.at[:, columns], coef.at[j], local_sem.at[j])

    tile_loads = [
        pltpu.make_async_copy(at_hbm, at.at[pl.ds(0, 16)], local_sem.at[NBLK]),
        pltpu.make_async_copy(bt_hbm, bt, local_sem.at[NBLK + 1]),
    ]

    def load_block(j, _):
        block_load(j).start()
        return 0

    lax.fori_loop(0, NBLK, load_block, 0)
    for load in small_loads[4:] + tile_loads:
        load.start()
    for load in small_loads[:4]:
        load.wait()

    def await_block(j, _):
        block_load(j).wait()
        return 0

    lax.fori_loop(0, NBLK, await_block, 0)

    def panel_of(block, allowed):
        panel = coef[block]
        return jnp.where(allowed, panel, jnp.zeros_like(panel))

    active = mblk[0]
    mine = panel_of(active, occ[0, active] > 0)
    panels[z] = jnp.concatenate([mine[:BLK], mine[BLK:]], axis=1)

    def pack(p):
        def one(flip, _):
            d = peer(p, flip)
            code = jnp.int32(0)
            for i in range(SLOTS):
                hit = sdev[d * SLOTS + i] == me_b
                code = jnp.where(hit, code * 32 + soff[d * SLOTS + i] + 1, code)
            hi, lo = code >> 5, code & 31
            first = jnp.where(hi > 0, hi, lo)
            second = jnp.where(hi > 0, lo, 0)
            for r, named in enumerate((first, second)):
                block = jnp.clip(named - 1, 0, NBLK - 1)
                panel = panel_of(block, (named > 0) & (occ[0, block] > 0))
                place = (flip + 2 * r) if p == 0 else (4 * p + 2 * flip + r)
                for h in range(2):
                    send[h, place] = panel[h * BLK : (h + 1) * BLK]
            return 0

        lax.fori_loop(0, 2, one, 0)

    pack(0)
    pl.semaphore_wait(barrier, 5 + X - 1 + jnp.where(has_next, 1, 0) + jnp.where(has_prev, 1, 0))

    places, count = {}, 0
    for hop in range(1, M):
        for dist in range(M, hop, -1):
            places[hop, dist] = count
            count += 2 if dist == M else 4

    L = len(order)

    def message(way, g):
        h, i = divmod(g, L)
        hop, dist = order[i]
        p = 0 if dist == M else Y - 1 - 2 * dist if way == 0 else Y - 2 * dist
        size = 2 if dist == M else 4
        first = 2 * way if dist == M else 4 * p
        chip = up if way == 0 else down

        def leg(src, at_, dst, to_at, length, core, flip):
            return pltpu.make_async_remote_copy(
                src_ref=src.at[pl.ds(at_, length)],
                dst_ref=dst.at[pl.ds(to_at, length)],
                send_sem=send_sem.at[way, g, flip],
                recv_sem=recv_sem.at[way, g, flip],
                device_id=(me_a, chip + core),
                device_id_type=MESH,
            )

        src, begin = (send.at[h], first) if hop == 1 else (passing.at[h, way], places[hop - 1, dist])
        if hop < dist:
            return [leg(src, begin, passing.at[h, way], places[hop, dist], size, c, 0)]
        half = size // 2
        return [
            leg(src, begin + half * flip, recv.at[h], first + half * flip, half, lax.rem(c + flip, 2), flip)
            for flip in range(2)
        ]

    def side_copy():
        return pltpu.make_async_remote_copy(
            src_ref=send.at[:, pl.ds(4 * own + 2, 2)],
            dst_ref=recv.at[:, pl.ds(4 * own + 2, 2)],
            send_sem=side_sem.at[0],
            recv_sem=side_sem.at[1],
            device_id=(me_a, y * 2 + 1 - c),
            device_id_type=MESH,
        )

    def advance(g):
        h, i = divmod(g, L)
        hop, dist = order[i]
        for way in range(2):
            if hop > 1:
                for copy in message(way, h * L + order.index((hop - 1, dist))):
                    copy.wait_recv()
            if g >= IN_FLIGHT:
                for copy in message(way, g - IN_FLIGHT):
                    copy.wait_send()
            for copy in message(way, g):
                copy.start()

    def expand(h, first, count):
        def two(n, _):
            start = first + 2 * n
            rows = recv[h, pl.ds(start, 2)].reshape(ROWS, BLK)

            def pair(q, _):
                result = jnp.dot(rows, wide[q], preferred_element_type=F32)
                for a in range(2):
                    for b in range(2):
                        products[(start + a) * 16 + 2 * q + b] = result[a * BLK : (a + 1) * BLK, b * BLK : (b + 1) * BLK]
                return 0

            lax.fori_loop(0, 8, pair, 0, unroll=4)
            return 0

        lax.fori_loop(0, count // 2, two, 0)

    def land(g):
        h, i = divmod(g, L)
        hop, dist = order[i]
        for way in range(2):
            for copy in message(way, g):
                copy.wait_recv()
        if dist == M:
            expand(h, 0, 4)
        else:
            expand(h, 4 * (Y - 1 - 2 * dist), 8)

    def panel_copy(way, s):
        origin, to = (z - s + 1, me_a + 1) if way == 0 else (z + s - 1, me_a - 1)
        origin = jnp.clip(origin, 0, Z - 1)
        return pltpu.make_async_remote_copy(
            src_ref=panels.at[origin],
            dst_ref=panels.at[origin],
            send_sem=zsend_sem.at[way, s],
            recv_sem=zrecv_sem.at[way, s],
            device_id=(to, me_b),
            device_id_type=MESH,
        )

    def panel_leaves(way, s):
        return (z - s + 1 >= 0) & has_next if way == 0 else (z + s - 1 < Z) & has_prev

    def panel_arrives(way, s):
        return z - s >= 0 if way == 0 else z + s < Z

    def start_panels(s):
        for way in range(2):

            @pl.when(panel_leaves(way, s))
            def _():
                panel_copy(way, s).start()

    def await_panels(s):
        for way in range(2):

            @pl.when(panel_arrives(way, s))
            def _():
                origin = jnp.clip(z - s if way == 0 else z + s, 0, Z - 1)
                pltpu.make_async_remote_copy(
                    src_ref=panels.at[origin],
                    dst_ref=panels.at[origin],
                    send_sem=zsend_sem.at[way, s],
                    recv_sem=zrecv_sem.at[way, s],
                    device_id=(jnp.where(has_next, me_a + 1, me_a - 1), me_b),
                    device_id_type=MESH,
                ).wait_recv()

    def sent_panels(s):
        for way in range(2):

            @pl.when(panel_leaves(way, s))
            def _():
                panel_copy(way, s).wait_send()

    def share_copy(i):
        return pltpu.make_async_remote_copy(
            src_ref=share.at[i],
            dst_ref=shares.at[i],
            send_sem=xsend_sem.at[i],
            recv_sem=xrecv_sem.at[i],
            device_id=(lax.rem(x + i, X) * Z + z, me_b),
            device_id_type=MESH,
        )

    def next_panels(s):
        if s < Z:
            await_panels(s)
        if s + 1 < Z:
            start_panels(s + 1)

    started = 0
    for p in range(Y):
        if p > 0:
            pack(p)
        if p == 0 and Z > 1:
            start_panels(1)
        if p % 2 == 0 and started < IN_FLIGHT and order[started][0] == 1:
            advance(started)
            started += 1
    side_copy().start()
    recv[:, pl.ds(4 * own, 2)] = send[:, pl.ds(4 * own, 2)]

    for load in small_loads[4:]:
        load.wait()

    def placed(i, _):
        s = sdev[me_b * SLOTS + i]
        rank = jnp.int32(0)
        for other in range(SLOTS):
            same = (sdev[me_b * SLOTS + other] == s) & (other < i)
            rank = rank + jnp.where(same, 1, 0)
        dy = lax.rem(y - (s >> 1) + Y, Y)
        p = jnp.where(dy < Y // 2, Y - 1 - 2 * dy, 2 * dy - Y)
        flip = (s + c) & 1
        rank = jnp.minimum(rank, 1)
        locs[i] = jnp.where(p == 0, flip + 2 * rank, 4 * p + 2 * flip + rank)
        return 0

    lax.fori_loop(0, SLOTS, placed, 0)

    adiag[...] = jnp.broadcast_to(ad[...], (BLK, BLK)).T

    for load in tile_loads:
        load.wait()

    def negate(i, _):
        at[16 + i] = -at[i]
        return 0

    lax.fori_loop(0, 16, negate, 0)
    at[32] = jnp.zeros((BLK, BLK), BF16)

    def widen(q, _):
        wide[q] = jnp.concatenate([bt[2 * q], bt[2 * q + 1]], axis=1)
        return 0

    lax.fori_loop(0, 8, widen, 0)

    def share_of(i):
        target = lax.rem(x + i, X) * Z + z
        tiles, sources = [], []
        for e in range(EA):
            s = asrc[e, target]
            here = lax.div(s, Z) == x
            tiles.append(at[jnp.where(here, akind[e, target] + 16 * apar[e, target], 32)])
            sources.append(panels[lax.rem(s, Z)])
        return jnp.dot(
            jnp.concatenate(tiles, axis=1), jnp.concatenate(sources, axis=0), preferred_element_type=F32
        )

    def give_shares():
        for i in range(1, X):
            share[i] = share_of(i).astype(BF16)
            share_copy(i).start()

    def close_mixed():
        inner = share_of(0)
        for i in range(1, X):
            share_copy(i).wait_recv()
            inner = inner + shares[i].astype(F32)
        inner = jnp.concatenate([inner[:, :BLK], inner[:, BLK:]], axis=0)
        coarse = inner.astype(BF16)
        fine = (inner - coarse.astype(F32)).astype(BF16)
        closing = bt[mkind[0]]
        mixed[...] = jnp.dot(
            jnp.concatenate([coarse, fine], axis=1),
            jnp.concatenate([closing, closing], axis=0),
            preferred_element_type=F32,
        )

    QUARTER = NBLK // 4

    def written(h, part):
        view = (pl.ds(h * BLK, BLK), pl.ds(part * QUARTER * BLK, QUARTER * BLK))
        return pltpu.make_async_copy(out.at[view], out_hbm.at[view], out_sem.at[h, part])

    def finish(h):
        rows = pl.ds(h * BLK, BLK)

        def block(j, _):
            columns = pl.ds(pl.multiple_of(j * BLK, BLK), BLK)
            struck = jnp.where(j == active, 1.0, 0.0).astype(F32)
            total = (adiag[...] + bd[pl.ds(j, 1), :]) * coef[j, rows, :].astype(F32)
            if h == 1:
                total = total + struck * mixed[rows, :]
            for e in range(EB):
                total = total + signs[j * EB + e] * products[plan[j * EB + e]]
            if h == 0:
                stash[...] = stash[...] + struck * total
            out[rows, columns] = (total * occ[0, j].astype(F32)).astype(BF16)
            return 0

        for part in range(4):
            lax.fori_loop(part * QUARTER, (part + 1) * QUARTER, block, 0)
            if h == 1:
                written(1, part).start()

    def amend():
        rows = pl.ds(0, BLK)
        whole = ((stash[...] + mixed[rows, :]) * occ[0, active].astype(F32)).astype(BF16)

        def block(j, _):
            columns = pl.ds(pl.multiple_of(j * BLK, BLK), BLK)
            out[rows, columns] = jnp.where(j == active, whole, out[rows, columns])
            return 0

        lax.fori_loop(0, NBLK, block, 0)
        for part in range(4):
            written(0, part).start()

    def look_up():
        def one(j, _):
            for e in range(EB):
                plan[j * EB + e] = locs[bslot[j, e]] * 16 + bkind[j, e]
                signs[j * EB + e] = (1 - 2 * bpar[j, e]).astype(F32)
            return 0

        lax.fori_loop(0, NBLK, one, 0)

    def first_plane():
        stash[...] = jnp.zeros((BLK, BLK), F32)
        finish(0)
        expand(1, 4 * own, 4)

    beside = []
    for n, (hop, dist) in enumerate(order):
        if hop == dist:
            beside.append((n + IN_FLIGHT, functools.partial(land, n)))
            beside.append((L + n + IN_FLIGHT, functools.partial(land, L + n)))
    beside.append((started, functools.partial(expand, 0, 4 * own, 2)))

    def beside_core():
        side_copy().wait_recv()
        expand(0, 4 * own + 2, 2)

    beside.append((started + 1, beside_core))
    beside.append((started + 1, look_up))
    beside.append((L + IN_FLIGHT - 1, first_plane))
    for s in range(1, Z):
        beside.append((started + 2 * (s - 1), functools.partial(next_panels, s)))
    late = 2 * L - 2
    beside.append((late - 2, give_shares))
    beside.append((late, close_mixed))
    beside.append((late + 1, amend))
    beside.sort(key=lambda entry: entry[0])
    for g in range(started, 2 * L):
        advance(g)
        while beside and beside[0][0] <= g:
            beside.pop(0)[1]()
    for _, work in beside:
        work()
    finish(1)

    side_copy().wait_send()
    for h in range(2):
        for part in range(4):
            written(h, part).wait()
    for g in range(2 * L - IN_FLIGHT, 2 * L):
        for way in range(2):
            for copy in message(way, g):
                copy.wait_send()

    def left_panels(s, _):
        sent_panels(s)
        return 0

    lax.fori_loop(1, Z, left_panels, 0)
    for i in range(1, X):
        share_copy(i).wait_send()


def solution(mesh):
    n_alpha, n_beta = mesh.shape["alpha"], mesh.shape["beta"]
    Z = 8 if n_alpha == 32 else 1
    X, Y = n_alpha // Z, n_beta // 2
    waiting = sum(2 if 2 * dist == Y else 4 for hop, dist in ORDERS[Y] if hop < dist)

    def local(
        coef,
        alpha_diag,
        beta_diag,
        alpha_tiles,
        beta_tiles,
        occupancy,
        alpha_source,
        alpha_kind,
        alpha_parity,
        slot_device,
        slot_offset,
        beta_slot,
        beta_kind,
        beta_parity,
        mixed_block,
        mixed_kind,
    ):
        hbm = pl.BlockSpec(memory_space=pl.ANY)
        columns = coef.shape[-1]
        small = (
            occupancy,
            slot_device.reshape(-1),
            slot_offset,
            mixed_block,
            mixed_kind,
            alpha_source.T,
            alpha_kind.T,
            alpha_parity.T,
            beta_slot,
            beta_kind,
            beta_parity,
            alpha_diag.reshape(1, BLK),
            beta_diag.reshape(NBLK, BLK),
        )
        result = pl.pallas_call(
            functools.partial(kernel, X, Z, Y),
            out_shape=jax.ShapeDtypeStruct((ROWS, columns), BF16),
            in_specs=[hbm] * (len(small) + 3),
            out_specs=hbm,
            scratch_shapes=[
                *(pltpu.SMEM(v.shape, v.dtype) for v in small[:11]),
                *(pltpu.VMEM(v.shape, v.dtype) for v in small[11:]),
                pltpu.VMEM((NBLK, ROWS, BLK), BF16),
                pltpu.VMEM((33, BLK, BLK), BF16),
                pltpu.VMEM((16, BLK, BLK), BF16),
                pltpu.VMEM((Z, BLK, ROWS), BF16),
                pltpu.VMEM((X, BLK, ROWS), BF16),
                pltpu.VMEM((X, BLK, ROWS), BF16),
                pltpu.VMEM((BLK, BLK), F32),
                pltpu.VMEM((ROWS, BLK), F32),
                pltpu.SMEM((SLOTS,), jnp.int32),
                pltpu.VMEM((2, 2 * n_beta, BLK, BLK), BF16),
                pltpu.VMEM((2, 2 * n_beta, BLK, BLK), BF16),
                pltpu.VMEM((2, 2, waiting, BLK, BLK), BF16),
                pltpu.VMEM((8, BLK, 2 * BLK), BF16),
                pltpu.VMEM((2 * n_beta * 16, BLK, BLK), F32),
                pltpu.VMEM((BLK, BLK), F32),
                pltpu.VMEM((ROWS, columns), BF16),
                pltpu.SMEM((NBLK * EB,), jnp.int32),
                pltpu.SMEM((NBLK * EB,), F32),
                pltpu.SemaphoreType.DMA((len(small),)),
                pltpu.SemaphoreType.DMA((2, 4)),
                pltpu.SemaphoreType.DMA((NBLK + 2,)),
                pltpu.SemaphoreType.DMA((2, 2 * len(ORDERS[Y]), 2)),
                pltpu.SemaphoreType.DMA((2, 2 * len(ORDERS[Y]), 2)),
                pltpu.SemaphoreType.DMA((2,)),
                pltpu.SemaphoreType.DMA((2, Z)),
                pltpu.SemaphoreType.DMA((2, Z)),
                pltpu.SemaphoreType.DMA((X,)),
                pltpu.SemaphoreType.DMA((X,)),
            ],
            compiler_params=pltpu.CompilerParams(
                collective_id=0, has_side_effects=True, vmem_limit_bytes=60 * 1024 * 1024
            ),
            cost_estimate=pl.CostEstimate(flops=2200000000, bytes_accessed=3300000, transcendentals=0),
        )(
            *small,
            coef.reshape(ROWS, columns),
            alpha_tiles,
            beta_tiles,
        )
        return result.reshape(coef.shape)

    in_specs = (
        P(None, "alpha", "beta"),
        P("alpha"),
        P("beta"),
        P(),
        P(),
        P("alpha", "beta"),
        P(),
        P(),
        P(),
        P(),
        P(),
        P("beta", None),
        P("beta", None),
        P("beta", None),
        P("beta"),
        P("beta"),
    )
    out_specs = P(None, "alpha", "beta")
    return jax.shard_map(local, mesh=mesh, in_specs=in_specs, out_specs=out_specs, check_vma=False)
```

```python
import functools

import jax
import jax.numpy as jnp
from jax import lax
from jax.experimental import pallas as pl
from jax.experimental.pallas import tpu as pltpu
from jax.sharding import PartitionSpec as P

MESH = pl.DeviceIdType.MESH
BLK = 128
NBLK = 16
SLOTS = 16
EB = 16
EA = 4
ROWS = 2 * BLK
ORDERS = {
    4: ((1, 2), (1, 1), (2, 2)),
    8: ((1, 4), (1, 3), (1, 2), (2, 4), (2, 3), (2, 2), (1, 1), (3, 4), (3, 3), (4, 4)),
}
IN_FLIGHT = 2
F32 = jnp.float32
BF16 = jnp.bfloat16


def kernel(X, Z, Y, *refs):
    small_hbm, (coef_hbm, at_hbm, bt_hbm, out_hbm), small = refs[:13], refs[13:17], refs[17:30]
    occ, sdev, soff, mblk, mkind, asrc, akind, apar, bslot, bkind, bpar, ad, bd = small
    coef, at, bt, panels, share, shares, adiag, mixed, locs, send, recv, passing, wide, products, stash, out, plan, signs = refs[30:48]
    (
        small_sem,
        out_sem,
        local_sem,
        send_sem,
        recv_sem,
        side_sem,
        zsend_sem,
        zrecv_sem,
        xsend_sem,
        xrecv_sem,
    ) = refs[48:]
    NB = 2 * Y
    me_a = lax.axis_index("alpha")
    me_b = lax.axis_index("beta")
    x, z = me_a // Z, lax.rem(me_a, Z)
    y, c = me_b // 2, lax.rem(me_b, 2)

    def peer(p, flip):
        dist = (Y - p) // 2
        dy = jnp.where(lax.rem(p, 2) == 1, dist, Y - dist)
        return lax.rem(y + dy, Y) * 2 + lax.rem(c + flip, 2)

    M = Y // 2
    own = Y - 1
    order = ORDERS[Y]
    up, down = lax.rem(y + 1, Y) * 2, lax.rem(y + Y - 1, Y) * 2

    barrier = pltpu.get_barrier_semaphore()

    for neighbour in (up, up + 1, down, down + 1, y * 2 + 1 - c):
        pl.semaphore_signal(barrier, 1, device_id=(me_a, neighbour), device_id_type=MESH)

    has_next, has_prev = z < Z - 1, z > 0

    @pl.when(has_next)
    def _():
        pl.semaphore_signal(barrier, 1, device_id=(me_a + 1, me_b), device_id_type=MESH)

    @pl.when(has_prev)
    def _():
        pl.semaphore_signal(barrier, 1, device_id=(me_a - 1, me_b), device_id_type=MESH)

    def greet_x(i, _):
        pl.semaphore_signal(barrier, 1, device_id=(lax.rem(x + i, X) * Z + z, me_b), device_id_type=MESH)
        return 0

    lax.fori_loop(1, X, greet_x, 0)

    small_loads = [
        pltpu.make_async_copy(src, dst, small_sem.at[i]) for i, (src, dst) in enumerate(zip(small_hbm, small))
    ]
    for load in small_loads[:4]:
        load.start()

    def block_load(j):
        columns = pl.ds(pl.multiple_of(j * BLK, BLK), BLK)
        return pltpu.make_async_copy(coef_hbm.at[:, columns], coef.at[j], local_sem.at[j])

    tile_loads = [
        pltpu.make_async_copy(at_hbm, at.at[pl.ds(0, 16)], local_sem.at[NBLK]),
        pltpu.make_async_copy(bt_hbm, bt, local_sem.at[NBLK + 1]),
    ]

    def load_block(j, _):
        block_load(j).start()
        return 0

    lax.fori_loop(0, NBLK, load_block, 0)
    for load in small_loads[4:] + tile_loads:
        load.start()
    for load in small_loads[:4]:
        load.wait()

    def await_block(j, _):
        block_load(j).wait()
        return 0

    lax.fori_loop(0, NBLK, await_block, 0)

    def panel_of(block, allowed):
        panel = coef[block]
        return jnp.where(allowed, panel, jnp.zeros_like(panel))

    active = mblk[0]
    mine = panel_of(active, occ[0, active] > 0)
    panels[z] = jnp.concatenate([mine[:BLK], mine[BLK:]], axis=1)

    def pack(p):
        def one(flip, _):
            d = peer(p, flip)
            code = jnp.int32(0)
            for i in range(SLOTS):
                hit = sdev[d * SLOTS + i] == me_b
                code = jnp.where(hit, code * 32 + soff[d * SLOTS + i] + 1, code)
            hi, lo = code >> 5, code & 31
            first = jnp.where(hi > 0, hi, lo)
            second = jnp.where(hi > 0, lo, 0)
            for r, named in enumerate((first, second)):
                block = jnp.clip(named - 1, 0, NBLK - 1)
                panel = panel_of(block, (named > 0) & (occ[0, block] > 0))
                place = (flip + 2 * r) if p == 0 else (4 * p + 2 * flip + r)
                for h in range(2):
                    send[h, place] = panel[h * BLK : (h + 1) * BLK]
            return 0

        lax.fori_loop(0, 2, one, 0)

    pack(0)
    pl.semaphore_wait(barrier, 5 + X - 1 + jnp.where(has_next, 1, 0) + jnp.where(has_prev, 1, 0))

    places, count = {}, 0
    for hop in range(1, M):
        for dist in range(M, hop, -1):
            places[hop, dist] = count
            count += 2 if dist == M else 4

    L = len(order)

    def message(way, g):
        h, i = divmod(g, L)
        hop, dist = order[i]
        p = 0 if dist == M else Y - 1 - 2 * dist if way == 0 else Y - 2 * dist
        size = 2 if dist == M else 4
        first = 2 * way if dist == M else 4 * p
        chip = up if way == 0 else down

        def leg(src, at_, dst, to_at, length, core, flip):
            return pltpu.make_async_remote_copy(
                src_ref=src.at[pl.ds(at_, length)],
                dst_ref=dst.at[pl.ds(to_at, length)],
                send_sem=send_sem.at[way, g, flip],
                recv_sem=recv_sem.at[way, g, flip],
                device_id=(me_a, chip + core),
                device_id_type=MESH,
            )

        src, begin = (send.at[h], first) if hop == 1 else (passing.at[h, way], places[hop - 1, dist])
        if hop < dist:
            return [leg(src, begin, passing.at[h, way], places[hop, dist], size, c, 0)]
        half = size // 2
        return [
            leg(src, begin + half * flip, recv.at[h], first + half * flip, half, lax.rem(c + flip, 2), flip)
            for flip in range(2)
        ]

    def side_copy():
        return pltpu.make_async_remote_copy(
            src_ref=send.at[:, pl.ds(4 * own + 2, 2)],
            dst_ref=recv.at[:, pl.ds(4 * own + 2, 2)],
            send_sem=side_sem.at[0],
            recv_sem=side_sem.at[1],
            device_id=(me_a, y * 2 + 1 - c),
            device_id_type=MESH,
        )

    def advance(g):
        h, i = divmod(g, L)
        hop, dist = order[i]
        for way in range(2):
            if hop > 1:
                for copy in message(way, h * L + order.index((hop - 1, dist))):
                    copy.wait_recv()
            if g >= IN_FLIGHT:
                for copy in message(way, g - IN_FLIGHT):
                    copy.wait_send()
            for copy in message(way, g):
                copy.start()

    def expand(h, first, count):
        def two(n, _):
            start = first + 2 * n
            rows = recv[h, pl.ds(start, 2)].reshape(ROWS, BLK)

            def pair(q, _):
                result = jnp.dot(rows, wide[q], preferred_element_type=F32)
                for a in range(2):
                    for b in range(2):
                        products[(start + a) * 16 + 2 * q + b] = result[a * BLK : (a + 1) * BLK, b * BLK : (b + 1) * BLK]
                return 0

            lax.fori_loop(0, 8, pair, 0, unroll=4)
            return 0

        lax.fori_loop(0, count // 2, two, 0)

    def land(g):
        h, i = divmod(g, L)
        hop, dist = order[i]
        for way in range(2):
            for copy in message(way, g):
                copy.wait_recv()
        if dist == M:
            expand(h, 0, 4)
        else:
            expand(h, 4 * (Y - 1 - 2 * dist), 8)

    def panel_copy(way, s):
        origin, to = (z - s + 1, me_a + 1) if way == 0 else (z + s - 1, me_a - 1)
        origin = jnp.clip(origin, 0, Z - 1)
        return pltpu.make_async_remote_copy(
            src_ref=panels.at[origin],
            dst_ref=panels.at[origin],
            send_sem=zsend_sem.at[way, s],
            recv_sem=zrecv_sem.at[way, s],
            device_id=(to, me_b),
            device_id_type=MESH,
        )

    def panel_leaves(way, s):
        return (z - s + 1 >= 0) & has_next if way == 0 else (z + s - 1 < Z) & has_prev

    def panel_arrives(way, s):
        return z - s >= 0 if way == 0 else z + s < Z

    def start_panels(s):
        for way in range(2):

            @pl.when(panel_leaves(way, s))
            def _():
                panel_copy(way, s).start()

    def await_panels(s):
        for way in range(2):

            @pl.when(panel_arrives(way, s))
            def _():
                origin = jnp.clip(z - s if way == 0 else z + s, 0, Z - 1)
                pltpu.make_async_remote_copy(
                    src_ref=panels.at[origin],
                    dst_ref=panels.at[origin],
                    send_sem=zsend_sem.at[way, s],
                    recv_sem=zrecv_sem.at[way, s],
                    device_id=(jnp.where(has_next, me_a + 1, me_a - 1), me_b),
                    device_id_type=MESH,
                ).wait_recv()

    def sent_panels(s):
        for way in range(2):

            @pl.when(panel_leaves(way, s))
            def _():
                panel_copy(way, s).wait_send()

    def share_copy(i):
        return pltpu.make_async_remote_copy(
            src_ref=share.at[i],
            dst_ref=shares.at[i],
            send_sem=xsend_sem.at[i],
            recv_sem=xrecv_sem.at[i],
            device_id=(lax.rem(x + i, X) * Z + z, me_b),
            device_id_type=MESH,
        )

    def next_panels(s):
        if s < Z:
            await_panels(s)
        if s + 1 < Z:
            start_panels(s + 1)

    started = 0
    for p in range(Y):
        if p > 0:
            pack(p)
        if p == 0 and Z > 1:
            start_panels(1)
        if p % 2 == 0 and started < IN_FLIGHT and order[started][0] == 1:
            advance(started)
            started += 1
    side_copy().start()
    recv[:, pl.ds(4 * own, 2)] = send[:, pl.ds(4 * own, 2)]

    for load in small_loads[4:]:
        load.wait()

    def placed(i, _):
        s = sdev[me_b * SLOTS + i]
        rank = jnp.int32(0)
        for other in range(SLOTS):
            same = (sdev[me_b * SLOTS + other] == s) & (other < i)
            rank = rank + jnp.where(same, 1, 0)
        dy = lax.rem(y - (s >> 1) + Y, Y)
        p = jnp.where(dy < Y // 2, Y - 1 - 2 * dy, 2 * dy - Y)
        flip = (s + c) & 1
        rank = jnp.minimum(rank, 1)
        locs[i] = jnp.where(p == 0, flip + 2 * rank, 4 * p + 2 * flip + rank)
        return 0

    lax.fori_loop(0, SLOTS, placed, 0)

    adiag[...] = jnp.broadcast_to(ad[...], (BLK, BLK)).T

    for load in tile_loads:
        load.wait()

    def negate(i, _):
        at[16 + i] = -at[i]
        return 0

    lax.fori_loop(0, 16, negate, 0)
    at[32] = jnp.zeros((BLK, BLK), BF16)

    def widen(q, _):
        wide[q] = jnp.concatenate([bt[2 * q], bt[2 * q + 1]], axis=1)
        return 0

    lax.fori_loop(0, 8, widen, 0)

    def share_of(i):
        target = lax.rem(x + i, X) * Z + z
        tiles, sources = [], []
        for e in range(EA):
            s = asrc[e, target]
            here = lax.div(s, Z) == x
            tiles.append(at[jnp.where(here, akind[e, target] + 16 * apar[e, target], 32)])
            sources.append(panels[lax.rem(s, Z)])
        return jnp.dot(
            jnp.concatenate(tiles, axis=1), jnp.concatenate(sources, axis=0), preferred_element_type=F32
        )

    def give_shares():
        for i in range(1, X):
            share[i] = share_of(i).astype(BF16)
            share_copy(i).start()

    def close_mixed():
        inner = share_of(0)
        for i in range(1, X):
            share_copy(i).wait_recv()
            inner = inner + shares[i].astype(F32)
        inner = jnp.concatenate([inner[:, :BLK], inner[:, BLK:]], axis=0)
        coarse = inner.astype(BF16)
        fine = (inner - coarse.astype(F32)).astype(BF16)
        closing = bt[mkind[0]]
        mixed[...] = jnp.dot(
            jnp.concatenate([coarse, fine], axis=1),
            jnp.concatenate([closing, closing], axis=0),
            preferred_element_type=F32,
        )

    QUARTER = NBLK // 4

    def written(h, part):
        view = (pl.ds(h * BLK, BLK), pl.ds(part * QUARTER * BLK, QUARTER * BLK))
        return pltpu.make_async_copy(out.at[view], out_hbm.at[view], out_sem.at[h, part])

    def finish(h):
        rows = pl.ds(h * BLK, BLK)

        def block(j, _):
            columns = pl.ds(pl.multiple_of(j * BLK, BLK), BLK)
            struck = jnp.where(j == active, 1.0, 0.0).astype(F32)
            total = (adiag[...] + bd[pl.ds(j, 1), :]) * coef[j, rows, :].astype(F32)
            if h == 1:
                total = total + struck * mixed[rows, :]
            for e in range(EB):
                total = total + signs[j * EB + e] * products[plan[j * EB + e]]
            if h == 0:
                stash[...] = stash[...] + struck * total
            out[rows, columns] = (total * occ[0, j].astype(F32)).astype(BF16)
            return 0

        for part in range(4):
            lax.fori_loop(part * QUARTER, (part + 1) * QUARTER, block, 0)
            if h == 1:
                written(1, part).start()

    def amend():
        rows = pl.ds(0, BLK)
        whole = ((stash[...] + mixed[rows, :]) * occ[0, active].astype(F32)).astype(BF16)

        def block(j, _):
            columns = pl.ds(pl.multiple_of(j * BLK, BLK), BLK)
            out[rows, columns] = jnp.where(j == active, whole, out[rows, columns])
            return 0

        lax.fori_loop(0, NBLK, block, 0)
        for part in range(4):
            written(0, part).start()

    def look_up():
        def one(j, _):
            for e in range(EB):
                plan[j * EB + e] = locs[bslot[j, e]] * 16 + bkind[j, e]
                signs[j * EB + e] = (1 - 2 * bpar[j, e]).astype(F32)
            return 0

        lax.fori_loop(0, NBLK, one, 0)

    def first_plane():
        stash[...] = jnp.zeros((BLK, BLK), F32)
        finish(0)
        expand(1, 4 * own, 4)

    beside = []
    for n, (hop, dist) in enumerate(order):
        if hop == dist:
            beside.append((n + IN_FLIGHT, functools.partial(land, n)))
            beside.append((L + n + IN_FLIGHT, functools.partial(land, L + n)))
    beside.append((started, functools.partial(expand, 0, 4 * own, 2)))

    def beside_core():
        side_copy().wait_recv()
        expand(0, 4 * own + 2, 2)

    beside.append((started + 1, beside_core))
    beside.append((started + 1, look_up))
    beside.append((L + IN_FLIGHT - 1, first_plane))
    for s in range(1, Z):
        beside.append((started + 2 * (s - 1), functools.partial(next_panels, s)))
    late = 2 * L - 2
    beside.append((late - 2, give_shares))
    beside.append((late, close_mixed))
    beside.append((late + 1, amend))
    beside.sort(key=lambda entry: entry[0])
    for g in range(started, 2 * L):
        advance(g)
        while beside and beside[0][0] <= g:
            beside.pop(0)[1]()
    for _, work in beside:
        work()
    finish(1)

    side_copy().wait_send()
    for h in range(2):
        for part in range(4):
            written(h, part).wait()
    for g in range(2 * L - IN_FLIGHT, 2 * L):
        for way in range(2):
            for copy in message(way, g):
                copy.wait_send()

    def left_panels(s, _):
        sent_panels(s)
        return 0

    lax.fori_loop(1, Z, left_panels, 0)
    for i in range(1, X):
        share_copy(i).wait_send()


def solution(mesh):
    n_alpha, n_beta = mesh.shape["alpha"], mesh.shape["beta"]
    Z = 8 if n_alpha == 32 else 1
    X, Y = n_alpha // Z, n_beta // 2
    waiting = sum(2 if 2 * dist == Y else 4 for hop, dist in ORDERS[Y] if hop < dist)

    def local(
        coef,
        alpha_diag,
        beta_diag,
        alpha_tiles,
        beta_tiles,
        occupancy,
        alpha_source,
        alpha_kind,
        alpha_parity,
        slot_device,
        slot_offset,
        beta_slot,
        beta_kind,
        beta_parity,
        mixed_block,
        mixed_kind,
    ):
        hbm = pl.BlockSpec(memory_space=pl.ANY)
        columns = coef.shape[-1]
        small = (
            occupancy,
            slot_device.reshape(-1),
            slot_offset,
            mixed_block,
            mixed_kind,
            alpha_source.T,
            alpha_kind.T,
            alpha_parity.T,
            beta_slot,
            beta_kind,
            beta_parity,
            alpha_diag.reshape(1, BLK),
            beta_diag.reshape(NBLK, BLK),
        )
        result = pl.pallas_call(
            functools.partial(kernel, X, Z, Y),
            out_shape=jax.ShapeDtypeStruct((ROWS, columns), BF16),
            in_specs=[hbm] * (len(small) + 3),
            out_specs=hbm,
            scratch_shapes=[
                *(pltpu.SMEM(v.shape, v.dtype) for v in small[:11]),
                *(pltpu.VMEM(v.shape, v.dtype) for v in small[11:]),
                pltpu.VMEM((NBLK, ROWS, BLK), BF16),
                pltpu.VMEM((33, BLK, BLK), BF16),
                pltpu.VMEM((16, BLK, BLK), BF16),
                pltpu.VMEM((Z, BLK, ROWS), BF16),
                pltpu.VMEM((X, BLK, ROWS), BF16),
                pltpu.VMEM((X, BLK, ROWS), BF16),
                pltpu.VMEM((BLK, BLK), F32),
                pltpu.VMEM((ROWS, BLK), F32),
                pltpu.SMEM((SLOTS,), jnp.int32),
                pltpu.VMEM((2, 2 * n_beta, BLK, BLK), BF16),
                pltpu.VMEM((2, 2 * n_beta, BLK, BLK), BF16),
                pltpu.VMEM((2, 2, waiting, BLK, BLK), BF16),
                pltpu.VMEM((8, BLK, 2 * BLK), BF16),
                pltpu.VMEM((2 * n_beta * 16, BLK, BLK), F32),
                pltpu.VMEM((BLK, BLK), F32),
                pltpu.VMEM((ROWS, columns), BF16),
                pltpu.SMEM((NBLK * EB,), jnp.int32),
                pltpu.SMEM((NBLK * EB,), F32),
                pltpu.SemaphoreType.DMA((len(small),)),
                pltpu.SemaphoreType.DMA((2, 4)),
                pltpu.SemaphoreType.DMA((NBLK + 2,)),
                pltpu.SemaphoreType.DMA((2, 2 * len(ORDERS[Y]), 2)),
                pltpu.SemaphoreType.DMA((2, 2 * len(ORDERS[Y]), 2)),
                pltpu.SemaphoreType.DMA((2,)),
                pltpu.SemaphoreType.DMA((2, Z)),
                pltpu.SemaphoreType.DMA((2, Z)),
                pltpu.SemaphoreType.DMA((X,)),
                pltpu.SemaphoreType.DMA((X,)),
            ],
            compiler_params=pltpu.CompilerParams(
                collective_id=0, has_side_effects=True, vmem_limit_bytes=60 * 1024 * 1024
            ),
            cost_estimate=pl.CostEstimate(flops=2200000000, bytes_accessed=3300000, transcendentals=0),
        )(
            *small,
            coef.reshape(ROWS, columns),
            alpha_tiles,
            beta_tiles,
        )
        return result.reshape(coef.shape)

    in_specs = (
        P(None, "alpha", "beta"),
        P("alpha"),
        P("beta"),
        P(),
        P(),
        P("alpha", "beta"),
        P(),
        P(),
        P(),
        P(),
        P(),
        P("beta", None),
        P("beta", None),
        P("beta", None),
        P("beta"),
        P("beta"),
    )
    out_specs = P(None, "alpha", "beta")
    return jax.shard_map(local, mesh=mesh, in_specs=in_specs, out_specs=out_specs, check_vma=False)
```
